256 devices in a mesh: lat: 8 (over x, y_lo), lon: 16 (over z, core), tp: 2 (over y_hi).
Axes of the slice: x: 4, y: 4 (y_hi: 2, y_lo: 2; y = y_hi * 2 + y_lo), z: 8, core: 2. Of those that a mesh axis runs over, the one named last changes fastest.
Arguments:
- tokens: bfloat16 [2, 96, 768, 512], P('tp', 'lat', 'lon'), may hold values from -6 to 6
- labels: int32 [2, 96, 768], P(None, 'lat', 'lon'), may hold values from 0 to 2
- gain_one: float32 [512], replicated, may hold values from 0.5 to 2
- second_norm_gain: float32 [512], replicated, may hold values from 0.5 to 2
- w_qkv: bfloat16 [3, 512, 512], P(None, None, 'tp'), may hold values from -8 to 8
- w_out: bfloat16 [512, 512], P('tp'), may hold values from -0.25 to 0.25
- w_fc1: bfloat16 [512, 2048], P(None, 'tp'), may hold values from -0.25 to 0.25
- w_fc2: bfloat16 [2048, 512], P('tp'), may hold values from -0.125 to 0.125
- cotangent: bfloat16 [2, 96, 768, 512], P('tp', 'lat', 'lon'), may hold values from -0.119628906 to 0.119628906
Outputs:
- output: bfloat16 [2, 96, 768, 512], P('tp', 'lat', 'lon')
- grad_qkv: bfloat16 [3, 512, 512], P(None, None, 'tp')
- grad_out: bfloat16 [512, 512], P('tp')
- grad_fc1: bfloat16 [512, 2048], P(None, 'tp')
- grad_fc2: bfloat16 [2048, 512], P('tp')
The draws below stay inside these ranges and needn't reach their ends.
All inputs are finite; a program needn't handle non-finite values.
Results may differ from the reference program's by a relative error of at most 0.024.
Values may be sent and summed in bfloat16 or wider, within the bound.
No kernel may reach another device: no remote copies, remote signals or barrier semaphores. Data moves between devices by JAX's collectives and lax.ppermute only.
A program may use at most 128 MiB of HBM per device.

```python
import math
import jax
import jax.numpy as jnp
from jax import lax

D = 512
HEADS = 8
FF = 2048
LV = 2
WLAT = 6
WLON = 12
NLAT = 96
NLON = 768


def draw_w_qkv(key, part):
    key = jax.random.fold_in(key, 7)
    base_key = jax.random.fold_in(key, 0)
    base = jax.random.normal(base_key, (3, D, D), jnp.float32) * D ** (-0.5)
    return jnp.clip(base, -8.0, 8.0).astype(jnp.bfloat16)


def with_ends(result, rng, smallest, largest):
    dims = result.shape
    place = [jax.random.randint(jax.random.fold_in(rng, axis), (), 0, dims[axis]) for axis in range(len(dims))]
    result = result.at[tuple(place)].set(smallest)
    longest = dims.index(max(dims))
    place[longest] = (place[longest] + 1) % dims[longest]
    return result.at[tuple(place)].set(largest)


def level_of(key, extent, cuts, least, high):
    def one(position, parts):
        draws = jax.random.uniform(jax.random.fold_in(jax.random.fold_in(key, 6), position), (parts,), jnp.float32, least / len(cuts), high / len(cuts))
        return jnp.repeat(jnp.exp(draws), extent[position] // parts).reshape((-1,) + (1,) * (len(extent) - position - 1))

    level = one(*cuts[0])
    for cut in cuts[1:]:
        level = level * one(*cut)
    return level


def normal_values(rng, extent, deviation, bound, pieces=(), held_as=jnp.bfloat16):
    entries = deviation * jax.random.normal(rng, extent, jnp.float32)
    if pieces:
        entries = entries * level_of(rng, extent, pieces, -0.22, 0.18)
    return jnp.clip(entries, -bound, bound).astype(held_as)


def setup_inputs(seed: int = 0) -> dict:
    key_list = jax.random.split(jax.random.key(seed), 10)
    tokens = normal_values(key_list[0], (LV, NLAT, NLON, D), 1.0, 6.0, ((0, 2), (1, 8), (2, 16)))
    labels = with_ends(jax.random.randint(key_list[1], (LV, NLAT, NLON), 0, 3), jax.random.fold_in(key_list[1], 1), 0, 2).astype(jnp.int32)
    gain_one = jnp.clip(jnp.exp(jax.random.uniform(key_list[2], (D,), jnp.float32, math.log(0.5), math.log(2.0))), 0.5, 2.0)
    second_norm_gain = jnp.clip(jnp.exp(jax.random.uniform(key_list[3], (D,), jnp.float32, math.log(0.5), math.log(2.0))), 0.5, 2.0)
    w_qkv = draw_w_qkv(jax.random.fold_in(key_list[9], 71), 0)
    w_out = normal_values(key_list[5], (D, D), D ** -0.5, 0.25, ((0, 2),))
    w_fc1 = normal_values(key_list[6], (D, FF), D ** -0.5, 0.25, ((1, 2),))
    w_fc2 = normal_values(key_list[7], (FF, D), FF ** -0.5, 0.125, ((0, 2),))
    cotangent = normal_values(key_list[8], (LV, NLAT, NLON, D), 0.02, 0.119628906, ((0, 2), (1, 8), (2, 16)))
    return {"tokens": tokens, "labels": labels, "gain_one": gain_one, "second_norm_gain": second_norm_gain, "w_qkv": w_qkv, "w_out": w_out, "w_fc1": w_fc1, "w_fc2": w_fc2, "cotangent": cotangent}


eps = 1e-05
gelu_c = 0.7978845608028654

def widen(value):
    return lax.optimization_barrier(value).astype(jnp.float32)

def apply_layer_norm(value, norm_gain):
    wide = value.astype(jnp.float32)
    centered_rows = wide - lax.optimization_barrier(jnp.mean(wide, -1, keepdims=True))
    inverse_deviation = lax.rsqrt(lax.optimization_barrier(jnp.mean(centered_rows * centered_rows, -1, keepdims=True)) + eps)
    standardized_input = centered_rows * inverse_deviation
    return (standardized_input * norm_gain.astype(jnp.float32), standardized_input, inverse_deviation)

def gelu_slope(value):
    inner = gelu_c * (value + 0.044715 * value * value * value)
    tanh_v = jnp.tanh(inner)
    return 0.5 * (1.0 + tanh_v) + 0.5 * value * (1.0 - tanh_v * tanh_v) * gelu_c * (1.0 + 3.0 * 0.044715 * value * value)

def to_windows(tile):
    levels, token_rows, cols, width = tile.shape
    block = tile.reshape(levels, token_rows // WLAT, WLAT, cols // WLON, WLON, width)
    block = block.transpose(1, 3, 0, 2, 4, 5)
    return block.reshape(token_rows // WLAT * (cols // WLON), levels * WLAT * WLON, width)

def from_windows(wins, levels, token_rows, cols):
    width = wins.shape[-1]
    block = wins.reshape(token_rows // WLAT, cols // WLON, levels, WLAT, WLON, width)
    block = block.transpose(2, 0, 3, 1, 4, 5)
    return block.reshape(levels, token_rows, cols, width)

def split_heads(value):
    count, seats, width = value.shape
    head_size = D // HEADS
    return widen(value).reshape(count, seats, width // head_size, head_size)

def attend(a_win, lab_win, w_qkv):
    head_size = D // HEADS
    qkv = jnp.einsum('wsd,idc->iwsc', widen(a_win), widen(w_qkv)).astype(jnp.bfloat16)
    query, key, value = (split_heads(qkv[0]), split_heads(qkv[1]), split_heads(qkv[2]))
    scores = jnp.einsum('wqhd,wkhd->whqk', query, key) * head_size ** (-0.5)
    same = (lab_win[:, :, None] == lab_win[:, None, :])[:, None]
    scores = jnp.where(same, scores, -1e+30)
    top = lax.optimization_barrier(jnp.max(scores, -1, keepdims=True))
    expo = jnp.exp(scores - top)
    prob = expo / lax.optimization_barrier(jnp.sum(expo, -1, keepdims=True))
    prob_b = widen(prob.astype(jnp.bfloat16))
    heads_out = jnp.einsum('whqk,wkhd->wqhd', prob_b, value)
    count, seats = (a_win.shape[0], a_win.shape[1])
    return (qkv, prob, heads_out.reshape(count, seats, -1).astype(jnp.bfloat16))

def attend_back(qkv, prob, d_heads):
    head_size = D // HEADS
    query, key, value = (split_heads(qkv[0]), split_heads(qkv[1]), split_heads(qkv[2]))
    d_out = split_heads(d_heads)
    prob_b = widen(prob.astype(jnp.bfloat16))
    d_prob = jnp.einsum('wqhd,wkhd->whqk', d_out, value)
    d_value = jnp.einsum('whqk,wqhd->wkhd', prob_b, d_out)
    d_scores = prob * (d_prob - lax.optimization_barrier(jnp.sum(prob * d_prob, -1, keepdims=True)))
    d_scores = widen((d_scores * head_size ** (-0.5)).astype(jnp.bfloat16))
    d_query = jnp.einsum('whqk,wkhd->wqhd', d_scores, key)
    d_key = jnp.einsum('whqk,wqhd->wkhd', d_scores, query)
    count, seats = (d_heads.shape[0], d_heads.shape[1])
    stacked = jnp.stack([d_query, d_key, d_value]).reshape(3, count, seats, -1)
    return stacked.astype(jnp.bfloat16)

def reference(tokens, labels, gain_one, second_norm_gain, w_qkv, w_out, w_fc1, w_fc2, cotangent):
    levels, nlat, nlon, width = tokens.shape
    half_lat, half_lon = (WLAT // 2, WLON // 2)
    bands = nlat // WLAT
    band_ids = jnp.arange(bands, dtype=jnp.int32)
    norm_one = apply_layer_norm(tokens, gain_one)[0].astype(jnp.bfloat16)
    rolled = jnp.roll(norm_one, (-half_lat, -half_lon), axis=(1, 2))

    def band_of(array, index):
        return lax.dynamic_slice_in_dim(array, (index * WLAT).astype(jnp.int32), WLAT, 1)

    def forward_band(index):
        a_win = to_windows(band_of(rolled, index))
        lab_win = to_windows(band_of(labels, index)[..., None])[..., 0]
        heads_out = attend(a_win, lab_win, w_qkv)[2]
        return from_windows(heads_out, levels, WLAT, nlon)
    banded = lax.map(forward_band, band_ids)
    heads_all = banded.transpose(1, 0, 2, 3, 4).reshape(levels, nlat, nlon, width)
    flat_heads = heads_all.reshape(-1, width)
    attn = jnp.dot(flat_heads, w_out, preferred_element_type=jnp.float32).astype(jnp.bfloat16)
    attn = attn.reshape(levels, nlat, nlon, width)
    back = jnp.roll(attn, (half_lat, half_lon), axis=(1, 2))
    mixed_rows = (tokens.astype(jnp.float32) + back.astype(jnp.float32)).astype(jnp.bfloat16)

    def mlp_band(carry, index):
        acc_fc1, acc_fc2 = carry
        token_rows = band_of(mixed_rows, index).reshape(-1, width)
        row_gradient = band_of(cotangent, index).reshape(-1, width)
        normed_rows, standardized_input, inverse_deviation = apply_layer_norm(token_rows, second_norm_gain)
        norm_two = normed_rows.astype(jnp.bfloat16)
        pre = jnp.dot(norm_two, w_fc1, preferred_element_type=jnp.float32)
        hidden = jax.nn.gelu(pre, approximate=True).astype(jnp.bfloat16)
        out_rows = (token_rows.astype(jnp.float32) + jnp.dot(hidden, w_fc2, preferred_element_type=jnp.float32)).astype(jnp.bfloat16)
        d_hidden = jnp.dot(row_gradient, w_fc2.T, preferred_element_type=jnp.float32)
        d_pre = (d_hidden * gelu_slope(pre)).astype(jnp.bfloat16)
        acc_fc2 = acc_fc2 + jnp.dot(hidden.T, row_gradient, preferred_element_type=jnp.float32)
        acc_fc1 = acc_fc1 + jnp.dot(norm_two.T, d_pre, preferred_element_type=jnp.float32)
        d_norm = jnp.dot(d_pre, w_fc1.T, preferred_element_type=jnp.float32)
        scaled_rows = d_norm * second_norm_gain.astype(jnp.float32)
        mixed_gradient = row_gradient.astype(jnp.float32) + inverse_deviation * (scaled_rows - lax.optimization_barrier(jnp.mean(scaled_rows, -1, keepdims=True)) - standardized_input * lax.optimization_barrier(jnp.mean(scaled_rows * standardized_input, -1, keepdims=True)))
        return ((acc_fc1, acc_fc2), (out_rows, mixed_gradient.astype(jnp.bfloat16)))
    start = (jnp.zeros((width, FF), jnp.float32), jnp.zeros((FF, width), jnp.float32))
    (acc_fc1, acc_fc2), (out_bands, dm_bands) = lax.scan(mlp_band, start, band_ids)

    def unband(stack):
        return stack.reshape(bands, levels, WLAT, nlon, width).transpose(1, 0, 2, 3, 4).reshape(levels, nlat, nlon, width)
    output = unband(out_bands)
    mixed_gradient = unband(dm_bands)
    d_attn = jnp.roll(mixed_gradient, (-half_lat, -half_lon), axis=(1, 2))
    flat_d = d_attn.reshape(-1, width)
    grad_out = jnp.dot(flat_heads.T, flat_d, preferred_element_type=jnp.float32)
    d_heads = jnp.dot(flat_d, w_out.T, preferred_element_type=jnp.float32).astype(jnp.bfloat16)
    d_heads = d_heads.reshape(levels, nlat, nlon, width)

    def back_band(acc, index):
        a_win = to_windows(band_of(rolled, index))
        lab_win = to_windows(band_of(labels, index)[..., None])[..., 0]
        qkv, prob, unused = attend(a_win, lab_win, w_qkv)
        d_qkv = attend_back(qkv, prob, to_windows(band_of(d_heads, index)))
        acc = acc + jnp.einsum('wsd,iwsc->idc', widen(a_win), widen(d_qkv))
        return (acc, None)
    acc_qkv, unused = lax.scan(back_band, jnp.zeros((3, width, width), jnp.float32), band_ids)
    return (output, acc_qkv.astype(jnp.bfloat16), grad_out.astype(jnp.bfloat16), acc_fc1.astype(jnp.bfloat16), acc_fc2.astype(jnp.bfloat16))
```

```python
import functools

import jax
import jax.numpy as jnp
from jax import lax
from jax.experimental import pallas as pl
from jax.experimental.pallas import tpu as pltpu
from jax.sharding import PartitionSpec as P

D = 512
FF = 2048
WLAT = 6
WLON = 12
SEATS = 144
WINS = 4
TOK = SEATS * WINS
EPS = 1e-05
GELU_C = 0.7978845608028654
BF = jnp.bfloat16
F32 = jnp.float32
AXES = ("lat", "lon", "tp")
VMEM_LIMIT = 48 * 1024 * 1024


def pairs_of(move):
    pairs = []
    for x in range(4):
        for yl in range(2):
            for z in range(8):
                for c in range(2):
                    for t in range(2):
                        dest = move(x, yl, z, c, t)
                        if dest is not None:
                            pairs.append((rank(x, yl, z, c, t), rank(*dest)))
    return pairs


def rank(x, yl, z, c, t):
    return ((2 * x + yl) * 16 + 2 * z + c) * 2 + t


def send(value, move):
    return lax.ppermute(value, AXES, pairs_of(move))


def flip(value, x=0, yl=0, z=0, c=0, t=0):
    return send(value, lambda a, b, d, e, f: (a ^ x, b ^ yl, d ^ z, e ^ c, f ^ t))


def shift_lat(x, yl, step):
    lat = (2 * x + yl + step) % 8
    return lat // 2, lat % 2


def shift_lon(z, c, step):
    lon = (2 * z + c + step) % 16
    return lon // 2, lon % 2


def lon_move(step):
    def move(x, yl, z, c, t):
        zz, cc = shift_lon(z, c, step)
        return x, yl, zz, cc, t

    return move


def far_move(x, yl, z, c, t):
    if t == 1:
        return x, yl, z, c, 0
    xx, yy = shift_lat(x, yl, -1)
    return xx, yy, z, c, 1


def far_back(x, yl, z, c, t):
    if t == 0:
        return x, yl, z, c, 1
    xx, yy = shift_lat(x, yl, 1)
    return xx, yy, z, c, 0


def lat_move(step):
    def move(x, yl, z, c, t):
        if t == 0:
            return None
        xx, yy = shift_lat(x, yl, step)
        return xx, yy, z, c, t

    return move


def gather_windows(tile, t):
    first = t == 0
    near = flip(jnp.where(first, tile[9:12], tile[3:6]), t=1)
    far = send(jnp.where(first, tile[0:3], tile[6:9]), far_move)
    below = send(tile[0:3], lat_move(-1))
    own = jnp.where(first, tile[3:9], jnp.concatenate([tile[9:12], below], 0))
    band = jnp.concatenate([own, near, far], 0)
    moved = send(band[:, :6], lon_move(-1))
    band = jnp.concatenate([band[:, 6:], moved], 1)
    return to_windows(band)


def to_windows(band):
    width = band.shape[-1]
    return band.reshape(12, WINS, WLON, width).transpose(1, 0, 2, 3).reshape(TOK, width)


def scatter_windows(wins, t):
    band = wins.reshape(WINS, 12, WLON, D).transpose(1, 0, 2, 3).reshape(12, 48, D)
    moved = send(band[:, 42:], lon_move(1))
    band = jnp.concatenate([moved, band[:, :42]], 1)
    own, near, far = band[0:6], band[6:9], band[9:12]
    near = flip(near, t=1)
    far = send(far, far_back)
    above = send(own[3:6], lat_move(1))
    return jnp.where(
        t == 0,
        jnp.concatenate([far, own, near], 0),
        jnp.concatenate([above, near, far, own[0:3]], 0),
    )


def norm(value, gain):
    centered = value - jnp.mean(value, -1, keepdims=True)
    rstd = lax.rsqrt(jnp.mean(centered * centered, -1, keepdims=True) + EPS)
    xhat = centered * rstd
    return xhat * gain, xhat, rstd


def dot(a, b):
    return lax.dot_general(a, b, (((1,), (0,)), ((), ())), preferred_element_type=F32)


def dot_nt(a, b):
    return lax.dot_general(a, b, (((1,), (1,)), ((), ())), preferred_element_type=F32)


def dot_tn(a, b):
    return lax.dot_general(a, b, (((0,), (0,)), ((), ())), preferred_element_type=F32)


def head_mask(h):
    lane = lax.broadcasted_iota(jnp.int32, (1, 128), 1)
    return (lane < 64) if h == 0 else (lane >= 64)


def attend_kernel(
    place, x_ref, labc, labr, g1, wq_own, wq_m, wq_s, wo_own, wo_m, wo_s,
    n1t_ref, qkv_ref, prob_ref, heads_ref, wo_full, mixed_ref, n1_scr,
):
    c = place[3]
    mine = pl.ds(pl.multiple_of(c * 256, 256), 256)
    sibs = pl.ds(pl.multiple_of((1 - c) * 256, 256), 256)
    x = x_ref[...].astype(F32)
    normed = norm(x, g1[...])[0]
    n1_scr[...] = normed.astype(BF)
    n1t_ref[...] = normed.T.astype(BF)
    n1 = n1_scr[...]
    for i in range(3):
        scale = 0.125 if i == 0 else 1.0
        own = dot(n1, wq_own[i]).astype(BF)
        other = (dot(n1_scr[:, mine], wq_m[i]) + dot(n1_scr[:, sibs], wq_s[i])).astype(BF)
        qkv_ref[:, i * 512 : i * 512 + 256] = own * BF(scale)
        qkv_ref[:, i * 512 + 256 : i * 512 + 512] = other * BF(scale)

    def window(w, carry):
        rows = pl.ds(pl.multiple_of(w * SEATS, 16), SEATS)
        same = labc[rows, 0:1] == labr[w, 0:1, :]
        for p in range(4):
            q2 = qkv_ref[rows, p * 128 : p * 128 + 128]
            k2 = qkv_ref[rows, 512 + p * 128 : 640 + p * 128]
            v2 = qkv_ref[rows, 1024 + p * 128 : 1152 + p * 128]
            total = None
            for h in range(2):
                keep = head_mask(h)
                scores = dot_nt(jnp.where(keep, q2, BF(0)), k2)
                scores = jnp.where(same, scores, -1e30)
                expo = jnp.exp(scores - jnp.max(scores, -1, keepdims=True))
                prob = (expo * (1.0 / jnp.sum(expo, -1, keepdims=True))).astype(BF)
                prob_ref[w * 8 + p * 2 + h] = prob
                part = dot(prob, jnp.where(keep, v2, BF(0)))
                total = part if total is None else total + part
            heads_ref[rows, p * 128 : p * 128 + 128] = total.astype(BF)
        return carry

    lax.fori_loop(0, WINS, window, 0)
    wo_full[0:256, :] = wo_own[...]
    wo_full[256:512, mine] = wo_m[...]
    wo_full[256:512, sibs] = wo_s[...]
    attn = dot(heads_ref[...], wo_full[...]).astype(BF).astype(F32)
    mixed_ref[...] = (x + attn).astype(BF)


def gelu_parts(v):
    square = v * v
    tanh_v = jnp.tanh(GELU_C * v * (1.0 + 0.044715 * square))
    half = 0.5 * (1.0 + tanh_v)
    slope = half + 0.5 * v * (1.0 - tanh_v * tanh_v) * (GELU_C + (3.0 * 0.044715 * GELU_C) * square)
    return v * half, slope


def store_rows(out, block, a, b, lead, mz, width):
    for yl in range(2):
        for z in range(8):
            out[lead(yl) + (z ^ mz,)] = block[z * 32 + yl * 16 : z * 32 + yl * 16 + 16].astype(BF)


def mlp_kernel(
    place, mixed_ref, cot_ref, g2, w1_own, w1_m, w1_s, w2_own, w2_m, w2_s,
    out_ref, dm_ref, keep_x, send_x, keep_y, send_y,
    n2t, cott, w1_scr, w2_scr, hid_scr, dpre_scr,
):
    mx, my, mz, c = place[0], place[1], place[2], place[3]
    mine = pl.ds(pl.multiple_of(c * 256, 256), 256)
    sibs = pl.ds(pl.multiple_of((1 - c) * 256, 256), 256)
    mine2 = pl.ds(pl.multiple_of(c * 512, 512), 512)
    sibs2 = pl.ds(pl.multiple_of((1 - c) * 512, 512), 512)
    w1_scr[mine, :] = w1_m[...]
    w1_scr[sibs, :] = w1_s[...]
    w2_scr[mine2, :] = w2_m[...]
    w2_scr[sibs2, :] = w2_s[...]
    gain = g2[...]
    mixed = mixed_ref[...].astype(F32)
    normed, xhat, rstd = norm(mixed, gain)
    n2 = normed.astype(BF)
    n2t[...] = normed.T.astype(BF)
    cot = cot_ref[...]
    cott[...] = cot.astype(F32).T.astype(BF)
    for t in range(2):
        w1, w2 = (w1_own, w2_own) if t == 0 else (w1_scr, w2_scr)
        for x in range(4):
            cols = slice(x * 256, x * 256 + 256)
            place_cols = slice(t * 1024 + x * 256, t * 1024 + x * 256 + 256)
            hidden, slope = gelu_parts(dot(n2, w1[:, cols]))
            hidden = hidden.astype(BF)
            dpre = (dot_nt(cot, w2[cols, :]) * slope).astype(BF)
            hid_scr[:, place_cols] = hidden
            dpre_scr[:, place_cols] = dpre
            for rows, gx, gy in ((sibs, send_x, send_y), (mine, keep_x, keep_y)):
                lead = lambda yl, t=t, x=x: (t, yl ^ my, x ^ mx)
                store_rows(gx, dot(n2t[rows, :], dpre), t, x, lead, mz, 256)
                store_rows(gy, dot(cott[rows, :], hidden), t, x, lead, mz, 256)
    summed = dot(hid_scr[:, :1024], w2_own[...]) + dot(hid_scr[:, 1024:], w2_scr[...])
    out_ref[...] = (mixed + summed).astype(BF)
    d_norm = dot_nt(dpre_scr[:, :1024], w1_own[...]) + dot_nt(dpre_scr[:, 1024:], w1_scr[...])
    scaled = d_norm * gain
    dm = cot.astype(F32) + rstd * (
        scaled
        - jnp.mean(scaled, -1, keepdims=True)
        - xhat * jnp.mean(scaled * xhat, -1, keepdims=True)
    )
    dm_ref[...] = dm.astype(BF)


def attend_back_kernel(
    place, dm_ref, heads_ref, prob_ref, qkv_ref, n1t_ref, wo_full,
    keep_x, send_x, keep_y, send_y,
    dmt, dheads, dqkv,
):
    mx, my, mz, c = place[0], place[1], place[2], place[3]
    mine = pl.ds(pl.multiple_of(c * 256, 256), 256)
    sibs = pl.ds(pl.multiple_of((1 - c) * 256, 256), 256)
    dm = dm_ref[...]
    dmt[...] = dm.astype(F32).T.astype(BF)
    dheads[...] = dot_nt(dm, wo_full[...]).astype(BF)

    def window(w, carry):
        rows = pl.ds(pl.multiple_of(w * SEATS, 16), SEATS)
        for p in range(4):
            pc = slice(p * 128, p * 128 + 128)
            q2 = qkv_ref[rows, p * 128 : p * 128 + 128]
            k2 = qkv_ref[rows, 512 + p * 128 : 640 + p * 128]
            v2 = qkv_ref[rows, 1024 + p * 128 : 1152 + p * 128]
            do2 = dheads[rows, pc]
            dq = dk = dv = None
            for h in range(2):
                keep = head_mask(h)
                prob_b = prob_ref[w * 8 + p * 2 + h]
                prob = prob_b.astype(F32)
                do_h = jnp.where(keep, do2, BF(0))
                d_prob = dot_nt(do_h, v2)
                moment = jnp.sum(prob * d_prob, -1, keepdims=True)
                d_scores = (prob * (d_prob - moment)).astype(BF)
                pq = dot(d_scores, jnp.where(keep, k2, BF(0)))
                pk = dot_tn(d_scores, jnp.where(keep, q2, BF(0)))
                pv = dot_tn(prob_b, do_h)
                dq = pq if dq is None else dq + pq
                dk = pk if dk is None else dk + pk
                dv = pv if dv is None else dv + pv
            dqkv[rows, p * 128 : p * 128 + 128] = (dq * 0.125).astype(BF)
            dqkv[rows, 512 + p * 128 : 640 + p * 128] = dk.astype(BF)
            dqkv[rows, 1024 + p * 128 : 1152 + p * 128] = dv.astype(BF)
        return carry

    lax.fori_loop(0, WINS, window, 0)
    for rows, gx, gy in ((sibs, send_x, send_y), (mine, keep_x, keep_y)):
        for t in range(2):
            for half in range(2):
                for which, out in ((0, gx), (1, gy)):
                    if which == 0 or half == 0:
                        start = (2 * which + half) * 512 + t * 256
                        grad = dot(n1t_ref[rows, :], dqkv[:, start : start + 256])
                    else:
                        grad = dot(dmt[rows, :], heads_ref[:, t * 256 : t * 256 + 256])
                    for sub in range(2):
                        x = half * 2 + sub
                        lead = lambda yl, t=t, x=x: (t, yl ^ my, x ^ mx)
                        store_rows(out, grad[:, sub * 128 : sub * 128 + 128], t, x, lead, mz, 128)


def whole(shape, dtype=BF):
    return jax.ShapeDtypeStruct(shape, dtype)


def vmem(n):
    return [pl.BlockSpec(memory_space=pltpu.VMEM)] * n


def call(kernel, args, outs, scratch=(), place=None, flops=0, name=None):
    specs = vmem(len(args))
    if place is not None:
        args = (place,) + tuple(args)
        specs = [pl.BlockSpec(memory_space=pltpu.SMEM)] + specs
    size = sum(a.size * a.dtype.itemsize for a in list(args) + list(outs))
    return pl.pallas_call(
        kernel,
        out_shape=tuple(outs),
        in_specs=specs,
        out_specs=tuple(vmem(len(outs))),
        scratch_shapes=list(scratch),
        compiler_params=pltpu.CompilerParams(vmem_limit_bytes=VMEM_LIMIT),
        cost_estimate=pl.CostEstimate(flops=flops, bytes_accessed=size, transcendentals=0),
        name=name,
    )(*args)


def add(*values):
    total = values[0].astype(F32)
    for value in values[1:]:
        total = total + value.astype(F32)
    return total.astype(BF)


def core_sum_kernel(kx, rx, ky, ry, *outs):
    for x in range(4):
        outs[x][...] = add(kx[:, :, x], rx[:, :, x])
    for y in range(4):
        outs[4 + y][...] = add(ky[y // 2, y % 2], ry[y // 2, y % 2])


def first_sum_kernel(*refs):
    ins, outs = refs[:16], refs[16:]
    fx, fy, ax, ay = ins[0:4], ins[4:8], ins[8:12], ins[12:16]
    for y in range(4):
        outs[y][:, :, :256] = add(*[r[y // 2, y % 2] for r in fx])
        outs[y][:, :, 256:] = add(*[r[y // 2, y % 2] for r in ax])
    for x in range(4):
        outs[4 + x][:, :, :256] = add(*[r[x] for r in fy])
        outs[4 + x][:, :, 256:] = add(*[r[x] for r in ay])


def second_sum_kernel(*refs):
    xs, ys, outs = refs[0:4], refs[4:8], refs[8:]
    for z in range(8):
        outs[z][0] = add(*[r[z] for r in xs])
        outs[z][1] = add(*[r[z] for r in ys])


def third_sum_kernel(*refs):
    refs[-1][...] = add(*[r[...] for r in refs[:-1]])


def stack_z_kernel(*refs):
    for z in range(8):
        refs[8][z] = refs[z][0]
        refs[9][z] = refs[z][1]


def stack_mid_kernel(x0, x1, y0, y1, y2, y3, xs, ys):
    xs[0] = x0[...]
    xs[1] = x1[...]
    for i, r in enumerate((y0, y1, y2, y3)):
        ys[i] = r[...]


def stack_last_kernel(x0, x1, x2, x3, y0, y1, out):
    for i, r in enumerate((x0, x1, x2, x3)):
        for b in range(2):
            out[0, b, i] = r[b]
    for b, r in enumerate((y0, y1)):
        for i in range(4):
            out[1, b, i] = r[i]


def place_kernel(place, mine, sib, gq, go, g1, g2, scr2, scro):
    mx, my, mz, c = place[0], place[1], place[2], place[3]
    for src, cc in ((mine, c), (sib, 1 - c)):
        base = cc * 256
        for yl in range(2):
            for x in range(4):
                for z in range(8):
                    rows = pl.ds(pl.multiple_of(base + z * 32 + yl * 16, 16), 16)
                    vx = src[0, yl ^ my, x ^ mx, z ^ mz]
                    vy = src[1, yl ^ my, x ^ mx, z ^ mz]
                    g1[rows, x * 256 : x * 256 + 256] = vx[:, :256]
                    scr2[rows, x * 256 : x * 256 + 256] = vy[:, :256]
                    lo = (x % 2) * 128
                    gq[x // 2, rows, lo : lo + 128] = vx[:, 256:]
                    if x < 2:
                        gq[2, rows, lo : lo + 128] = vy[:, 256:]
                    else:
                        scro[rows, lo : lo + 128] = vy[:, 256:]
    for i in range(4):
        g2[i * 256 : i * 256 + 256, :] = scr2[:, i * 256 : i * 256 + 256].astype(F32).T.astype(BF)
    go[...] = scro[...].astype(F32).T.astype(BF)


def core_phase(keep_x, send_x, keep_y, send_y, width):
    rx, ry = flip(send_x, c=1), flip(send_y, c=1)
    outs = [whole((2, 2, 8, 16, width))] * 4 + [whole((4, 8, 16, width))] * 4
    return call(core_sum_kernel, (keep_x, rx, keep_y, ry), outs, name="core_sum")


def first_phase(cut):
    xs = [cut[0]] + [flip(cut[k], x=k) for k in (1, 2, 3)]
    ys = [cut[4]] + [flip(cut[4 + k], t=k // 2, yl=k % 2) for k in (1, 2, 3)]
    return xs, ys


def reduce_and_gather(place, fx, fy, ax, ay):
    outs = [whole((8, 16, 384))] * 8
    cut = call(first_sum_kernel, (*fx, *fy, *ax, *ay), outs, name="first_sum")
    xs = [cut[0]] + [flip(cut[k], t=k // 2, yl=k % 2) for k in (1, 2, 3)]
    ys = [cut[4]] + [flip(cut[4 + k], x=k) for k in (1, 2, 3)]
    cut = call(second_sum_kernel, (*xs, *ys), [whole((2, 16, 384))] * 8, name="second_sum")
    zs = [cut[0]] + [flip(cut[k], z=k) for k in range(1, 8)]
    (chunk,) = call(third_sum_kernel, zs, [whole((2, 16, 384))], name="third_sum")
    zs = [chunk] + [flip(chunk, z=k) for k in range(1, 8)]
    x0, y0 = call(stack_z_kernel, zs, [whole((8, 16, 384))] * 2, name="stack_z")
    x1 = flip(x0, yl=1)
    y1, y2, y3 = [flip(y0, x=k) for k in (1, 2, 3)]
    xs, ys = call(
        stack_mid_kernel, (x0, x1, y0, y1, y2, y3),
        [whole((2, 8, 16, 384)), whole((4, 8, 16, 384))], name="stack_mid",
    )
    xk = [xs] + [flip(xs, x=k) for k in (1, 2, 3)]
    yk = [ys, flip(ys, yl=1)]
    (mine,) = call(stack_last_kernel, (*xk, *yk), [whole((2, 2, 4, 8, 16, 384))], name="stack_last")
    sib = flip(mine, c=1)
    outs = [whole((3, 512, 256)), whole((256, 512)), whole((512, 1024)), whole((1024, 512))]
    scratch = [pltpu.VMEM((512, 1024), BF), pltpu.VMEM((512, 256), BF)]
    return call(place_kernel, (mine, sib), outs, scratch, place, name="place")


def per_device(tokens, labels, gain_one, second_norm_gain, w_qkv, w_out, w_fc1, w_fc2, cotangent):
    lat, lon, t = lax.axis_index("lat"), lax.axis_index("lon"), lax.axis_index("tp")
    x, yl, z, c = lat // 2, lat % 2, lon // 2, lon % 2
    place = jnp.stack([x, yl, z, c, t]).astype(jnp.int32)

    def cross(value, axis):
        size = value.shape[axis] // 2
        part = lax.dynamic_slice_in_dim(value, c * size, size, axis)
        part = flip(part, yl=1, t=1)
        return part, flip(part, c=1)

    wins = gather_windows(tokens[0], t)
    wq_m, wq_s = cross(w_qkv, 1)
    wo_m, wo_s = cross(w_out, 1)
    w1_m, w1_s = cross(w_fc1, 0)
    w2_m, w2_s = cross(w_fc2, 0)
    cots = gather_windows(cotangent[0], t)

    band = lax.dynamic_slice_in_dim(labels, t * 6, 6, 1)
    band = jnp.where(t == 0, band, band[::-1]).reshape(12, 48, 1)
    lab = to_windows(band).reshape(TOK)
    labc = jnp.broadcast_to(lab[:, None], (TOK, 128))
    labr = jnp.broadcast_to(lab.reshape(WINS, 1, SEATS), (WINS, 8, SEATS))

    n1t, qkv, prob, heads, wo_full, mixed = call(
        attend_kernel,
        (wins, labc, labr, gain_one[None], w_qkv, wq_m, wq_s, w_out, wo_m, wo_s),
        [
            whole((D, TOK)), whole((TOK, 3 * D)), whole((WINS * 8, SEATS, SEATS)),
            whole((TOK, D)), whole((D, D)), whole((TOK, D)),
        ],
        [pltpu.VMEM((TOK, D), BF)],
        place,
        flops=3 * 10**9,
        name="attend",
    )
    grads = [whole((2, 2, 4, 8, 16, 256))] * 4
    output, dm, *fc = call(
        mlp_kernel,
        (mixed, cots, second_norm_gain[None], w_fc1, w1_m, w1_s, w_fc2, w2_m, w2_s),
        [whole((TOK, D)), whole((TOK, D))] + grads,
        [
            pltpu.VMEM((D, TOK), BF), pltpu.VMEM((D, TOK), BF),
            pltpu.VMEM((D, 1024), BF), pltpu.VMEM((1024, D), BF),
            pltpu.VMEM((TOK, FF), BF), pltpu.VMEM((TOK, FF), BF),
        ],
        place,
        flops=8 * 10**9,
        name="mlp",
    )
    fc_cut = core_phase(*fc, 256)
    fx, fy = first_phase(fc_cut)
    grads = [whole((2, 2, 4, 8, 16, 128))] * 4
    at = call(
        attend_back_kernel,
        (dm, heads, prob, qkv, n1t, wo_full),
        grads,
        [pltpu.VMEM((D, TOK), BF), pltpu.VMEM((TOK, D), BF), pltpu.VMEM((TOK, 3 * D), BF)],
        place,
        flops=5 * 10**9,
        name="attend_back",
    )
    at_cut = core_phase(*at, 128)
    ax, ay = first_phase(at_cut)
    out_tile = scatter_windows(output, t)
    gq, go, g1, g2 = reduce_and_gather(place, fx, fy, ax, ay)
    return out_tile[None], gq, go, g1, g2


def solution(mesh):
    return jax.shard_map(
        per_device,
        mesh=mesh,
        in_specs=(
            P("tp", "lat", "lon", None),
            P(None, "lat", "lon"),
            P(),
            P(),
            P(None, None, "tp"),
            P("tp", None),
            P(None, "tp"),
            P("tp", None),
            P("tp", "lat", "lon", None),
        ),
        out_specs=(
            P("tp", "lat", "lon", None),
            P(None, None, "tp"),
            P("tp", None),
            P(None, "tp"),
            P("tp", None),
        ),
        check_vma=False,
    )
```

```python
import functools

import jax
import jax.numpy as jnp
from jax import lax
from jax.experimental import pallas as pl
from jax.experimental.pallas import tpu as pltpu
from jax.sharding import Mesh
from jax.sharding import PartitionSpec as P

D = 512
FF = 2048
WLAT = 6
WLON = 12
SEATS = 144
WINS = 4
TOK = SEATS * WINS
EPS = 1e-05
GELU_C = 0.7978845608028654
BF = jnp.bfloat16
F32 = jnp.float32
AXES = ("x", "yl", "z", "c", "tp")
VMEM_LIMIT = 48 * 1024 * 1024


def pairs_of(move):
    pairs = []
    for x in range(4):
        for yl in range(2):
            for z in range(8):
                for c in range(2):
                    for t in range(2):
                        dest = move(x, yl, z, c, t)
                        if dest is not None:
                            pairs.append((rank(x, yl, z, c, t), rank(*dest)))
    return pairs


def rank(x, yl, z, c, t):
    return ((2 * x + yl) * 16 + 2 * z + c) * 2 + t


def send(value, move):
    return lax.ppermute(value, AXES, pairs_of(move))


def flip(value, x=0, yl=0, z=0, c=0, t=0):
    return send(value, lambda a, b, d, e, f: (a ^ x, b ^ yl, d ^ z, e ^ c, f ^ t))


def shift_lat(x, yl, step):
    lat = (2 * x + yl + step) % 8
    return lat // 2, lat % 2


def shift_lon(z, c, step):
    lon = (2 * z + c + step) % 16
    return lon // 2, lon % 2


def lon_move(step):
    def move(x, yl, z, c, t):
        zz, cc = shift_lon(z, c, step)
        return x, yl, zz, cc, t

    return move


def far_move(x, yl, z, c, t):
    if t == 1:
        return x, yl, z, c, 0
    xx, yy = shift_lat(x, yl, -1)
    return xx, yy, z, c, 1


def far_back(x, yl, z, c, t):
    if t == 0:
        return x, yl, z, c, 1
    xx, yy = shift_lat(x, yl, 1)
    return xx, yy, z, c, 0


def lat_move(step):
    def move(x, yl, z, c, t):
        if t == 0:
            return None
        xx, yy = shift_lat(x, yl, step)
        return xx, yy, z, c, t

    return move


def fence(values, after):
    n = len(values)
    anywhere = pl.BlockSpec(memory_space=pl.ANY)
    return pl.pallas_call(
        lambda *refs: None,
        out_shape=tuple(jax.ShapeDtypeStruct(v.shape, v.dtype) for v in values),
        in_specs=[anywhere] * (n + len(after)),
        out_specs=tuple([anywhere] * n),
        input_output_aliases={i: i for i in range(n)},
        name="fence",
    )(*values, *after)


def band_pieces(tile, t):
    first = t == 0
    return (
        jnp.where(first, tile[9:12], tile[3:6]),
        jnp.where(first, tile[0:3], tile[6:9]),
        tile[0:3],
    )


def exchange_rows(pieces):
    near, far, below = pieces
    return flip(near, t=1), send(far, far_move), send(below, lat_move(-1))


def first_columns(tile, near, far, below, t):
    edge = tile[:, :6]
    own = jnp.where(t == 0, edge[3:9], jnp.concatenate([edge[9:12], below[:, :6]], 0))
    return jnp.concatenate([own, near[:, :6], far[:, :6]], 0)


def to_windows(band):
    width = band.shape[-1]
    return band.reshape(12, WINS, WLON, width).transpose(1, 0, 2, 3).reshape(TOK, width)


def load_windows(t, tile, near, far, below, moved, stage, wins):
    for row in range(12):
        if row < 3:
            value = tile[3 + row + 6 * t].astype(F32)
        elif row < 6:
            value = jnp.where(t == 0, tile[3 + row].astype(F32), below[row - 3].astype(F32))
        elif row < 9:
            value = near[row - 6].astype(F32)
        else:
            value = far[row - 9].astype(F32)
        stage[row, 0:48] = value
        stage[row, 48:54] = moved[row].astype(F32)
        for w in range(WINS):
            start = w * SEATS + row * WLON
            wins[start : start + WLON, :] = stage[row, 6 + 12 * w : 18 + 12 * w]


def store_windows(wins, stage, band, tail):
    for row in range(12):
        for w in range(WINS):
            start = w * SEATS + row * WLON
            stage[row, 6 + 12 * w : 18 + 12 * w] = wins[start : start + WLON, :]
        band[row] = stage[row, 0:48].astype(BF)
        tail[row] = stage[row, 48:54].astype(BF)


def norm(value, gain):
    centered = value - jnp.mean(value, -1, keepdims=True)
    rstd = lax.rsqrt(jnp.mean(centered * centered, -1, keepdims=True) + EPS)
    xhat = centered * rstd
    return xhat * gain, xhat, rstd


def dot(a, b):
    return lax.dot_general(a, b, (((1,), (0,)), ((), ())), preferred_element_type=F32)


def dot_nt(a, b):
    return lax.dot_general(a, b, (((1,), (1,)), ((), ())), preferred_element_type=F32)


def dot_tn(a, b):
    return lax.dot_general(a, b, (((0,), (0,)), ((), ())), preferred_element_type=F32)


def head_mask(h):
    lane = lax.broadcasted_iota(jnp.int32, (1, 128), 1)
    return (lane < 64) if h == 0 else (lane >= 64)


def attend_kernel(
    place, tile, near, far, below, moved, labc, labr, g1, wq_own, wo_own, wqo_m, wqo_s,
    n1t_ref, qkv_ref, prob_ref, heads_ref, wo_full, mixed_ref, n1_scr, stage, wins,
):
    c = place[3]
    mine = pl.ds(pl.multiple_of(c * 256, 256), 256)
    sibs = pl.ds(pl.multiple_of((1 - c) * 256, 256), 256)
    load_windows(place[4], tile, near, far, below, moved, stage, wins)
    x = wins[...]
    normed = norm(x, g1[...])[0]
    n1_scr[...] = normed.astype(BF)
    n1t_ref[...] = normed.T.astype(BF)
    n1 = n1_scr[...]
    for i in range(3):
        scale = 0.125 if i == 0 else 1.0
        own = dot(n1, wq_own[i]).astype(BF)
        other = (dot(n1_scr[:, mine], wqo_m[i]) + dot(n1_scr[:, sibs], wqo_s[i])).astype(BF)
        qkv_ref[:, i * 512 : i * 512 + 256] = own * BF(scale)
        qkv_ref[:, i * 512 + 256 : i * 512 + 512] = other * BF(scale)

    def window(w, carry):
        rows = pl.ds(pl.multiple_of(w * SEATS, 16), SEATS)
        same = labc[rows, 0:1] == labr[w, 0:1, :]
        for p in range(4):
            q2 = qkv_ref[rows, p * 128 : p * 128 + 128]
            k2 = qkv_ref[rows, 512 + p * 128 : 640 + p * 128]
            v2 = qkv_ref[rows, 1024 + p * 128 : 1152 + p * 128]
            total = None
            for h in range(2):
                keep = head_mask(h)
                scores = dot_nt(jnp.where(keep, q2, BF(0)), k2)
                scores = jnp.where(same, scores, -1e30)
                expo = jnp.exp(scores - jnp.max(scores, -1, keepdims=True))
                prob = (expo * (1.0 / jnp.sum(expo, -1, keepdims=True))).astype(BF)
                prob_ref[w * 8 + p * 2 + h] = prob
                part = dot(prob, jnp.where(keep, v2, BF(0)))
                total = part if total is None else total + part
            heads_ref[rows, p * 128 : p * 128 + 128] = total.astype(BF)
        return carry

    lax.fori_loop(0, WINS, window, 0)
    wo_full[0:256, :] = wo_own[...]
    wo_full[256:512, mine] = wqo_m[3]
    wo_full[256:512, sibs] = wqo_s[3]
    attn = dot(heads_ref[...], wo_full[...]).astype(BF).astype(F32)
    mixed_ref[...] = (x + attn).astype(BF)


def gelu_parts(v):
    square = v * v
    tanh_v = jnp.tanh(GELU_C * v * (1.0 + 0.044715 * square))
    half = 0.5 * (1.0 + tanh_v)
    slope = half + 0.5 * v * (1.0 - tanh_v * tanh_v) * (GELU_C + (3.0 * 0.044715 * GELU_C) * square)
    return v * half, slope


def store_rows(out, block, lead, cols):
    for yl in range(2):
        for z in range(8):
            rows = slice(z * 32 + yl * 16, z * 32 + yl * 16 + 16)
            out[lead + (yl, z, slice(None), cols)] = block[rows].astype(BF)


def mlp_kernel(
    place, mixed_ref, tile, near, far, below, moved, g2, w1_own, w2_own, w12_m, w12_s,
    band, tail, dm_ref, keep, away,
    n2t, cott, hid_scr, dpre_scr, stage, wins,
):
    mx, c, mt = place[0], place[3], place[4]
    mine = pl.ds(pl.multiple_of(c * 256, 256), 256)
    sibs = pl.ds(pl.multiple_of((1 - c) * 256, 256), 256)
    load_windows(mt, tile, near, far, below, moved, stage, wins)
    gain = g2[...]
    mixed = mixed_ref[...].astype(F32)
    normed, xhat, rstd = norm(mixed, gain)
    n2 = normed.astype(BF)
    n2t[...] = normed.T.astype(BF)
    cott[...] = wins[...].T.astype(BF)
    cot = wins[...].astype(BF)
    blocks = [(0, x, w1_own, w2_own, x) for x in range(4)]
    for pair, half in ((w12_m, c), (w12_s, 1 - c)):
        blocks += [(1, 2 * half + i, pair.at[0], pair.at[1], i) for i in range(2)]
    for n, (t, x, w1, w2, i) in enumerate(blocks):
        cols = slice(i * 256, i * 256 + 256)
        place_cols = slice(n * 256, n * 256 + 256)
        hidden, slope = gelu_parts(dot(n2, w1[:, cols]))
        hidden = hidden.astype(BF)
        dpre = (dot_nt(cot, w2[cols, :]) * slope).astype(BF)
        hid_scr[:, place_cols] = hidden
        dpre_scr[:, place_cols] = dpre
        lead = (x ^ mx, t ^ mt)
        for rows, out in ((sibs, away), (mine, keep)):
            store_rows(out, dot(n2t[rows, :], dpre), lead, slice(0, 256))
            store_rows(out, dot(cott[rows, :], hidden), lead, slice(256, 512))
    d_norm = (
        dot_nt(dpre_scr[:, :1024], w1_own[...])
        + dot_nt(dpre_scr[:, 1024:1536], w12_m[0])
        + dot_nt(dpre_scr[:, 1536:], w12_s[0])
    )
    scaled = d_norm * gain
    dm = wins[...] + rstd * (
        scaled
        - jnp.mean(scaled, -1, keepdims=True)
        - xhat * jnp.mean(scaled * xhat, -1, keepdims=True)
    )
    dm_ref[...] = dm.astype(BF)
    wins[...] = mixed + (
        dot(hid_scr[:, :1024], w2_own[...])
        + dot(hid_scr[:, 1024:1536], w12_m[1])
        + dot(hid_scr[:, 1536:], w12_s[1])
    )
    store_windows(wins, stage, band, tail)


def attend_back_kernel(
    place, dm_ref, heads_ref, prob_ref, qkv_ref, n1t_ref, wo_full, first, second,
    keep, away,
    dmt, dheads, dqkv,
):
    mx, c, mt = place[0], place[3], place[4]
    mine = pl.ds(pl.multiple_of(c * 256, 256), 256)
    sibs = pl.ds(pl.multiple_of((1 - c) * 256, 256), 256)
    dm = dm_ref[...]
    dmt[...] = dm.astype(F32).T.astype(BF)
    dheads[...] = dot_nt(dm, wo_full[...]).astype(BF)

    def window(w, carry):
        rows = pl.ds(pl.multiple_of(w * SEATS, 16), SEATS)
        for p in range(4):
            pc = slice(p * 128, p * 128 + 128)
            q2 = qkv_ref[rows, p * 128 : p * 128 + 128]
            k2 = qkv_ref[rows, 512 + p * 128 : 640 + p * 128]
            v2 = qkv_ref[rows, 1024 + p * 128 : 1152 + p * 128]
            do2 = dheads[rows, pc]
            dq = dk = dv = None
            for h in range(2):
                keep = head_mask(h)
                prob_b = prob_ref[w * 8 + p * 2 + h]
                prob = prob_b.astype(F32)
                do_h = jnp.where(keep, do2, BF(0))
                d_prob = dot_nt(do_h, v2)
                moment = jnp.sum(prob * d_prob, -1, keepdims=True)
                d_scores = (prob * (d_prob - moment)).astype(BF)
                pq = dot(d_scores, jnp.where(keep, k2, BF(0)))
                pk = dot_tn(d_scores, jnp.where(keep, q2, BF(0)))
                pv = dot_tn(prob_b, do_h)
                dq = pq if dq is None else dq + pq
                dk = pk if dk is None else dk + pk
                dv = pv if dv is None else dv + pv
            dqkv[rows, p * 128 : p * 128 + 128] = (dq * 0.125).astype(BF)
            dqkv[rows, 512 + p * 128 : 640 + p * 128] = dk.astype(BF)
            dqkv[rows, 1024 + p * 128 : 1152 + p * 128] = dv.astype(BF)
        return carry

    lax.fori_loop(0, WINS, window, 0)
    for rows, out in ((sibs, away), (mine, keep)):
        for t in range(2):
            for half in range(2):
                for which in range(2):
                    if which == 0 or half == 0:
                        start = (2 * which + half) * 512 + t * 256
                        grad = dot(n1t_ref[rows, :], dqkv[:, start : start + 256])
                    else:
                        grad = dot(dmt[rows, :], heads_ref[:, t * 256 : t * 256 + 256])
                    for sub in range(2):
                        lead = ((half * 2 + sub) ^ mx, t ^ mt)
                        cols = slice(which * 128, which * 128 + 128)
                        store_rows(out, grad[:, sub * 128 : sub * 128 + 128], lead, cols)


def whole(shape, dtype=BF):
    return jax.ShapeDtypeStruct(shape, dtype)


def call(kernel, args, outs, scratch=(), place=None, flops=0, name=None, after=()):
    spec = pl.BlockSpec(memory_space=pltpu.VMEM)
    specs = [spec] * len(args) + [pl.BlockSpec(memory_space=pl.ANY)] * len(after)
    args = tuple(args) + tuple(after)
    if place is not None:
        args = (place,) + args
        specs = [pl.BlockSpec(memory_space=pltpu.SMEM)] + specs
    size = sum(a.size * a.dtype.itemsize for a in list(args) + list(outs))
    return pl.pallas_call(
        kernel,
        out_shape=tuple(outs),
        in_specs=specs,
        out_specs=tuple([spec] * len(outs)),
        scratch_shapes=list(scratch),
        compiler_params=pltpu.CompilerParams(vmem_limit_bytes=VMEM_LIMIT),
        cost_estimate=pl.CostEstimate(flops=flops, bytes_accessed=size, transcendentals=0),
        name=name,
    )(*args)


def add(*values):
    total = values[0].astype(F32)
    for value in values[1:]:
        total = total + value.astype(F32)
    return total.astype(BF)


def core_sum_kernel(keep, arrived, *outs):
    for x in range(4):
        outs[x][...] = add(keep[x], arrived[x])


def x_sum_kernel(*refs):
    fc, at, out = refs[0:4], refs[4:8], refs[-1]
    out[:, :, :, :, :512] = add(*[r[...] for r in fc])
    out[:, :, :, :, 512:] = add(*[r[...] for r in at])


def last_sum_kernel(parts, out):
    total = parts[0].astype(F32)
    for i in range(1, 32):
        total = total + parts[i].astype(F32)
    for z in range(8):
        out[z] = total.astype(BF)


def copies_kernel(part, out):
    for i in range(8):
        out[i] = part[...]


def place_kernel(place, mine, sib, gq, go, g1, g2, scr2, scro):
    c = place[3]
    for src, cc in ((mine, c), (sib, 1 - c)):
        base = cc * 256
        for yl in range(2):
            for x in range(4):
                for z in range(8):
                    rows = pl.ds(pl.multiple_of(base + z * 32 + yl * 16, 16), 16)
                    chunk = src[2 * x + yl, z]
                    lo = (x % 2) * 128
                    g1[rows, x * 256 : x * 256 + 256] = chunk[:, :256]
                    scr2[rows, x * 256 : x * 256 + 256] = chunk[:, 256:512]
                    gq[x // 2, rows, lo : lo + 128] = chunk[:, 512:640]
                    if x < 2:
                        gq[2, rows, lo : lo + 128] = chunk[:, 640:]
                    else:
                        scro[rows, lo : lo + 128] = chunk[:, 640:]
    for i in range(4):
        g2[i * 256 : i * 256 + 256, :] = scr2[:, i * 256 : i * 256 + 256].astype(F32).T.astype(BF)
    go[...] = scro[...].astype(F32).T.astype(BF)


def core_phase(keep, away, width):
    outs = [whole((2, 2, 8, 16, width))] * 4
    return call(core_sum_kernel, (keep, flip(away, c=1)), outs, name="core_sum")


def x_phase(cut):
    return [cut[0]] + [flip(cut[k], x=k) for k in (1, 2, 3)]


def reduce_and_gather(place, fc, at, after):
    (total,) = call(x_sum_kernel, (*fc, *at), [whole((2, 2, 8, 16, 768))], name="x_sum", after=after)
    parts = lax.all_to_all(total.reshape(32, 16, 768), ("tp", "yl", "z"), 0, 0)
    (chunks,) = call(last_sum_kernel, (parts,), [whole((8, 16, 768))], name="last_sum")
    column = lax.all_to_all(chunks, "z", 0, 0)
    (columns,) = call(copies_kernel, (column,), [whole((8, 8, 16, 768))], name="copies")
    mine = lax.all_to_all(columns, ("x", "yl"), 0, 0)
    sib = flip(mine, c=1)
    outs = [whole((3, 512, 256)), whole((256, 512)), whole((512, 1024)), whole((1024, 512))]
    scratch = [pltpu.VMEM((512, 1024), BF), pltpu.VMEM((512, 256), BF)]
    return call(place_kernel, (mine, sib), outs, scratch, place, name="place")


def per_device(tokens, labels, gain_one, second_norm_gain, w_qkv, w_out, w_fc1, w_fc2, cotangent):
    x, yl, z, c, t = [lax.axis_index(name) for name in AXES]
    place = jnp.stack([x, yl, z, c, t]).astype(jnp.int32)
    tile, cot = tokens[0], cotangent[0]

    rows = exchange_rows(band_pieces(tile, t))
    wqo = jnp.concatenate(
        [
            lax.dynamic_slice_in_dim(w_qkv, c * 256, 256, 1),
            lax.dynamic_slice_in_dim(w_out, c * 256, 256, 1)[None],
        ],
        0,
    )
    wqo = flip(wqo, yl=1, t=1)
    edge = first_columns(tile, *rows, t)
    moved = send(edge, lon_move(-1))

    w12 = jnp.stack(
        [
            lax.dynamic_slice_in_dim(w_fc1, c * 512, 512, 1),
            lax.dynamic_slice_in_dim(w_fc2, c * 512, 512, 0),
        ]
    )
    *pieces, w12 = fence((*band_pieces(cot, t), w12), (edge,))
    cot_rows = exchange_rows(pieces)
    w12 = flip(w12, yl=1, t=1)
    cot_edge = first_columns(cot, *cot_rows, t)
    cot_moved = send(cot_edge, lon_move(-1))
    wqo_sib = flip(wqo, c=1)

    band = lax.dynamic_slice_in_dim(labels, t * 6, 6, 1)
    band = jnp.where(t == 0, band, band[::-1]).reshape(12, 48, 1)
    lab = to_windows(band).reshape(TOK)
    labc = jnp.broadcast_to(lab[:, None], (TOK, 128))
    labr = jnp.broadcast_to(lab.reshape(WINS, 1, SEATS), (WINS, 8, SEATS))

    stage = [pltpu.VMEM((12, 56, D), F32), pltpu.VMEM((TOK, D), F32)]
    n1t, qkv, prob, heads, wo_full, mixed = call(
        without(attend_kernel, 13, 1),
        (tile, *rows, moved, labc, labr, gain_one[None], w_qkv, w_out, wqo, wqo_sib),
        [
            whole((D, TOK)), whole((TOK, 3 * D)), whole((WINS * 8, SEATS, SEATS)),
            whole((TOK, D)), whole((D, D)), whole((TOK, D)),
        ],
        [pltpu.VMEM((TOK, D), BF)] + stage,
        place,
        flops=3 * 10**9,
        name="attend",
        after=(cot_edge,),
    )
    w12_sib = flip(w12, c=1)
    grads = [whole((4, 2, 2, 8, 16, 512))] * 2
    out_band, tail, dm, *fc = call(
        mlp_kernel,
        (mixed, cot, *cot_rows, cot_moved, second_norm_gain[None], w_fc1, w_fc2, w12, w12_sib),
        [whole((12, 48, D)), whole((12, 6, D)), whole((TOK, D))] + grads,
        [
            pltpu.VMEM((D, TOK), BF), pltpu.VMEM((D, TOK), BF),
            pltpu.VMEM((TOK, FF), BF), pltpu.VMEM((TOK, FF), BF),
        ]
        + stage,
        place,
        flops=8 * 10**9,
        name="mlp",
    )
    fc_cut = core_phase(*fc, 512)
    out_moved = send(tail, lon_move(1))
    fc_parts = x_phase(fc_cut)
    grads = [whole((4, 2, 2, 8, 16, 256))] * 2
    at = call(
        attend_back_kernel,
        (dm, heads, prob, qkv, n1t, wo_full),
        grads,
        [pltpu.VMEM((D, TOK), BF), pltpu.VMEM((TOK, D), BF), pltpu.VMEM((TOK, 3 * D), BF)],
        place,
        flops=5 * 10**9,
        name="attend_back",
        after=(fc_cut[0], out_moved),
    )
    at_cut = core_phase(*at, 256)
    at_parts = x_phase(at_cut)

    out = jnp.concatenate([out_moved, out_band[:, 6:]], 1)
    near, far, above = fence((out[6:9], out[9:12], out[3:6]), (at_cut[0],))
    near, far, above = flip(near, t=1), send(far, far_back), send(above, lat_move(1))
    gq, go, g1, g2 = reduce_and_gather(place, fc_parts, at_parts, (near, far, above))
    out = jnp.where(
        t == 0,
        jnp.concatenate([far, out[0:6], near], 0),
        jnp.concatenate([above, near, far, out[0:3]], 0),
    )
    return out[None], gq, go, g1, g2


def without(kernel, start, count):
    return lambda *refs: kernel(*refs[:start], *refs[start + count :])


def solution(mesh):
    fine = Mesh(mesh.devices.reshape(4, 2, 8, 2, 2), AXES)
    lat, lon = ("x", "yl"), ("z", "c")
    return jax.shard_map(
        per_device,
        mesh=fine,
        in_specs=(
            P("tp", lat, lon, None),
            P(None, lat, lon),
            P(),
            P(),
            P(None, None, "tp"),
            P("tp", None),
            P(None, "tp"),
            P("tp", None),
            P("tp", lat, lon, None),
        ),
        out_specs=(
            P("tp", lat, lon, None),
            P(None, None, "tp"),
            P("tp", None),
            P(None, "tp"),
            P("tp", None),
        ),
        check_vma=False,
    )
```

```python
import functools

import jax
import jax.numpy as jnp
from jax import lax
from jax.experimental import pallas as pl
from jax.experimental.pallas import tpu as pltpu
from jax.sharding import Mesh
from jax.sharding import PartitionSpec as P

D = 512
FF = 2048
WLAT = 6
WLON = 12
SEATS = 144
WINS = 4
TOK = SEATS * WINS
EPS = 1e-05
GELU_C = 0.7978845608028654
BF = jnp.bfloat16
F32 = jnp.float32
AXES = ("x", "yl", "z", "c", "tp")
VMEM_LIMIT = 48 * 1024 * 1024


def pairs_of(move):
    pairs = []
    for x in range(4):
        for yl in range(2):
            for z in range(8):
                for c in range(2):
                    for t in range(2):
                        dest = move(x, yl, z, c, t)
                        if dest is not None:
                            pairs.append((rank(x, yl, z, c, t), rank(*dest)))
    return pairs


def rank(x, yl, z, c, t):
    return ((2 * x + yl) * 16 + 2 * z + c) * 2 + t


def send(value, move):
    return lax.ppermute(value, AXES, pairs_of(move))


def flip(value, x=0, yl=0, z=0, c=0, t=0):
    return send(value, lambda a, b, d, e, f: (a ^ x, b ^ yl, d ^ z, e ^ c, f ^ t))


def shift_lat(x, yl, step):
    lat = (2 * x + yl + step) % 8
    return lat // 2, lat % 2


def shift_lon(z, c, step):
    lon = (2 * z + c + step) % 16
    return lon // 2, lon % 2


def lon_move(step):
    def move(x, yl, z, c, t):
        zz, cc = shift_lon(z, c, step)
        return x, yl, zz, cc, t

    return move


def far_move(x, yl, z, c, t):
    if t == 1:
        return x, yl, z, c, 0
    xx, yy = shift_lat(x, yl, -1)
    return xx, yy, z, c, 1


def far_back(x, yl, z, c, t):
    if t == 0:
        return x, yl, z, c, 1
    xx, yy = shift_lat(x, yl, 1)
    return xx, yy, z, c, 0


def lat_move(step):
    def move(x, yl, z, c, t):
        if t == 0:
            return None
        xx, yy = shift_lat(x, yl, step)
        return xx, yy, z, c, t

    return move


def fence(values, after):
    n = len(values)
    anywhere = pl.BlockSpec(memory_space=pl.ANY)
    return pl.pallas_call(
        lambda *refs: None,
        out_shape=tuple(jax.ShapeDtypeStruct(v.shape, v.dtype) for v in values),
        in_specs=[anywhere] * (n + len(after)),
        out_specs=tuple([anywhere] * n),
        input_output_aliases={i: i for i in range(n)},
        name="fence",
    )(*values, *after)


def pieces_kernel(place, tile, near, far, below):
    t = place[4]
    for i in range(3):
        near[i] = tile[9 + i - 6 * t]
        far[i] = tile[i + 6 * t]
        below[i] = tile[i]


def band_pieces(place, tile, name):
    return call(pieces_kernel, (tile,), [whole((3, 48, D))] * 3, place=place, name=name)


def exchange_rows(pieces):
    near, far, below = pieces
    return flip(near, t=1), send(far, far_move), send(below, lat_move(-1))


def edge_kernel(place, tile, near, far, below, edge):
    t = place[4]
    for i in range(3):
        edge[i] = tile[3 + i + 6 * t, :6]
        edge[3 + i] = jnp.where(t == 0, tile[6 + i, :6].astype(F32), below[i, :6].astype(F32)).astype(BF)
        edge[6 + i] = near[i, :6]
        edge[9 + i] = far[i, :6]


def first_columns(place, tile, rows, name, after=()):
    kernel = without(edge_kernel, 5, len(after))
    (edge,) = call(kernel, (tile, *rows), [whole((12, 6, D))], place=place, name=name, after=after)
    return edge


def half_of_attend_weights(place, w_qkv, w_out):
    def kernel(place, wq, wo, out):
        out[0:3] = wq[...]
        out[3] = wo[...]

    return halves(
        kernel, place, (w_qkv, w_out), (4, 256, 256),
        [((3, 256, 256), lambda i, p: (0, p[3], 0)), ((256, 256), lambda i, p: (0, p[3]))], "half_attend",
    )


def half_of_mlp_weights(place, w_fc1, w_fc2):
    def kernel(place, w1, w2, out):
        out[0] = w1[...]
        out[1] = w2[...]

    return halves(
        kernel, place, (w_fc1, w_fc2), (2, 512, 512),
        [((512, 512), lambda i, p: (0, p[3])), ((512, 512), lambda i, p: (p[3], 0))], "half_mlp",
    )


def halves(kernel, place, args, shape, specs, name):
    return pl.pallas_call(
        kernel,
        out_shape=whole(shape),
        grid_spec=pltpu.PrefetchScalarGridSpec(
            num_scalar_prefetch=1,
            grid=(1,),
            in_specs=[pl.BlockSpec(block, index) for block, index in specs],
            out_specs=pl.BlockSpec(shape, lambda i, p: (0,) * len(shape)),
        ),
        compiler_params=pltpu.CompilerParams(vmem_limit_bytes=VMEM_LIMIT),
        name=name,
    )(place, *args)


def to_windows(band):
    width = band.shape[-1]
    return band.reshape(12, WINS, WLON, width).transpose(1, 0, 2, 3).reshape(TOK, width)


def load_windows(t, tile, near, far, below, moved, stage, wins):
    for row in range(12):
        if row < 3:
            value = tile[3 + row + 6 * t].astype(F32)
        elif row < 6:
            value = jnp.where(t == 0, tile[3 + row].astype(F32), below[row - 3].astype(F32))
        elif row < 9:
            value = near[row - 6].astype(F32)
        else:
            value = far[row - 9].astype(F32)
        stage[row, 0:48] = value
        stage[row, 48:54] = moved[row].astype(F32)
        for w in range(WINS):
            start = w * SEATS + row * WLON
            wins[start : start + WLON, :] = stage[row, 6 + 12 * w : 18 + 12 * w]


def store_windows(wins, stage, band, tail):
    for row in range(12):
        for w in range(WINS):
            start = w * SEATS + row * WLON
            stage[row, 6 + 12 * w : 18 + 12 * w] = wins[start : start + WLON, :]
        band[row] = stage[row, 0:48].astype(BF)
        tail[row] = stage[row, 48:54].astype(BF)


def norm(value, gain):
    centered = value - jnp.mean(value, -1, keepdims=True)
    rstd = lax.rsqrt(jnp.mean(centered * centered, -1, keepdims=True) + EPS)
    xhat = centered * rstd
    return xhat * gain, xhat, rstd


def dot(a, b):
    return lax.dot_general(a, b, (((1,), (0,)), ((), ())), preferred_element_type=F32)


def dot_nt(a, b):
    return lax.dot_general(a, b, (((1,), (1,)), ((), ())), preferred_element_type=F32)


def dot_tn(a, b):
    return lax.dot_general(a, b, (((0,), (0,)), ((), ())), preferred_element_type=F32)


def head_mask(h):
    lane = lax.broadcasted_iota(jnp.int32, (1, 128), 1)
    return (lane < 64) if h == 0 else (lane >= 64)


def attend_kernel(
    place, tile, near, far, below, moved, labc, labr, g1, wq_own, wo_own, wqo_m, wqo_s,
    n1t_ref, qkv_ref, prob_ref, heads_ref, wo_full, mixed_ref, n1_scr, stage, wins,
):
    c = place[3]
    mine = pl.ds(pl.multiple_of(c * 256, 256), 256)
    sibs = pl.ds(pl.multiple_of((1 - c) * 256, 256), 256)
    load_windows(place[4], tile, near, far, below, moved, stage, wins)
    x = wins[...]
    normed = norm(x, g1[...])[0]
    n1_scr[...] = normed.astype(BF)
    n1t_ref[...] = normed.T.astype(BF)
    n1 = n1_scr[...]
    for i in range(3):
        scale = 0.125 if i == 0 else 1.0
        own = dot(n1, wq_own[i]).astype(BF)
        other = (dot(n1_scr[:, mine], wqo_m[i]) + dot(n1_scr[:, sibs], wqo_s[i])).astype(BF)
        qkv_ref[:, i * 512 : i * 512 + 256] = own * BF(scale)
        qkv_ref[:, i * 512 + 256 : i * 512 + 512] = other * BF(scale)

    def window(w, carry):
        rows = pl.ds(pl.multiple_of(w * SEATS, 16), SEATS)
        same = labc[rows, 0:1] == labr[w, 0:1, :]
        for p in range(4):
            q2 = qkv_ref[rows, p * 128 : p * 128 + 128]
            k2 = qkv_ref[rows, 512 + p * 128 : 640 + p * 128]
            v2 = qkv_ref[rows, 1024 + p * 128 : 1152 + p * 128]
            total = None
            for h in range(2):
                keep = head_mask(h)
                scores = dot_nt(jnp.where(keep, q2, BF(0)), k2)
                scores = jnp.where(same, scores, -1e30)
                expo = jnp.exp(scores - jnp.max(scores, -1, keepdims=True))
                prob = (expo * (1.0 / jnp.sum(expo, -1, keepdims=True))).astype(BF)
                prob_ref[w * 8 + p * 2 + h] = prob
                part = dot(prob, jnp.where(keep, v2, BF(0)))
                total = part if total is None else total + part
            heads_ref[rows, p * 128 : p * 128 + 128] = total.astype(BF)
        return carry

    lax.fori_loop(0, WINS, window, 0)
    wo_full[0:256, :] = wo_own[...]
    wo_full[256:512, mine] = wqo_m[3]
    wo_full[256:512, sibs] = wqo_s[3]
    attn = dot(heads_ref[...], wo_full[...]).astype(BF).astype(F32)
    mixed_ref[...] = (x + attn).astype(BF)


def gelu_parts(v):
    square = v * v
    tanh_v = jnp.tanh(GELU_C * v * (1.0 + 0.044715 * square))
    half = 0.5 * (1.0 + tanh_v)
    slope = half + 0.5 * v * (1.0 - tanh_v * tanh_v) * (GELU_C + (3.0 * 0.044715 * GELU_C) * square)
    return v * half, slope


def store_rows(out, block, lead, cols):
    for yl in range(2):
        for z in range(8):
            rows = slice(z * 32 + yl * 16, z * 32 + yl * 16 + 16)
            out[lead + (yl, z, slice(None), cols)] = block[rows].astype(BF)


def mlp_block(w1, w2, cols, n2, cot):
    hidden, slope = gelu_parts(dot(n2, w1[:, cols]))
    return hidden.astype(BF), (dot_nt(cot, w2[cols, :]) * slope).astype(BF)


def store_grads(n2t, cott, hidden, dpre, lead, c, keep, away):
    mine = pl.ds(pl.multiple_of(c * 256, 256), 256)
    sibs = pl.ds(pl.multiple_of((1 - c) * 256, 256), 256)
    for rows, out in ((sibs, away), (mine, keep)):
        store_rows(out, dot(n2t[rows, :], dpre), lead, slice(0, 256))
        store_rows(out, dot(cott[rows, :], hidden), lead, slice(256, 512))


def mlp_own_kernel(
    place, mixed_ref, tile, near, far, below, moved, g2, w1_own, w2_own,
    n2_ref, n2t, cot_ref, cott, out_acc, norm_acc, keep, away,
    hid_scr, dpre_scr, stage, wins,
):
    mx, c = place[0], place[3]
    load_windows(place[4], tile, near, far, below, moved, stage, wins)
    mixed = mixed_ref[...].astype(F32)
    normed = norm(mixed, g2[...])[0]
    n2_ref[...] = normed.astype(BF)
    n2t[...] = normed.T.astype(BF)
    cott[...] = wins[...].T.astype(BF)
    cot_ref[...] = wins[...].astype(BF)
    n2, cot = n2_ref[...], cot_ref[...]
    for x in range(4):
        cols = slice(x * 256, x * 256 + 256)
        hidden, dpre = mlp_block(w1_own, w2_own, cols, n2, cot)
        hid_scr[:, cols] = hidden
        dpre_scr[:, cols] = dpre
        store_grads(n2t, cott, hidden, dpre, (x ^ mx,), c, keep, away)
    out_acc[...] = mixed + dot(hid_scr[...], w2_own[...])
    norm_acc[...] = dot_nt(dpre_scr[...], w1_own[...])


def mlp_other_kernel(
    place, mixed_ref, n2_ref, n2t, cot_ref, cott, out_acc, norm_acc, g2, w12_m, w12_s,
    band, tail, dm_ref, keep, away,
    hid_scr, dpre_scr, stage, wins,
):
    mx, c = place[0], place[3]
    n2, cot = n2_ref[...], cot_ref[...]
    for n, (pair, half) in enumerate(((w12_m, c), (w12_s, 1 - c))):
        for i in range(2):
            cols = slice(i * 256, i * 256 + 256)
            hidden, dpre = mlp_block(pair.at[0], pair.at[1], cols, n2, cot)
            hid_scr[:, n * 512 + i * 256 : n * 512 + i * 256 + 256] = hidden
            dpre_scr[:, n * 512 + i * 256 : n * 512 + i * 256 + 256] = dpre
            store_grads(n2t, cott, hidden, dpre, ((2 * half + i) ^ mx,), c, keep, away)
    d_norm = norm_acc[...] + (
        dot_nt(dpre_scr[:, :512], w12_m[0]) + dot_nt(dpre_scr[:, 512:], w12_s[0])
    )
    gain = g2[...]
    xhat, rstd = norm(mixed_ref[...].astype(F32), gain)[1:]
    scaled = d_norm * gain
    dm = cot.astype(F32) + rstd * (
        scaled
        - jnp.mean(scaled, -1, keepdims=True)
        - xhat * jnp.mean(scaled * xhat, -1, keepdims=True)
    )
    dm_ref[...] = dm.astype(BF)
    wins[...] = out_acc[...] + (dot(hid_scr[:, :512], w12_m[1]) + dot(hid_scr[:, 512:], w12_s[1]))
    store_windows(wins, stage, band, tail)


def attend_back_kernel(
    dm_ref, prob_ref, qkv_ref, wo_full, first, second,
    dqkv, dmt,
    dheads,
):
    dm = dm_ref[...]
    dmt[...] = dm.astype(F32).T.astype(BF)
    dheads[...] = dot_nt(dm, wo_full[...]).astype(BF)

    def window(w, carry):
        rows = pl.ds(pl.multiple_of(w * SEATS, 16), SEATS)
        for p in range(4):
            pc = slice(p * 128, p * 128 + 128)
            q2 = qkv_ref[rows, p * 128 : p * 128 + 128]
            k2 = qkv_ref[rows, 512 + p * 128 : 640 + p * 128]
            v2 = qkv_ref[rows, 1024 + p * 128 : 1152 + p * 128]
            do2 = dheads[rows, pc]
            dq = dk = dv = None
            for h in range(2):
                keep = head_mask(h)
                prob_b = prob_ref[w * 8 + p * 2 + h]
                prob = prob_b.astype(F32)
                do_h = jnp.where(keep, do2, BF(0))
                d_prob = dot_nt(do_h, v2)
                moment = jnp.sum(prob * d_prob, -1, keepdims=True)
                d_scores = (prob * (d_prob - moment)).astype(BF)
                pq = dot(d_scores, jnp.where(keep, k2, BF(0)))
                pk = dot_tn(d_scores, jnp.where(keep, q2, BF(0)))
                pv = dot_tn(prob_b, do_h)
                dq = pq if dq is None else dq + pq
                dk = pk if dk is None else dk + pk
                dv = pv if dv is None else dv + pv
            dqkv[rows, p * 128 : p * 128 + 128] = (dq * 0.125).astype(BF)
            dqkv[rows, 512 + p * 128 : 640 + p * 128] = dk.astype(BF)
            dqkv[rows, 1024 + p * 128 : 1152 + p * 128] = dv.astype(BF)
        return carry

    lax.fori_loop(0, WINS, window, 0)


def attend_grads_kernel(
    place, dqkv, dmt, heads_ref, n1t_ref, first, second, third,
    keep, away,
):
    mx, c, mt = place[0], place[3], place[4]
    mine = pl.ds(pl.multiple_of(c * 256, 256), 256)
    sibs = pl.ds(pl.multiple_of((1 - c) * 256, 256), 256)
    for rows, out in ((sibs, away), (mine, keep)):
        for t in range(2):
            for half in range(2):
                for which in range(2):
                    if which == 0 or half == 0:
                        start = (2 * which + half) * 512 + t * 256
                        grad = dot(n1t_ref[rows, :], dqkv[:, start : start + 256])
                    else:
                        grad = dot(dmt[rows, :], heads_ref[:, t * 256 : t * 256 + 256])
                    for sub in range(2):
                        lead = ((half * 2 + sub) ^ mx, t ^ mt)
                        cols = slice(which * 128, which * 128 + 128)
                        store_rows(out, grad[:, sub * 128 : sub * 128 + 128], lead, cols)


def whole(shape, dtype=BF):
    return jax.ShapeDtypeStruct(shape, dtype)


def call(kernel, args, outs, scratch=(), place=None, flops=0, name=None, after=()):
    spec = pl.BlockSpec(memory_space=pltpu.VMEM)
    specs = [spec] * len(args) + [pl.BlockSpec(memory_space=pl.ANY)] * len(after)
    args = tuple(args) + tuple(after)
    if place is not None:
        args = (place,) + args
        specs = [pl.BlockSpec(memory_space=pltpu.SMEM)] + specs
    size = sum(a.size * a.dtype.itemsize for a in list(args) + list(outs))
    return pl.pallas_call(
        kernel,
        out_shape=tuple(outs),
        in_specs=specs,
        out_specs=tuple([spec] * len(outs)),
        scratch_shapes=list(scratch),
        compiler_params=pltpu.CompilerParams(vmem_limit_bytes=VMEM_LIMIT),
        cost_estimate=pl.CostEstimate(flops=flops, bytes_accessed=size, transcendentals=0),
        name=name,
    )(*args)


def add(*values):
    total = values[0].astype(F32)
    for value in values[1:]:
        total = total + value.astype(F32)
    return total.astype(BF)


def core_sum_kernel(keep, arrived, *outs):
    for x in range(4):
        outs[x][...] = add(keep[x], arrived[x])


def x_sum_kernel(place, *refs):
    own, other, at, out = refs[0:4], refs[4:8], refs[8:12], refs[-1]
    t = place[4]
    out[t, :, :, :, :512] = add(*[r[...] for r in own])
    out[1 - t, :, :, :, :512] = add(*[r[...] for r in other])
    out[:, :, :, :, 512:] = add(*[r[...] for r in at])


def last_sum_kernel(parts, out):
    total = parts[0].astype(F32)
    for i in range(1, 32):
        total = total + parts[i].astype(F32)
    for z in range(8):
        out[z] = total.astype(BF)


def copies_kernel(part, out):
    for i in range(8):
        out[i] = part[...]


def place_kernel(place, mine, sib, gq, go, g1, g2, scr2, scro):
    c = place[3]
    for src, cc in ((mine, c), (sib, 1 - c)):
        base = cc * 256
        for yl in range(2):
            for x in range(4):
                for z in range(8):
                    rows = pl.ds(pl.multiple_of(base + z * 32 + yl * 16, 16), 16)
                    chunk = src[2 * x + yl, z]
                    lo = (x % 2) * 128
                    g1[rows, x * 256 : x * 256 + 256] = chunk[:, :256]
                    scr2[rows, x * 256 : x * 256 + 256] = chunk[:, 256:512]
                    gq[x // 2, rows, lo : lo + 128] = chunk[:, 512:640]
                    if x < 2:
                        gq[2, rows, lo : lo + 128] = chunk[:, 640:]
                    else:
                        scro[rows, lo : lo + 128] = chunk[:, 640:]
    for i in range(4):
        g2[i * 256 : i * 256 + 256, :] = scr2[:, i * 256 : i * 256 + 256].astype(F32).T.astype(BF)
    go[...] = scro[...].astype(F32).T.astype(BF)


def core_phase(keep, away):
    outs = [whole(keep.shape[1:])] * 4
    return call(core_sum_kernel, (keep, flip(away, c=1)), outs, name="core_sum")


def x_phase(cut):
    return [cut[0]] + [flip(cut[k], x=k) for k in (1, 2, 3)]


def reduce_and_gather(place, own, other, at, after):
    (total,) = call(
        x_sum_kernel, (*own, *other, *at), [whole((2, 2, 8, 16, 768))], (), place, name="x_sum", after=after
    )
    parts = lax.all_to_all(total.reshape(32, 16, 768), ("tp", "yl", "z"), 0, 0)
    (chunks,) = call(last_sum_kernel, (parts,), [whole((8, 16, 768))], name="last_sum")
    column = lax.all_to_all(chunks, "z", 0, 0)
    (columns,) = call(copies_kernel, (column,), [whole((8, 8, 16, 768))], name="copies")
    mine = lax.all_to_all(columns, ("x", "yl"), 0, 0)
    sib = flip(mine, c=1)
    outs = [whole((3, 512, 256)), whole((256, 512)), whole((512, 1024)), whole((1024, 512))]
    scratch = [pltpu.VMEM((512, 1024), BF), pltpu.VMEM((512, 256), BF)]
    return call(place_kernel, (mine, sib), outs, scratch, place, name="place")


def per_device(tokens, labels, gain_one, second_norm_gain, w_qkv, w_out, w_fc1, w_fc2, cotangent):
    x, yl, z, c, t = [lax.axis_index(name) for name in AXES]
    place = jnp.stack([x, yl, z, c, t]).astype(jnp.int32)
    tile, cot = tokens[0], cotangent[0]

    pieces = band_pieces(place, tile, "pieces")
    rows = exchange_rows(pieces)
    (wqo,) = fence((half_of_attend_weights(place, w_qkv, w_out),), (pieces[0],))
    wqo = flip(wqo, yl=1, t=1)
    edge = first_columns(place, tile, rows, "edge")
    moved = send(edge, lon_move(-1))
    (wqo,) = fence((wqo,), (edge,))

    cot_rows = exchange_rows(fence(band_pieces(place, cot, "cot_pieces"), (edge,)))
    wqo_sib = flip(wqo, c=1)
    (w12,) = fence((half_of_mlp_weights(place, w_fc1, w_fc2),), (wqo, moved))
    w12 = flip(w12, yl=1, t=1)
    cot_edge = first_columns(place, cot, cot_rows, "cot_edge", (moved,))
    cot_moved = send(cot_edge, lon_move(-1))

    band = lax.dynamic_slice_in_dim(labels, t * 6, 6, 1)
    band = jnp.where(t == 0, band, band[::-1]).reshape(12, 48, 1)
    lab = to_windows(band).reshape(TOK)
    labc = jnp.broadcast_to(lab[:, None], (TOK, 128))
    labr = jnp.broadcast_to(lab.reshape(WINS, 1, SEATS), (WINS, 8, SEATS))

    stage = [pltpu.VMEM((12, 56, D), F32), pltpu.VMEM((TOK, D), F32)]
    n1t, qkv, prob, heads, wo_full, mixed = call(
        without(attend_kernel, 13, 1),
        (tile, *rows, moved, labc, labr, gain_one[None], w_qkv, w_out, wqo, wqo_sib),
        [
            whole((D, TOK)), whole((TOK, 3 * D)), whole((WINS * 8, SEATS, SEATS)),
            whole((TOK, D)), whole((D, D)), whole((TOK, D)),
        ],
        [pltpu.VMEM((TOK, D), BF)] + stage,
        place,
        flops=3 * 10**9,
        name="attend",
        after=(cot_edge,),
    )
    grads = [whole((4, 2, 8, 16, 512))] * 2
    scratch = [pltpu.VMEM((TOK, 1024), BF), pltpu.VMEM((TOK, 1024), BF)] + stage
    tokens_like = [whole((TOK, D)), whole((D, TOK))] * 2 + [whole((TOK, D), F32)] * 2
    *carried, keep, away = call(
        mlp_own_kernel,
        (mixed, cot, *cot_rows, cot_moved, second_norm_gain[None], w_fc1, w_fc2),
        tokens_like + grads,
        scratch,
        place,
        flops=4 * 10**9,
        name="mlp_own",
    )
    own = (keep, away)
    (w12,) = fence((w12,), (keep,))
    w12_sib = flip(w12, c=1)
    out_band, tail, dm, *other = call(
        mlp_other_kernel,
        (mixed, *carried, second_norm_gain[None], w12, w12_sib),
        [whole((12, 48, D)), whole((12, 6, D)), whole((TOK, D))] + grads,
        scratch,
        place,
        flops=4 * 10**9,
        name="mlp_other",
    )
    own_cut = core_phase(*own)
    own_parts = x_phase(own_cut)
    other_cut = core_phase(*other)
    other_parts = x_phase(other_cut)
    out_moved = send(tail, lon_move(1))
    dqkv, dmt = call(
        attend_back_kernel,
        (dm, prob, qkv, wo_full),
        [whole((TOK, 3 * D)), whole((D, TOK))],
        [pltpu.VMEM((TOK, D), BF)],
        flops=4 * 10**9,
        name="attend_back",
        after=(other_cut[0], out_moved),
    )
    at = call(
        attend_grads_kernel,
        (dqkv, dmt, heads, n1t),
        [whole((4, 2, 2, 8, 16, 256))] * 2,
        (),
        place,
        flops=1 * 10**9,
        name="attend_grads",
        after=own_parts[1:],
    )
    at_cut = core_phase(*at)
    at_parts = x_phase((at_cut[0], *fence(at_cut[1:], other_parts[1:])))

    out = jnp.concatenate([out_moved, out_band[:, 6:]], 1)
    near, far, above = fence((out[6:9], out[9:12], out[3:6]), (at_cut[0],))
    near, far, above = flip(near, t=1), send(far, far_back), send(above, lat_move(1))
    gq, go, g1, g2 = reduce_and_gather(place, own_parts, other_parts, at_parts, (near, far, above))
    out = jnp.where(
        t == 0,
        jnp.concatenate([far, out[0:6], near], 0),
        jnp.concatenate([above, near, far, out[0:3]], 0),
    )
    return out[None], gq, go, g1, g2


def without(kernel, start, count):
    return lambda *refs: kernel(*refs[:start], *refs[start + count :])


def solution(mesh):
    fine = Mesh(mesh.devices.reshape(4, 2, 8, 2, 2), AXES)
    lat, lon = ("x", "yl"), ("z", "c")
    return jax.shard_map(
        per_device,
        mesh=fine,
        in_specs=(
            P("tp", lat, lon, None),
            P(None, lat, lon),
            P(),
            P(),
            P(None, None, "tp"),
            P("tp", None),
            P(None, "tp"),
            P("tp", None),
            P("tp", lat, lon, None),
        ),
        out_specs=(
            P("tp", lat, lon, None),
            P(None, None, "tp"),
            P("tp", None),
            P(None, "tp"),
            P("tp", None),
        ),
        check_vma=False,
    )
```

```python
import functools

import jax
import jax.numpy as jnp
from jax import lax
from jax.experimental import pallas as pl
from jax.experimental.pallas import tpu as pltpu
from jax.sharding import Mesh
from jax.sharding import PartitionSpec as P

D = 512
FF = 2048
WLAT = 6
WLON = 12
SEATS = 144
WINS = 4
TOK = SEATS * WINS
EPS = 1e-05
GELU_C = 0.7978845608028654
BF = jnp.bfloat16
F32 = jnp.float32
AXES = ("x", "yl", "z", "c", "tp")
MIB = 1024 * 1024


def pairs_of(move):
    pairs = []
    for x in range(4):
        for yl in range(2):
            for z in range(8):
                for c in range(2):
                    for t in range(2):
                        dest = move(x, yl, z, c, t)
                        if dest is not None:
                            pairs.append((rank(x, yl, z, c, t), rank(*dest)))
    return pairs


def rank(x, yl, z, c, t):
    return ((2 * x + yl) * 16 + 2 * z + c) * 2 + t


def send(value, move):
    return lax.ppermute(value, AXES, pairs_of(move))


def flip(value, x=0, yl=0, z=0, c=0, t=0):
    return send(value, lambda a, b, d, e, f: (a ^ x, b ^ yl, d ^ z, e ^ c, f ^ t))


def shift_lat(x, yl, step):
    lat = (2 * x + yl + step) % 8
    return lat // 2, lat % 2


def shift_lon(z, c, step):
    lon = (2 * z + c + step) % 16
    return lon // 2, lon % 2


def lon_move(step):
    def move(x, yl, z, c, t):
        zz, cc = shift_lon(z, c, step)
        return x, yl, zz, cc, t

    return move


def far_move(x, yl, z, c, t):
    if t == 1:
        return x, yl, z, c, 0
    xx, yy = shift_lat(x, yl, -1)
    return xx, yy, z, c, 1


def far_back(x, yl, z, c, t):
    if t == 0:
        return x, yl, z, c, 1
    xx, yy = shift_lat(x, yl, 1)
    return xx, yy, z, c, 0


def lat_move(step):
    def move(x, yl, z, c, t):
        if t == 0:
            return None
        xx, yy = shift_lat(x, yl, step)
        return xx, yy, z, c, t

    return move


def fence(values, after):
    n = len(values)
    anywhere = pl.BlockSpec(memory_space=pl.ANY)
    return pl.pallas_call(
        lambda *refs: None,
        out_shape=tuple(jax.ShapeDtypeStruct(v.shape, v.dtype) for v in values),
        in_specs=[anywhere] * (n + len(after)),
        out_specs=tuple([anywhere] * n),
        input_output_aliases={i: i for i in range(n)},
        compiler_params=pltpu.CompilerParams(vmem_limit_bytes=MIB),
        name="fence",
    )(*values, *after)


def pieces_kernel(place, tile, near, far, below):
    t = place[4]
    for i in range(3):
        near[i] = tile[9 + i - 6 * t]
        far[i] = tile[i + 6 * t]
        below[i] = tile[i]


def band_pieces(place, tile, name):
    return call(pieces_kernel, (tile,), [whole((3, 48, D))] * 3, place=place, name=name)


def exchange_rows(pieces):
    near, far, below = pieces
    return flip(near, t=1), send(far, far_move), send(below, lat_move(-1))


def edge_kernel(place, tile, near, far, below, edge):
    t = place[4]
    for i in range(3):
        edge[i] = tile[3 + i + 6 * t, :6]
        edge[3 + i] = jnp.where(t == 0, tile[6 + i, :6].astype(F32), below[i, :6].astype(F32)).astype(BF)
        edge[6 + i] = near[i, :6]
        edge[9 + i] = far[i, :6]


def first_columns(place, tile, rows, name, after=()):
    kernel = without(edge_kernel, 5, len(after))
    (edge,) = call(kernel, (tile, *rows), [whole((12, 6, D))], place=place, name=name, after=after)
    return edge


def part_of_attend_weights(place, w_qkv, w_out):
    def kernel(place, wq, wo, out):
        out[0:3] = wq[...]
        out[3] = wo[...]

    specs = [
        ((3, 64, 256), lambda i, p: (0, p[3] * 4 + p[0], 0)),
        ((64, 256), lambda i, p: (p[0], p[3])),
    ]
    return parts_of(kernel, place, (w_qkv, w_out), (4, 64, 256), specs, "part_attend")


def part_of_mlp_weights(place, w_fc1, w_fc2):
    def kernel(place, w1, w2, out):
        out[0] = w1[...]
        out[1] = w2[...]

    specs = [
        ((128, 512), lambda i, p: (p[0], p[3])),
        ((128, 512), lambda i, p: (p[3] * 4 + p[0], 0)),
    ]
    return parts_of(kernel, place, (w_fc1, w_fc2), (2, 128, 512), specs, "part_mlp")


def join_kernel(place, *refs):
    out = refs[4]
    rows = refs[0].shape[1]
    for k in range(4):
        out[:, pl.ds(pl.multiple_of((place[0] ^ k) * rows, rows), rows), :] = refs[k][...]


def spread(part):
    return [part] + [flip(part, x=k) for k in (1, 2, 3)]


def join(place, parts, name, after=()):
    shape = parts[0].shape
    out = whole((shape[0], 4 * shape[1], shape[2]))
    (out,) = call(without(join_kernel, 5, len(after)), parts, [out], (), place, name=name, after=after)
    return out


def parts_of(kernel, place, args, shape, specs, name):
    return pl.pallas_call(
        kernel,
        out_shape=whole(shape),
        grid_spec=pltpu.PrefetchScalarGridSpec(
            num_scalar_prefetch=1,
            grid=(1,),
            in_specs=[pl.BlockSpec(block, index) for block, index in specs],
            out_specs=pl.BlockSpec(shape, lambda i, p: (0,) * len(shape)),
        ),
        compiler_params=pltpu.CompilerParams(vmem_limit_bytes=4 * MIB),
        name=name,
    )(place, *args)


def to_windows(band):
    width = band.shape[-1]
    return band.reshape(12, WINS, WLON, width).transpose(1, 0, 2, 3).reshape(TOK, width)


def load_windows(t, tile, near, far, below, moved, stage, wins):
    for row in range(12):
        if row < 3:
            value = tile[3 + row + 6 * t].astype(F32)
        elif row < 6:
            value = jnp.where(t == 0, tile[3 + row].astype(F32), below[row - 3].astype(F32))
        elif row < 9:
            value = near[row - 6].astype(F32)
        else:
            value = far[row - 9].astype(F32)
        stage[row, 0:48] = value
        stage[row, 48:54] = moved[row].astype(F32)
        for w in range(WINS):
            start = w * SEATS + row * WLON
            wins[start : start + WLON, :] = stage[row, 6 + 12 * w : 18 + 12 * w]


def store_windows(wins, stage, band, tail):
    for row in range(12):
        for w in range(WINS):
            start = w * SEATS + row * WLON
            stage[row, 6 + 12 * w : 18 + 12 * w] = wins[start : start + WLON, :]
        band[row] = stage[row, 0:48].astype(BF)
        tail[row] = stage[row, 48:54].astype(BF)


def norm(value, gain):
    centered = value - jnp.mean(value, -1, keepdims=True)
    rstd = lax.rsqrt(jnp.mean(centered * centered, -1, keepdims=True) + EPS)
    xhat = centered * rstd
    return xhat * gain, xhat, rstd


def dot(a, b):
    return lax.dot_general(a, b, (((1,), (0,)), ((), ())), preferred_element_type=F32)


def dot_nt(a, b):
    return lax.dot_general(a, b, (((1,), (1,)), ((), ())), preferred_element_type=F32)


def dot_tn(a, b):
    return lax.dot_general(a, b, (((0,), (0,)), ((), ())), preferred_element_type=F32)


def head_mask(h):
    lane = lax.broadcasted_iota(jnp.int32, (1, 128), 1)
    return (lane < 64) if h == 0 else (lane >= 64)


def attend_kernel(
    place, tile, near, far, below, moved, labc, labr, g1, wq_own, wo_own, wqo_m, wqo_s,
    n1t_ref, qkv_ref, prob_ref, heads_ref, wo_full, mixed_ref, n1_scr, stage, wins,
):
    c = place[3]
    mine = pl.ds(pl.multiple_of(c * 256, 256), 256)
    sibs = pl.ds(pl.multiple_of((1 - c) * 256, 256), 256)
    load_windows(place[4], tile, near, far, below, moved, stage, wins)
    x = wins[...]
    normed = norm(x, g1[...])[0]
    n1_scr[...] = normed.astype(BF)
    n1t_ref[...] = normed.T.astype(BF)
    n1 = n1_scr[...]
    for i in range(3):
        scale = 0.125 if i == 0 else 1.0
        own = dot(n1, wq_own[i]).astype(BF)
        other = (dot(n1_scr[:, mine], wqo_m[i]) + dot(n1_scr[:, sibs], wqo_s[i])).astype(BF)
        qkv_ref[:, i * 512 : i * 512 + 256] = own * BF(scale)
        qkv_ref[:, i * 512 + 256 : i * 512 + 512] = other * BF(scale)

    def window(w, carry):
        rows = pl.ds(pl.multiple_of(w * SEATS, 16), SEATS)
        same = labc[rows, 0:1] == labr[w, 0:1, :]
        for p in range(4):
            q2 = qkv_ref[rows, p * 128 : p * 128 + 128]
            k2 = qkv_ref[rows, 512 + p * 128 : 640 + p * 128]
            v2 = qkv_ref[rows, 1024 + p * 128 : 1152 + p * 128]
            total = None
            for h in range(2):
                keep = head_mask(h)
                scores = dot_nt(jnp.where(keep, q2, BF(0)), k2)
                scores = jnp.where(same, scores, -1e30)
                expo = jnp.exp(scores - jnp.max(scores, -1, keepdims=True))
                prob = (expo * (1.0 / jnp.sum(expo, -1, keepdims=True))).astype(BF)
                prob_ref[w * 8 + p * 2 + h] = prob
                part = dot(prob, jnp.where(keep, v2, BF(0)))
                total = part if total is None else total + part
            heads_ref[rows, p * 128 : p * 128 + 128] = total.astype(BF)
        return carry

    lax.fori_loop(0, WINS, window, 0)
    wo_full[0:256, :] = wo_own[...]
    wo_full[256:512, mine] = wqo_m[3]
    wo_full[256:512, sibs] = wqo_s[3]
    attn = dot(heads_ref[...], wo_full[...]).astype(BF).astype(F32)
    mixed_ref[...] = (x + attn).astype(BF)


def gelu_parts(v):
    square = v * v
    tanh_v = jnp.tanh(GELU_C * v * (1.0 + 0.044715 * square))
    half = 0.5 * (1.0 + tanh_v)
    slope = half + 0.5 * v * (1.0 - tanh_v * tanh_v) * (GELU_C + (3.0 * 0.044715 * GELU_C) * square)
    return v * half, slope


def store_rows(out, block, lead, cols):
    for yl in range(2):
        for z in range(8):
            rows = slice(z * 32 + yl * 16, z * 32 + yl * 16 + 16)
            out[lead + (yl, z, slice(None), cols)] = block[rows].astype(BF)


def mlp_block(w1, w2, cols, n2, cot):
    hidden, slope = gelu_parts(dot(n2, w1[:, cols]))
    return hidden.astype(BF), (dot_nt(cot, w2[cols, :]) * slope).astype(BF)


def store_grads(n2t, cott, hidden, dpre, lead, c, keep, away):
    mine = pl.ds(pl.multiple_of(c * 256, 256), 256)
    sibs = pl.ds(pl.multiple_of((1 - c) * 256, 256), 256)
    for rows, out in ((sibs, away), (mine, keep)):
        store_rows(out, dot(n2t[rows, :], dpre), lead, slice(0, 256))
        store_rows(out, dot(cott[rows, :], hidden), lead, slice(256, 512))


def mlp_own_kernel(
    place, mixed_ref, tile, near, far, below, moved, g2, w1_own, w2_own,
    n2_ref, n2t, cot_ref, cott, out_acc, norm_acc, keep, away,
    hid_scr, dpre_scr, stage, wins,
):
    mx, c = place[0], place[3]
    load_windows(place[4], tile, near, far, below, moved, stage, wins)
    mixed = mixed_ref[...].astype(F32)
    normed = norm(mixed, g2[...])[0]
    n2_ref[...] = normed.astype(BF)
    n2t[...] = normed.T.astype(BF)
    cott[...] = wins[...].T.astype(BF)
    cot_ref[...] = wins[...].astype(BF)
    n2, cot = n2_ref[...], cot_ref[...]
    for x in range(4):
        cols = slice(x * 256, x * 256 + 256)
        hidden, dpre = mlp_block(w1_own, w2_own, cols, n2, cot)
        hid_scr[:, cols] = hidden
        dpre_scr[:, cols] = dpre
        store_grads(n2t, cott, hidden, dpre, (x ^ mx,), c, keep, away)
    out_acc[...] = mixed + dot(hid_scr[...], w2_own[...])
    norm_acc[...] = dot_nt(dpre_scr[...], w1_own[...])


def mlp_other_kernel(
    place, mixed_ref, n2_ref, n2t, cot_ref, cott, out_acc, norm_acc, g2, w12_m, w12_s,
    band, tail, dm_ref, keep, away,
    hid_scr, dpre_scr, stage, wins,
):
    mx, c = place[0], place[3]
    n2, cot = n2_ref[...], cot_ref[...]
    for n, (pair, half) in enumerate(((w12_m, c), (w12_s, 1 - c))):
        for i in range(2):
            cols = slice(i * 256, i * 256 + 256)
            hidden, dpre = mlp_block(pair.at[0], pair.at[1], cols, n2, cot)
            hid_scr[:, n * 512 + i * 256 : n * 512 + i * 256 + 256] = hidden
            dpre_scr[:, n * 512 + i * 256 : n * 512 + i * 256 + 256] = dpre
            store_grads(n2t, cott, hidden, dpre, ((2 * half + i) ^ mx,), c, keep, away)
    d_norm = norm_acc[...] + (
        dot_nt(dpre_scr[:, :512], w12_m[0]) + dot_nt(dpre_scr[:, 512:], w12_s[0])
    )
    gain = g2[...]
    xhat, rstd = norm(mixed_ref[...].astype(F32), gain)[1:]
    scaled = d_norm * gain
    dm = cot.astype(F32) + rstd * (
        scaled
        - jnp.mean(scaled, -1, keepdims=True)
        - xhat * jnp.mean(scaled * xhat, -1, keepdims=True)
    )
    dm_ref[...] = dm.astype(BF)
    wins[...] = out_acc[...] + (dot(hid_scr[:, :512], w12_m[1]) + dot(hid_scr[:, 512:], w12_s[1]))
    store_windows(wins, stage, band, tail)


def attend_back_kernel(
    dm_ref, prob_ref, qkv_ref, wo_full, first, second,
    dqkv, dmt,
    dheads,
):
    dm = dm_ref[...]
    dmt[...] = dm.astype(F32).T.astype(BF)
    dheads[...] = dot_nt(dm, wo_full[...]).astype(BF)

    def window(w, carry):
        rows = pl.ds(pl.multiple_of(w * SEATS, 16), SEATS)
        for p in range(4):
            pc = slice(p * 128, p * 128 + 128)
            q2 = qkv_ref[rows, p * 128 : p * 128 + 128]
            k2 = qkv_ref[rows, 512 + p * 128 : 640 + p * 128]
            v2 = qkv_ref[rows, 1024 + p * 128 : 1152 + p * 128]
            do2 = dheads[rows, pc]
            dq = dk = dv = None
            for h in range(2):
                keep = head_mask(h)
                prob_b = prob_ref[w * 8 + p * 2 + h]
                prob = prob_b.astype(F32)
                do_h = jnp.where(keep, do2, BF(0))
                d_prob = dot_nt(do_h, v2)
                moment = jnp.sum(prob * d_prob, -1, keepdims=True)
                d_scores = (prob * (d_prob - moment)).astype(BF)
                pq = dot(d_scores, jnp.where(keep, k2, BF(0)))
                pk = dot_tn(d_scores, jnp.where(keep, q2, BF(0)))
                pv = dot_tn(prob_b, do_h)
                dq = pq if dq is None else dq + pq
                dk = pk if dk is None else dk + pk
                dv = pv if dv is None else dv + pv
            dqkv[rows, p * 128 : p * 128 + 128] = (dq * 0.125).astype(BF)
            dqkv[rows, 512 + p * 128 : 640 + p * 128] = dk.astype(BF)
            dqkv[rows, 1024 + p * 128 : 1152 + p * 128] = dv.astype(BF)
        return carry

    lax.fori_loop(0, WINS, window, 0)


def attend_grads_kernel(
    place, dqkv, dmt, heads_ref, n1t_ref, first, second, third,
    keep, away,
):
    mx, c, mt = place[0], place[3], place[4]
    mine = pl.ds(pl.multiple_of(c * 256, 256), 256)
    sibs = pl.ds(pl.multiple_of((1 - c) * 256, 256), 256)
    for rows, out in ((sibs, away), (mine, keep)):
        for t in range(2):
            for half in range(2):
                for which in range(2):
                    if which == 0 or half == 0:
                        start = (2 * which + half) * 512 + t * 256
                        grad = dot(n1t_ref[rows, :], dqkv[:, start : start + 256])
                    else:
                        grad = dot(dmt[rows, :], heads_ref[:, t * 256 : t * 256 + 256])
                    for sub in range(2):
                        lead = ((half * 2 + sub) ^ mx, t ^ mt)
                        cols = slice(which * 128, which * 128 + 128)
                        store_rows(out, grad[:, sub * 128 : sub * 128 + 128], lead, cols)


def whole(shape, dtype=BF):
    return jax.ShapeDtypeStruct(shape, dtype)


def call(kernel, args, outs, scratch=(), place=None, flops=0, name=None, after=(), limit=8):
    spec = pl.BlockSpec(memory_space=pltpu.VMEM)
    specs = [spec] * len(args) + [pl.BlockSpec(memory_space=pl.ANY)] * len(after)
    args = tuple(args) + tuple(after)
    if place is not None:
        args = (place,) + args
        specs = [pl.BlockSpec(memory_space=pltpu.SMEM)] + specs
    size = sum(a.size * a.dtype.itemsize for a in list(args) + list(outs))
    return pl.pallas_call(
        kernel,
        out_shape=tuple(outs),
        in_specs=specs,
        out_specs=tuple([spec] * len(outs)),
        scratch_shapes=list(scratch),
        compiler_params=pltpu.CompilerParams(vmem_limit_bytes=limit * MIB),
        cost_estimate=pl.CostEstimate(flops=flops, bytes_accessed=size, transcendentals=0),
        name=name,
    )(*args)


def add(*values):
    total = values[0].astype(F32)
    for value in values[1:]:
        total = total + value.astype(F32)
    return total.astype(BF)


def core_sum_kernel(keep, arrived, *outs):
    for x in range(4):
        outs[x][...] = add(keep[x], arrived[x])


def x_sum_kernel(place, *refs):
    own, other, at, out = refs[0:4], refs[4:8], refs[8:12], refs[-1]
    t = place[4]
    out[t, :, :, :, :512] = add(*[r[...] for r in own])
    out[1 - t, :, :, :, :512] = add(*[r[...] for r in other])
    out[:, :, :, :, 512:] = add(*[r[...] for r in at])


def last_sum_kernel(parts, out):
    total = parts[0].astype(F32)
    for i in range(1, 32):
        total = total + parts[i].astype(F32)
    for z in range(8):
        out[z] = total.astype(BF)


def copies_kernel(part, out):
    for i in range(8):
        out[i] = part[...]


def place_kernel(place, mine, sib, gq, go, g1, g2, scr2, scro):
    c = place[3]
    for src, cc in ((mine, c), (sib, 1 - c)):
        base = cc * 256
        for yl in range(2):
            for x in range(4):
                for z in range(8):
                    rows = pl.ds(pl.multiple_of(base + z * 32 + yl * 16, 16), 16)
                    chunk = src[2 * x + yl, z]
                    lo = (x % 2) * 128
                    g1[rows, x * 256 : x * 256 + 256] = chunk[:, :256]
                    scr2[rows, x * 256 : x * 256 + 256] = chunk[:, 256:512]
                    gq[x // 2, rows, lo : lo + 128] = chunk[:, 512:640]
                    if x < 2:
                        gq[2, rows, lo : lo + 128] = chunk[:, 640:]
                    else:
                        scro[rows, lo : lo + 128] = chunk[:, 640:]
    for i in range(4):
        g2[i * 256 : i * 256 + 256, :] = scr2[:, i * 256 : i * 256 + 256].astype(F32).T.astype(BF)
    go[...] = scro[...].astype(F32).T.astype(BF)


def core_phase(keep, away):
    outs = [whole(keep.shape[1:])] * 4
    return call(core_sum_kernel, (keep, flip(away, c=1)), outs, name="core_sum")


def x_phase(cut):
    return [cut[0]] + [flip(cut[k], x=k) for k in (1, 2, 3)]


def reduce_and_gather(place, own, other, at, after):
    (total,) = call(
        x_sum_kernel, (*own, *other, *at), [whole((2, 2, 8, 16, 768))], (), place, name="x_sum", after=after
    )
    parts = lax.all_to_all(total.reshape(32, 16, 768), ("tp", "yl", "z"), 0, 0)
    (chunks,) = call(last_sum_kernel, (parts,), [whole((8, 16, 768))], name="last_sum")
    column = lax.all_to_all(chunks, "z", 0, 0)
    (columns,) = call(copies_kernel, (column,), [whole((8, 8, 16, 768))], name="copies")
    mine = lax.all_to_all(columns, ("x", "yl"), 0, 0)
    sib = flip(mine, c=1)
    outs = [whole((3, 512, 256)), whole((256, 512)), whole((512, 1024)), whole((1024, 512))]
    scratch = [pltpu.VMEM((512, 1024), BF), pltpu.VMEM((512, 256), BF)]
    return call(place_kernel, (mine, sib), outs, scratch, place, name="place")


def per_device(tokens, labels, gain_one, second_norm_gain, w_qkv, w_out, w_fc1, w_fc2, cotangent):
    x, yl, z, c, t = [lax.axis_index(name) for name in AXES]
    place = jnp.stack([x, yl, z, c, t]).astype(jnp.int32)
    tile, cot = tokens[0], cotangent[0]

    pieces = band_pieces(place, tile, "pieces")
    rows = exchange_rows(pieces)
    (wqo,) = fence((part_of_attend_weights(place, w_qkv, w_out),), (pieces[0],))
    wqo = flip(wqo, yl=1, t=1)
    edge = first_columns(place, tile, rows, "edge")
    (wqo,) = fence((wqo,), (edge,))
    wqo = spread(wqo)
    moved = send(edge, lon_move(-1))
    cot_rows = exchange_rows(fence(band_pieces(place, cot, "cot_pieces"), (edge,)))
    wqo = join(place, wqo, "join_attend", (moved,))
    wqo_sib = flip(wqo, c=1)
    (w12,) = fence((part_of_mlp_weights(place, w_fc1, w_fc2),), (wqo,))
    w12 = spread(flip(w12, yl=1, t=1))
    cot_edge = first_columns(place, cot, cot_rows, "cot_edge", (moved,))
    cot_moved = send(cot_edge, lon_move(-1))

    band = lax.dynamic_slice_in_dim(labels, t * 6, 6, 1)
    band = jnp.where(t == 0, band, band[::-1]).reshape(12, 48, 1)
    lab = to_windows(band).reshape(TOK)
    labc = jnp.broadcast_to(lab[:, None], (TOK, 128))
    labr = jnp.broadcast_to(lab.reshape(WINS, 1, SEATS), (WINS, 8, SEATS))

    stage = [pltpu.VMEM((12, 56, D), F32), pltpu.VMEM((TOK, D), F32)]
    n1t, qkv, prob, heads, wo_full, mixed = call(
        without(attend_kernel, 13, 1),
        (tile, *rows, moved, labc, labr, gain_one[None], w_qkv, w_out, wqo, wqo_sib),
        [
            whole((D, TOK)), whole((TOK, 3 * D)), whole((WINS * 8, SEATS, SEATS)),
            whole((TOK, D)), whole((D, D)), whole((TOK, D)),
        ],
        [pltpu.VMEM((TOK, D), BF)] + stage,
        place,
        flops=3 * 10**9,
        name="attend",
        limit=20,
        after=(cot_edge,),
    )
    grads = [whole((4, 2, 8, 16, 512))] * 2
    scratch = [pltpu.VMEM((TOK, 1024), BF), pltpu.VMEM((TOK, 1024), BF)] + stage
    tokens_like = [whole((TOK, D)), whole((D, TOK))] * 2 + [whole((TOK, D), F32)] * 2
    *carried, keep, away = call(
        mlp_own_kernel,
        (mixed, cot, *cot_rows, cot_moved, second_norm_gain[None], w_fc1, w_fc2),
        tokens_like + grads,
        scratch,
        place,
        flops=4 * 10**9,
        name="mlp_own",
        limit=20,
    )
    own = (keep, away)
    w12 = join(place, fence(w12, (keep,)), "join_mlp")
    w12_sib = flip(w12, c=1)
    out_band, tail, dm, *other = call(
        mlp_other_kernel,
        (mixed, *carried, second_norm_gain[None], w12, w12_sib),
        [whole((12, 48, D)), whole((12, 6, D)), whole((TOK, D))] + grads,
        scratch,
        place,
        flops=4 * 10**9,
        name="mlp_other",
        limit=20,
    )
    own_cut = core_phase(*own)
    own_parts = x_phase(own_cut)
    other_cut = core_phase(*other)
    other_parts = x_phase(other_cut)
    out_moved = send(tail, lon_move(1))
    dqkv, dmt = call(
        attend_back_kernel,
        (dm, prob, qkv, wo_full),
        [whole((TOK, 3 * D)), whole((D, TOK))],
        [pltpu.VMEM((TOK, D), BF)],
        flops=4 * 10**9,
        name="attend_back",
        limit=20,
        after=(other_cut[0], out_moved),
    )
    at = call(
        attend_grads_kernel,
        (dqkv, dmt, heads, n1t),
        [whole((4, 2, 2, 8, 16, 256))] * 2,
        (),
        place,
        flops=1 * 10**9,
        name="attend_grads",
        limit=20,
        after=own_parts[1:],
    )
    at_cut = core_phase(*at)
    at_parts = x_phase((at_cut[0], *fence(at_cut[1:], other_parts[1:])))

    out = jnp.concatenate([out_moved, out_band[:, 6:]], 1)
    near, far, above = fence((out[6:9], out[9:12], out[3:6]), (at_cut[0],))
    near, far, above = flip(near, t=1), send(far, far_back), send(above, lat_move(1))
    gq, go, g1, g2 = reduce_and_gather(place, own_parts, other_parts, at_parts, (near, far, above))
    out = jnp.where(
        t == 0,
        jnp.concatenate([far, out[0:6], near], 0),
        jnp.concatenate([above, near, far, out[0:3]], 0),
    )
    return out[None], gq, go, g1, g2


def without(kernel, start, count):
    return lambda *refs: kernel(*refs[:start], *refs[start + count :])


def solution(mesh):
    fine = Mesh(mesh.devices.reshape(4, 2, 8, 2, 2), AXES)
    lat, lon = ("x", "yl"), ("z", "c")
    return jax.shard_map(
        per_device,
        mesh=fine,
        in_specs=(
            P("tp", lat, lon, None),
            P(None, lat, lon),
            P(),
            P(),
            P(None, None, "tp"),
            P("tp", None),
            P(None, "tp"),
            P("tp", None),
            P("tp", lat, lon, None),
        ),
        out_specs=(
            P("tp", lat, lon, None),
            P(None, None, "tp"),
            P("tp", None),
            P(None, "tp"),
            P("tp", None),
        ),
        check_vma=False,
    )
```

```python
import functools

import jax
import jax.numpy as jnp
from jax import lax
from jax.experimental import pallas as pl
from jax.experimental.pallas import tpu as pltpu
from jax.sharding import Mesh
from jax.sharding import PartitionSpec as P

D = 512
FF = 2048
WLAT = 6
WLON = 12
SEATS = 144
WINS = 4
TOK = SEATS * WINS
EPS = 1e-05
GELU_C = 0.7978845608028654
BF = jnp.bfloat16
F32 = jnp.float32
AXES = ("x", "yl", "z", "c", "tp")
MIB = 1024 * 1024


def pairs_of(move):
    pairs = []
    for x in range(4):
        for yl in range(2):
            for z in range(8):
                for c in range(2):
                    for t in range(2):
                        dest = move(x, yl, z, c, t)
                        if dest is not None:
                            pairs.append((rank(x, yl, z, c, t), rank(*dest)))
    return pairs


def rank(x, yl, z, c, t):
    return ((2 * x + yl) * 16 + 2 * z + c) * 2 + t


def send(value, move):
    return lax.ppermute(value, AXES, pairs_of(move))


def flip(value, x=0, yl=0, z=0, c=0, t=0):
    return send(value, lambda a, b, d, e, f: (a ^ x, b ^ yl, d ^ z, e ^ c, f ^ t))


def shift_lat(x, yl, step):
    lat = (2 * x + yl + step) % 8
    return lat // 2, lat % 2


def shift_lon(z, c, step):
    lon = (2 * z + c + step) % 16
    return lon // 2, lon % 2


def lon_move(step):
    def move(x, yl, z, c, t):
        zz, cc = shift_lon(z, c, step)
        return x, yl, zz, cc, t

    return move


def far_move(x, yl, z, c, t):
    if t == 1:
        return x, yl, z, c, 0
    xx, yy = shift_lat(x, yl, -1)
    return xx, yy, z, c, 1


def far_back(x, yl, z, c, t):
    if t == 0:
        return x, yl, z, c, 1
    xx, yy = shift_lat(x, yl, 1)
    return xx, yy, z, c, 0


def lat_move(step):
    def move(x, yl, z, c, t):
        if t == 0:
            return None
        xx, yy = shift_lat(x, yl, step)
        return xx, yy, z, c, t

    return move


def fence(values, after):
    n = len(values)
    anywhere = pl.BlockSpec(memory_space=pl.ANY)
    return pl.pallas_call(
        lambda *refs: None,
        out_shape=tuple(jax.ShapeDtypeStruct(v.shape, v.dtype) for v in values),
        in_specs=[anywhere] * (n + len(after)),
        out_specs=tuple([anywhere] * n),
        input_output_aliases={i: i for i in range(n)},
        compiler_params=pltpu.CompilerParams(vmem_limit_bytes=MIB),
        name="fence",
    )(*values, *after)


def pieces_kernel(place, tile, cot, near, far, below):
    t = place[4]
    for n, ref in enumerate((tile, cot)):
        for i in range(3):
            near[n, i] = ref[9 + i - 6 * t]
            far[n, i] = ref[i + 6 * t]
            below[n, i] = ref[i]


def edge_kernel(place, tile, cot, near, far, below, edge):
    t = place[4]
    for n, ref in enumerate((tile, cot)):
        for i in range(3):
            edge[n, i] = ref[3 + i + 6 * t, :6]
            row = jnp.where(t == 0, ref[6 + i, :6].astype(F32), below[n, i, :6].astype(F32))
            edge[n, 3 + i] = row.astype(BF)
            edge[n, 6 + i] = near[n, i, :6]
            edge[n, 9 + i] = far[n, i, :6]


def weight_parts(place, w_qkv, w_out, w_fc1, w_fc2):
    def kernel(place, wq, wo, w1, w2, attend, mlp):
        attend[0:3] = wq[...]
        attend[3] = wo[...]
        mlp[0] = w1[...]
        mlp[1, :, :512] = w2[:32]
        mlp[1, :, 512:] = w2[32:]

    specs = [
        ((3, 64, 256), lambda i, p: (0, p[3] * 4 + p[0], 0)),
        ((64, 256), lambda i, p: (p[0], p[3])),
        ((32, 1024), lambda i, p: (p[2] * 2 + p[3], 0)),
        ((64, 512), lambda i, p: (p[2] * 2 + p[3], 0)),
    ]
    shapes = ((4, 64, 256), (2, 32, 1024))
    return pl.pallas_call(
        kernel,
        out_shape=tuple(whole(shape) for shape in shapes),
        grid_spec=pltpu.PrefetchScalarGridSpec(
            num_scalar_prefetch=1,
            grid=(1,),
            in_specs=[pl.BlockSpec(block, index) for block, index in specs],
            out_specs=tuple(pl.BlockSpec(shape, lambda i, p: (0, 0, 0)) for shape in shapes),
        ),
        compiler_params=pltpu.CompilerParams(vmem_limit_bytes=4 * MIB),
        name="weight_parts",
    )(place, w_qkv, w_out, w_fc1, w_fc2)


def join_kernel(place, *refs):
    out = refs[4]
    rows = refs[0].shape[1]
    for k in range(4):
        out[:, pl.ds(pl.multiple_of((place[0] ^ k) * rows, rows), rows), :] = refs[k][...]


def to_windows(band):
    width = band.shape[-1]
    return band.reshape(12, WINS, WLON, width).transpose(1, 0, 2, 3).reshape(TOK, width)


def load_windows(t, n, tile, near, far, below, moved, stage, wins):
    for row in range(12):
        if row < 3:
            value = tile[3 + row + 6 * t].astype(F32)
        elif row < 6:
            value = jnp.where(t == 0, tile[3 + row].astype(F32), below[n, row - 3].astype(F32))
        elif row < 9:
            value = near[n, row - 6].astype(F32)
        else:
            value = far[n, row - 9].astype(F32)
        stage[row, 0:48] = value
        stage[row, 48:54] = moved[n, row].astype(F32)
        for w in range(WINS):
            start = w * SEATS + row * WLON
            wins[start : start + WLON, :] = stage[row, 6 + 12 * w : 18 + 12 * w]


def store_windows(wins, stage, band, tail):
    for row in range(12):
        for w in range(WINS):
            start = w * SEATS + row * WLON
            stage[row, 6 + 12 * w : 18 + 12 * w] = wins[start : start + WLON, :]
        band[row] = stage[row, 0:48].astype(BF)
        tail[row] = stage[row, 48:54].astype(BF)


def norm(value, gain):
    centered = value - jnp.mean(value, -1, keepdims=True)
    rstd = lax.rsqrt(jnp.mean(centered * centered, -1, keepdims=True) + EPS)
    xhat = centered * rstd
    return xhat * gain, xhat, rstd


def dot(a, b):
    return lax.dot_general(a, b, (((1,), (0,)), ((), ())), preferred_element_type=F32)


def dot_nt(a, b):
    return lax.dot_general(a, b, (((1,), (1,)), ((), ())), preferred_element_type=F32)


def dot_tn(a, b):
    return lax.dot_general(a, b, (((0,), (0,)), ((), ())), preferred_element_type=F32)


def head_mask(h):
    lane = lax.broadcasted_iota(jnp.int32, (1, 128), 1)
    return (lane < 64) if h == 0 else (lane >= 64)


def attend_kernel(
    place, tile, near, far, below, moved, labc, labr, g1, wq_own, wo_own, wqo_m, wqo_s,
    n1t_ref, qkv_ref, prob_ref, heads_ref, wo_full, mixed_ref, n1_scr, stage, wins,
):
    c = place[3]
    mine = pl.ds(pl.multiple_of(c * 256, 256), 256)
    sibs = pl.ds(pl.multiple_of((1 - c) * 256, 256), 256)
    load_windows(place[4], 0, tile, near, far, below, moved, stage, wins)
    x = wins[...]
    normed = norm(x, g1[...])[0]
    n1_scr[...] = normed.astype(BF)
    n1t_ref[...] = normed.T.astype(BF)
    n1 = n1_scr[...]
    for i in range(3):
        scale = 0.125 if i == 0 else 1.0
        own = dot(n1, wq_own[i]).astype(BF)
        other = (dot(n1_scr[:, mine], wqo_m[i]) + dot(n1_scr[:, sibs], wqo_s[i])).astype(BF)
        qkv_ref[:, i * 512 : i * 512 + 256] = own * BF(scale)
        qkv_ref[:, i * 512 + 256 : i * 512 + 512] = other * BF(scale)

    def window(w, carry):
        rows = pl.ds(pl.multiple_of(w * SEATS, 16), SEATS)
        same = labc[rows, 0:1] == labr[w, 0:1, :]
        for p in range(4):
            q2 = qkv_ref[rows, p * 128 : p * 128 + 128]
            k2 = qkv_ref[rows, 512 + p * 128 : 640 + p * 128]
            v2 = qkv_ref[rows, 1024 + p * 128 : 1152 + p * 128]
            total = None
            for h in range(2):
                keep = head_mask(h)
                scores = dot_nt(jnp.where(keep, q2, BF(0)), k2)
                scores = jnp.where(same, scores, -1e30)
                expo = jnp.exp(scores - jnp.max(scores, -1, keepdims=True))
                prob = (expo * (1.0 / jnp.sum(expo, -1, keepdims=True))).astype(BF)
                prob_ref[w * 8 + p * 2 + h] = prob
                part = dot(prob, jnp.where(keep, v2, BF(0)))
                total = part if total is None else total + part
            heads_ref[rows, p * 128 : p * 128 + 128] = total.astype(BF)
        return carry

    lax.fori_loop(0, WINS, window, 0)
    wo_full[0:256, :] = wo_own[...]
    wo_full[256:512, mine] = wqo_m[3]
    wo_full[256:512, sibs] = wqo_s[3]
    attn = dot(heads_ref[...], wo_full[...]).astype(BF).astype(F32)
    mixed_ref[...] = (x + attn).astype(BF)


def gelu_parts(v):
    square = v * v
    tanh_v = jnp.tanh(GELU_C * v * (1.0 + 0.044715 * square))
    half = 0.5 * (1.0 + tanh_v)
    slope = half + 0.5 * v * (1.0 - tanh_v * tanh_v) * (GELU_C + (3.0 * 0.044715 * GELU_C) * square)
    return v * half, slope


def store_rows(out, block, lead, cols):
    for yl in range(2):
        for z in range(8):
            rows = slice(z * 32 + yl * 16, z * 32 + yl * 16 + 16)
            out[lead + (yl, z, slice(None), cols)] = block[rows].astype(BF)


def mlp_block(w1, w2, cols, n2, cot):
    hidden, slope = gelu_parts(dot(n2, w1[:, cols]))
    return hidden.astype(BF), (dot_nt(cot, w2[cols, :]) * slope).astype(BF)


def store_grads(n2t, cott, hidden, dpre, lead, c, keep, away):
    mine = pl.ds(pl.multiple_of(c * 256, 256), 256)
    sibs = pl.ds(pl.multiple_of((1 - c) * 256, 256), 256)
    for rows, out in ((sibs, away), (mine, keep)):
        store_rows(out, dot(n2t[rows, :], dpre), lead, slice(0, 256))
        store_rows(out, dot(cott[rows, :], hidden), lead, slice(256, 512))


def mlp_own_kernel(
    place, mixed_ref, tile, near, far, below, moved, g2, w1_own, w2_own,
    n2_ref, n2t, cot_ref, cott, out_acc, norm_acc, keep, away,
    hid_scr, dpre_scr, stage, wins,
):
    mx, c = place[0], place[3]
    load_windows(place[4], 1, tile, near, far, below, moved, stage, wins)
    mixed = mixed_ref[...].astype(F32)
    normed = norm(mixed, g2[...])[0]
    n2_ref[...] = normed.astype(BF)
    n2t[...] = normed.T.astype(BF)
    cott[...] = wins[...].T.astype(BF)
    cot_ref[...] = wins[...].astype(BF)
    n2, cot = n2_ref[...], cot_ref[...]
    for x in range(4):
        cols = slice(x * 256, x * 256 + 256)
        hidden, dpre = mlp_block(w1_own, w2_own, cols, n2, cot)
        hid_scr[:, cols] = hidden
        dpre_scr[:, cols] = dpre
        store_grads(n2t, cott, hidden, dpre, (x ^ mx,), c, keep, away)
    out_acc[...] = mixed + dot(hid_scr[...], w2_own[...])
    norm_acc[...] = dot_nt(dpre_scr[...], w1_own[...])


def mlp_other_kernel(
    place, mixed_ref, n2_ref, n2t, cot_ref, cott, out_acc, norm_acc, g2, gathered,
    band, tail, dm_ref, keep, away,
    hid_scr, dpre_scr, stage, wins, w1, w2,
):
    mx, c = place[0], place[3]
    n2, cot = n2_ref[...], cot_ref[...]
    for p in range(16):
        w1[32 * p : 32 * p + 32, :] = gathered[p, 0]
        w2[64 * p : 64 * p + 32, :] = gathered[p, 1, :, :512]
        w2[64 * p + 32 : 64 * p + 64, :] = gathered[p, 1, :, 512:]
    for x in range(4):
        cols = slice(x * 256, x * 256 + 256)
        hidden, dpre = mlp_block(w1, w2, cols, n2, cot)
        hid_scr[:, cols] = hidden
        dpre_scr[:, cols] = dpre
        store_grads(n2t, cott, hidden, dpre, (x ^ mx,), c, keep, away)
    d_norm = norm_acc[...] + dot_nt(dpre_scr[...], w1[...])
    gain = g2[...]
    xhat, rstd = norm(mixed_ref[...].astype(F32), gain)[1:]
    scaled = d_norm * gain
    dm = cot.astype(F32) + rstd * (
        scaled
        - jnp.mean(scaled, -1, keepdims=True)
        - xhat * jnp.mean(scaled * xhat, -1, keepdims=True)
    )
    dm_ref[...] = dm.astype(BF)
    wins[...] = out_acc[...] + dot(hid_scr[...], w2[...])
    store_windows(wins, stage, band, tail)


def attend_back_kernel(
    dm_ref, prob_ref, qkv_ref, wo_full, first, second,
    dqkv, dmt,
    dheads,
):
    dm = dm_ref[...]
    dmt[...] = dm.astype(F32).T.astype(BF)
    dheads[...] = dot_nt(dm, wo_full[...]).astype(BF)

    def window(w, carry):
        rows = pl.ds(pl.multiple_of(w * SEATS, 16), SEATS)
        for p in range(4):
            pc = slice(p * 128, p * 128 + 128)
            q2 = qkv_ref[rows, p * 128 : p * 128 + 128]
            k2 = qkv_ref[rows, 512 + p * 128 : 640 + p * 128]
            v2 = qkv_ref[rows, 1024 + p * 128 : 1152 + p * 128]
            do2 = dheads[rows, pc]
            dq = dk = dv = None
            for h in range(2):
                keep = head_mask(h)
                prob_b = prob_ref[w * 8 + p * 2 + h]
                prob = prob_b.astype(F32)
                do_h = jnp.where(keep, do2, BF(0))
                d_prob = dot_nt(do_h, v2)
                moment = jnp.sum(prob * d_prob, -1, keepdims=True)
                d_scores = (prob * (d_prob - moment)).astype(BF)
                pq = dot(d_scores, jnp.where(keep, k2, BF(0)))
                pk = dot_tn(d_scores, jnp.where(keep, q2, BF(0)))
                pv = dot_tn(prob_b, do_h)
                dq = pq if dq is None else dq + pq
                dk = pk if dk is None else dk + pk
                dv = pv if dv is None else dv + pv
            dqkv[rows, p * 128 : p * 128 + 128] = (dq * 0.125).astype(BF)
            dqkv[rows, 512 + p * 128 : 640 + p * 128] = dk.astype(BF)
            dqkv[rows, 1024 + p * 128 : 1152 + p * 128] = dv.astype(BF)
        return carry

    lax.fori_loop(0, WINS, window, 0)


def attend_grads_kernel(
    place, dqkv, dmt, heads_ref, n1t_ref, first, second, third, fourth, fifth,
    keep, away,
):
    mx, c, mt = place[0], place[3], place[4]
    mine = pl.ds(pl.multiple_of(c * 256, 256), 256)
    sibs = pl.ds(pl.multiple_of((1 - c) * 256, 256), 256)
    for rows, out in ((sibs, away), (mine, keep)):
        for t in range(2):
            for half in range(2):
                for which in range(2):
                    if which == 0 or half == 0:
                        start = (2 * which + half) * 512 + t * 256
                        grad = dot(n1t_ref[rows, :], dqkv[:, start : start + 256])
                    else:
                        grad = dot(dmt[rows, :], heads_ref[:, t * 256 : t * 256 + 256])
                    for sub in range(2):
                        lead = ((half * 2 + sub) ^ mx, t ^ mt)
                        cols = slice(which * 128, which * 128 + 128)
                        store_rows(out, grad[:, sub * 128 : sub * 128 + 128], lead, cols)


def whole(shape, dtype=BF):
    return jax.ShapeDtypeStruct(shape, dtype)


def call(kernel, args, outs, scratch=(), place=None, flops=0, name=None, after=(), limit=8):
    spec = pl.BlockSpec(memory_space=pltpu.VMEM)
    specs = [spec] * len(args) + [pl.BlockSpec(memory_space=pl.ANY)] * len(after)
    args = tuple(args) + tuple(after)
    if place is not None:
        args = (place,) + args
        specs = [pl.BlockSpec(memory_space=pltpu.SMEM)] + specs
    size = sum(a.size * a.dtype.itemsize for a in list(args) + list(outs))
    return pl.pallas_call(
        kernel,
        out_shape=tuple(outs),
        in_specs=specs,
        out_specs=tuple([spec] * len(outs)),
        scratch_shapes=list(scratch),
        compiler_params=pltpu.CompilerParams(vmem_limit_bytes=limit * MIB),
        cost_estimate=pl.CostEstimate(flops=flops, bytes_accessed=size, transcendentals=0),
        name=name,
    )(*args)


def add(*values):
    total = values[0].astype(F32)
    for value in values[1:]:
        total = total + value.astype(F32)
    return total.astype(BF)


def core_sum_kernel(keep, arrived, *outs):
    for x in range(4):
        outs[x][...] = add(keep[x], arrived[x])


def core_sum_two_kernel(keep, arrived, keep_two, arrived_two, *outs):
    for x in range(4):
        outs[x][0] = add(keep[x], arrived[x])
        outs[x][1] = add(keep_two[x], arrived_two[x])


def x_sum_kernel(place, *refs):
    fc, at, out = refs[0:4], refs[4:8], refs[-1]
    t = place[4]
    out[t, :, :, :, :512] = add(*[r[0] for r in fc])
    out[1 - t, :, :, :, :512] = add(*[r[1] for r in fc])
    out[:, :, :, :, 512:] = add(*[r[...] for r in at])


def last_sum_kernel(parts, out):
    total = parts[0].astype(F32)
    for i in range(1, 32):
        total = total + parts[i].astype(F32)
    for z in range(8):
        out[z] = total.astype(BF)


def copies_kernel(part, out):
    for i in range(8):
        out[i] = part[...]


def place_kernel(place, mine, sib, gq, go, g1, g2, scr2, scro):
    c = place[3]
    for src, cc in ((mine, c), (sib, 1 - c)):
        base = cc * 256
        for yl in range(2):
            for x in range(4):
                for z in range(8):
                    rows = pl.ds(pl.multiple_of(base + z * 32 + yl * 16, 16), 16)
                    chunk = src[2 * x + yl, z]
                    lo = (x % 2) * 128
                    g1[rows, x * 256 : x * 256 + 256] = chunk[:, :256]
                    scr2[rows, x * 256 : x * 256 + 256] = chunk[:, 256:512]
                    gq[x // 2, rows, lo : lo + 128] = chunk[:, 512:640]
                    if x < 2:
                        gq[2, rows, lo : lo + 128] = chunk[:, 640:]
                    else:
                        scro[rows, lo : lo + 128] = chunk[:, 640:]
    for i in range(4):
        g2[i * 256 : i * 256 + 256, :] = scr2[:, i * 256 : i * 256 + 256].astype(F32).T.astype(BF)
    go[...] = scro[...].astype(F32).T.astype(BF)


def core_phase(keep, away, after):
    outs = [whole(keep.shape[1:])] * 4
    kernel = without(core_sum_kernel, 2, len(after))
    return call(kernel, (keep, flip(away, c=1)), outs, name="core_sum", after=after)


def core_phase_two(keep, arrived, keep_two, arrived_two):
    outs = [whole((2,) + keep.shape[1:])] * 4
    return call(core_sum_two_kernel, (keep, arrived, keep_two, arrived_two), outs, name="core_sum_two")


def x_phase(cut):
    return [cut[0]] + [flip(cut[k], x=k) for k in (1, 2, 3)]


def reduce_and_gather(place, fc, at, after):
    (total,) = call(
        x_sum_kernel, (*fc, *at), [whole((2, 2, 8, 16, 768))], (), place, name="x_sum", after=after
    )
    parts = lax.all_to_all(total.reshape(32, 16, 768), ("tp", "yl", "z"), 0, 0)
    (chunks,) = call(last_sum_kernel, (parts,), [whole((8, 16, 768))], name="last_sum")
    column = lax.all_to_all(chunks, "z", 0, 0)
    (columns,) = call(copies_kernel, (column,), [whole((8, 8, 16, 768))], name="copies")
    mine = lax.all_to_all(columns, ("x", "yl"), 0, 0)
    sib = flip(mine, c=1)
    outs = [whole((3, 512, 256)), whole((256, 512)), whole((512, 1024)), whole((1024, 512))]
    scratch = [pltpu.VMEM((512, 1024), BF), pltpu.VMEM((512, 256), BF)]
    return call(place_kernel, (mine, sib), outs, scratch, place, name="place")


def per_device(tokens, labels, gain_one, second_norm_gain, w_qkv, w_out, w_fc1, w_fc2, cotangent):
    x, yl, z, c, t = [lax.axis_index(name) for name in AXES]
    place = jnp.stack([x, yl, z, c, t]).astype(jnp.int32)
    tile, cot = tokens[0], cotangent[0]

    part_attend, part_mlp = weight_parts(place, w_qkv, w_out, w_fc1, w_fc2)
    wqo = flip(part_attend, yl=1, t=1)
    pieces = call(pieces_kernel, (tile, cot), [whole((2, 3, 48, D))] * 3, (), place, name="pieces")
    rows = (flip(pieces[0], t=1), send(pieces[1], far_move), send(pieces[2], lat_move(-1)))
    (edge,) = call(edge_kernel, (tile, cot, *rows), [whole((2, 12, 6, D))], (), place, name="edge")
    moved = send(edge, lon_move(-1))
    wqo, w12 = fence((wqo, flip(part_mlp, yl=1, t=1)), (edge,))
    w12 = lax.all_gather(w12, ("z", "c"), axis=0)
    (wqo,) = call(
        without(join_kernel, 5, 1),
        [wqo] + [flip(wqo, x=k) for k in (1, 2, 3)],
        [whole((4, 256, 256))],
        (),
        place,
        name="join",
        after=(moved,),
    )
    wqo_sib = flip(wqo, c=1)

    band = lax.dynamic_slice_in_dim(labels, t * 6, 6, 1)
    band = jnp.where(t == 0, band, band[::-1]).reshape(12, 48, 1)
    lab = to_windows(band).reshape(TOK)
    labc = jnp.broadcast_to(lab[:, None], (TOK, 128))
    labr = jnp.broadcast_to(lab.reshape(WINS, 1, SEATS), (WINS, 8, SEATS))

    stage = [pltpu.VMEM((12, 56, D), F32), pltpu.VMEM((TOK, D), F32)]
    n1t, qkv, prob, heads, wo_full, mixed = call(
        attend_kernel,
        (tile, *rows, moved, labc, labr, gain_one[None], w_qkv, w_out, wqo, wqo_sib),
        [
            whole((D, TOK)), whole((TOK, 3 * D)), whole((WINS * 8, SEATS, SEATS)),
            whole((TOK, D)), whole((D, D)), whole((TOK, D)),
        ],
        [pltpu.VMEM((TOK, D), BF)] + stage,
        place,
        flops=3 * 10**9,
        name="attend",
        limit=12,
    )
    grads = [whole((4, 2, 8, 16, 512))] * 2
    scratch = [pltpu.VMEM((TOK, 1024), BF), pltpu.VMEM((TOK, 1024), BF)] + stage
    tokens_like = [whole((TOK, D)), whole((D, TOK))] * 2 + [whole((TOK, D), F32)] * 2
    *carried, keep, away = call(
        mlp_own_kernel,
        (mixed, cot, *rows, moved, second_norm_gain[None], w_fc1, w_fc2),
        tokens_like + grads,
        scratch,
        place,
        flops=4 * 10**9,
        name="mlp_own",
        limit=12,
    )
    arrived = flip(away, c=1)
    out_band, tail, dm, keep_two, away_two = call(
        mlp_other_kernel,
        (mixed, *carried, second_norm_gain[None], w12),
        [whole((12, 48, D)), whole((12, 6, D)), whole((TOK, D))] + grads,
        scratch + [pltpu.VMEM((D, 1024), BF), pltpu.VMEM((1024, D), BF)],
        place,
        flops=4 * 10**9,
        name="mlp_other",
        limit=12,
    )
    fc_cut = core_phase_two(keep, arrived, keep_two, flip(away_two, c=1))
    fc_parts = x_phase(fc_cut)
    out_moved = send(tail, lon_move(1))
    out = jnp.concatenate([out_moved, out_band[:, 6:]], 1)
    near, far, above = flip(out[6:9], t=1), send(out[9:12], far_back), send(out[3:6], lat_move(1))
    dqkv, dmt = call(
        attend_back_kernel,
        (dm, prob, qkv, wo_full),
        [whole((TOK, 3 * D)), whole((D, TOK))],
        [pltpu.VMEM((TOK, D), BF)],
        flops=4 * 10**9,
        name="attend_back",
        limit=12,
        after=(fc_cut[0], out_moved),
    )
    at = call(
        attend_grads_kernel,
        (dqkv, dmt, heads, n1t),
        [whole((4, 2, 2, 8, 16, 256))] * 2,
        (),
        place,
        flops=1 * 10**9,
        name="attend_grads",
        limit=12,
        after=(fc_parts[1], fc_parts[3], near, far, above),
    )
    at_cut = core_phase(*at, ())
    at_parts = x_phase(at_cut)
    gq, go, g1, g2 = reduce_and_gather(place, fc_parts, at_parts, (above,))
    out = jnp.where(
        t == 0,
        jnp.concatenate([far, out[0:6], near], 0),
        jnp.concatenate([above, near, far, out[0:3]], 0),
    )
    return out[None], gq, go, g1, g2


def without(kernel, start, count):
    return lambda *refs: kernel(*refs[:start], *refs[start + count :])


def solution(mesh):
    fine = Mesh(mesh.devices.reshape(4, 2, 8, 2, 2), AXES)
    lat, lon = ("x", "yl"), ("z", "c")
    return jax.shard_map(
        per_device,
        mesh=fine,
        in_specs=(
            P("tp", lat, lon, None),
            P(None, lat, lon),
            P(),
            P(),
            P(None, None, "tp"),
            P("tp", None),
            P(None, "tp"),
            P("tp", None),
            P("tp", lat, lon, None),
        ),
        out_specs=(
            P("tp", lat, lon, None),
            P(None, None, "tp"),
            P("tp", None),
            P(None, "tp"),
            P("tp", None),
        ),
        check_vma=False,
    )
```

```python
import functools

import jax
import jax.numpy as jnp
from jax import lax
from jax.experimental import pallas as pl
from jax.experimental.pallas import tpu as pltpu
from jax.sharding import Mesh
from jax.sharding import PartitionSpec as P

D = 512
FF = 2048
WLAT = 6
WLON = 12
SEATS = 144
WINS = 4
TOK = SEATS * WINS
EPS = 1e-05
GELU_C = 0.7978845608028654
BF = jnp.bfloat16
F32 = jnp.float32
AXES = ("x", "yl", "z", "c", "tp")
MIB = 1024 * 1024


def pairs_of(move):
    pairs = []
    for x in range(4):
        for yl in range(2):
            for z in range(8):
                for c in range(2):
                    for t in range(2):
                        dest = move(x, yl, z, c, t)
                        if dest is not None:
                            pairs.append((rank(x, yl, z, c, t), rank(*dest)))
    return pairs


def rank(x, yl, z, c, t):
    return ((2 * x + yl) * 16 + 2 * z + c) * 2 + t


def send(value, move):
    return lax.ppermute(value, AXES, pairs_of(move))


def flip(value, x=0, yl=0, z=0, c=0, t=0):
    return send(value, lambda a, b, d, e, f: (a ^ x, b ^ yl, d ^ z, e ^ c, f ^ t))


def shift_lat(x, yl, step):
    lat = (2 * x + yl + step) % 8
    return lat // 2, lat % 2


def shift_lon(z, c, step):
    lon = (2 * z + c + step) % 16
    return lon // 2, lon % 2


def lon_move(step):
    def move(x, yl, z, c, t):
        zz, cc = shift_lon(z, c, step)
        return x, yl, zz, cc, t

    return move


def far_move(x, yl, z, c, t):
    if t == 1:
        return x, yl, z, c, 0
    xx, yy = shift_lat(x, yl, -1)
    return xx, yy, z, c, 1


def far_back(x, yl, z, c, t):
    if t == 0:
        return x, yl, z, c, 1
    xx, yy = shift_lat(x, yl, 1)
    return xx, yy, z, c, 0


def lat_move(step):
    def move(x, yl, z, c, t):
        if t == 0:
            return None
        xx, yy = shift_lat(x, yl, step)
        return xx, yy, z, c, t

    return move


def fence(values, after):
    n = len(values)
    spec = pl.BlockSpec(memory_space=pltpu.VMEM)
    return pl.pallas_call(
        lambda *refs: None,
        out_shape=tuple(jax.ShapeDtypeStruct(v.shape, v.dtype) for v in values),
        in_specs=[spec] * (n + len(after)),
        out_specs=tuple([spec] * n),
        input_output_aliases={i: i for i in range(n)},
        compiler_params=pltpu.CompilerParams(vmem_limit_bytes=MIB),
        name="fence",
    )(*values, *after)


def cut_kernel(place, tile, cot, wq, wo, w1, w2, near, far, below, attend, mlp, sems):
    x, c, t = place[0], place[3], place[4]
    eighth = c * 4 + x
    copies = []
    for n, ref in enumerate((tile, cot)):
        copies.append((ref.at[pl.ds(9 - 6 * t, 3)], near.at[n]))
        copies.append((ref.at[pl.ds(6 * t, 3)], far.at[n]))
        copies.append((ref.at[pl.ds(0, 3)], below.at[n]))
    copies.append((wq.at[:, pl.ds(pl.multiple_of(eighth * 64, 64), 64)], attend.at[pl.ds(0, 3)]))
    copies.append(
        (
            wo.at[pl.ds(pl.multiple_of(x * 64, 64), 64), pl.ds(pl.multiple_of(c * 256, 256), 256)],
            attend.at[3],
        )
    )
    copies.append(
        (
            w1.at[pl.ds(pl.multiple_of(x * 128, 128), 128), pl.ds(pl.multiple_of(c * 512, 512), 512)],
            mlp.at[0],
        )
    )
    copies.append((w2.at[pl.ds(pl.multiple_of(eighth * 128, 128), 128)], mlp.at[1]))
    copies = [pltpu.make_async_copy(a, b, sems.at[i]) for i, (a, b) in enumerate(copies)]
    for copy in copies:
        copy.start()
    for copy in copies:
        copy.wait()


def cut_parts(place, *arrays):
    shapes = [(2, 3, 48, D)] * 3 + [(4, 64, 256), (2, 128, 512)]
    hbm = pl.BlockSpec(memory_space=pltpu.HBM)
    return pl.pallas_call(
        cut_kernel,
        out_shape=tuple(whole(shape) for shape in shapes),
        in_specs=[pl.BlockSpec(memory_space=pltpu.SMEM)] + [hbm] * len(arrays),
        out_specs=tuple([pl.BlockSpec(memory_space=pltpu.VMEM)] * len(shapes)),
        scratch_shapes=[pltpu.SemaphoreType.DMA((10,))],
        compiler_params=pltpu.CompilerParams(vmem_limit_bytes=MIB),
        name="cut",
    )(place, *arrays)


def edge_kernel(place, tile, cot, near, far, below, edge):
    t = place[4]
    for n, ref in enumerate((tile, cot)):
        for i in range(3):
            edge[n, i] = ref[3 + i + 6 * t, :6]
            row = jnp.where(t == 0, ref[6 + i, :6].astype(F32), below[n, i, :6].astype(F32))
            edge[n, 3 + i] = row.astype(BF)
            edge[n, 6 + i] = near[n, i, :6]
            edge[n, 9 + i] = far[n, i, :6]


def join_kernel(place, *refs):
    out = refs[4]
    rows = refs[0].shape[1]
    for k in range(4):
        out[:, pl.ds(pl.multiple_of((place[0] ^ k) * rows, rows), rows), :] = refs[k][...]


def join(place, part, name, after=()):
    depth, rows, width = part.shape
    parts = [part] + [flip(part, x=k) for k in (1, 2, 3)]
    out = whole((depth, 4 * rows, width))
    (out,) = call(without(join_kernel, 5, len(after)), parts, [out], (), place, name=name, after=after)
    return out


def to_windows(band):
    width = band.shape[-1]
    return band.reshape(12, WINS, WLON, width).transpose(1, 0, 2, 3).reshape(TOK, width)


def load_windows(t, n, tile, near, far, below, moved, stage, wins):
    for row in range(12):
        if row < 3:
            value = tile[3 + row + 6 * t].astype(F32)
        elif row < 6:
            value = jnp.where(t == 0, tile[3 + row].astype(F32), below[n, row - 3].astype(F32))
        elif row < 9:
            value = near[n, row - 6].astype(F32)
        else:
            value = far[n, row - 9].astype(F32)
        stage[row, 0:48] = value
        stage[row, 48:54] = moved[n, row].astype(F32)
        for w in range(WINS):
            start = w * SEATS + row * WLON
            wins[start : start + WLON, :] = stage[row, 6 + 12 * w : 18 + 12 * w]


def store_windows(wins, stage, band, tail):
    for row in range(12):
        for w in range(WINS):
            start = w * SEATS + row * WLON
            stage[row, 6 + 12 * w : 18 + 12 * w] = wins[start : start + WLON, :]
        band[row] = stage[row, 0:48].astype(BF)
        tail[row] = stage[row, 48:54].astype(BF)


def norm(value, gain):
    centered = value - jnp.mean(value, -1, keepdims=True)
    rstd = lax.rsqrt(jnp.mean(centered * centered, -1, keepdims=True) + EPS)
    xhat = centered * rstd
    return xhat * gain, xhat, rstd


def dot(a, b):
    return lax.dot_general(a, b, (((1,), (0,)), ((), ())), preferred_element_type=F32)


def dot_nt(a, b):
    return lax.dot_general(a, b, (((1,), (1,)), ((), ())), preferred_element_type=F32)


def dot_tn(a, b):
    return lax.dot_general(a, b, (((0,), (0,)), ((), ())), preferred_element_type=F32)


def head_mask(h):
    lane = lax.broadcasted_iota(jnp.int32, (1, 128), 1)
    return (lane < 64) if h == 0 else (lane >= 64)


def attend_kernel(
    place, tile, near, far, below, moved, labc, labr, g1, wq_own, wo_own, wqo_m, wqo_s,
    n1t_ref, qkv_ref, prob_ref, heads_ref, wo_full, mixed_ref, n1_scr, stage, wins,
):
    c = place[3]
    mine = pl.ds(pl.multiple_of(c * 256, 256), 256)
    sibs = pl.ds(pl.multiple_of((1 - c) * 256, 256), 256)
    load_windows(place[4], 0, tile, near, far, below, moved, stage, wins)
    x = wins[...]
    normed = norm(x, g1[...])[0]
    n1_scr[...] = normed.astype(BF)
    n1t_ref[...] = normed.T.astype(BF)
    n1 = n1_scr[...]
    for i in range(3):
        scale = 0.125 if i == 0 else 1.0
        own = dot(n1, wq_own[i]).astype(BF)
        other = (dot(n1_scr[:, mine], wqo_m[i]) + dot(n1_scr[:, sibs], wqo_s[i])).astype(BF)
        qkv_ref[:, i * 512 : i * 512 + 256] = own * BF(scale)
        qkv_ref[:, i * 512 + 256 : i * 512 + 512] = other * BF(scale)

    def window(w, carry):
        rows = pl.ds(pl.multiple_of(w * SEATS, 16), SEATS)
        same = labc[rows, 0:1] == labr[w, 0:1, :]
        for p in range(4):
            q2 = qkv_ref[rows, p * 128 : p * 128 + 128]
            k2 = qkv_ref[rows, 512 + p * 128 : 640 + p * 128]
            v2 = qkv_ref[rows, 1024 + p * 128 : 1152 + p * 128]
            total = None
            for h in range(2):
                keep = head_mask(h)
                scores = dot_nt(jnp.where(keep, q2, BF(0)), k2)
                scores = jnp.where(same, scores, -1e30)
                expo = jnp.exp(scores - jnp.max(scores, -1, keepdims=True))
                prob = (expo * (1.0 / jnp.sum(expo, -1, keepdims=True))).astype(BF)
                prob_ref[w * 8 + p * 2 + h] = prob
                part = dot(prob, jnp.where(keep, v2, BF(0)))
                total = part if total is None else total + part
            heads_ref[rows, p * 128 : p * 128 + 128] = total.astype(BF)
        return carry

    lax.fori_loop(0, WINS, window, 0)
    wo_full[0:256, :] = wo_own[...]
    wo_full[256:512, mine] = wqo_m[3]
    wo_full[256:512, sibs] = wqo_s[3]
    attn = dot(heads_ref[...], wo_full[...]).astype(BF).astype(F32)
    mixed_ref[...] = (x + attn).astype(BF)


def gelu_parts(v):
    square = v * v
    tanh_v = jnp.tanh(GELU_C * v * (1.0 + 0.044715 * square))
    half = 0.5 * (1.0 + tanh_v)
    slope = half + 0.5 * v * (1.0 - tanh_v * tanh_v) * (GELU_C + (3.0 * 0.044715 * GELU_C) * square)
    return v * half, slope


def store_rows(out, block, lead, cols):
    for yl in range(2):
        for z in range(8):
            rows = slice(z * 32 + yl * 16, z * 32 + yl * 16 + 16)
            out[lead + (yl, z, slice(None), cols)] = block[rows].astype(BF)


def mlp_block(w1, w2, cols, n2, cot):
    hidden, slope = gelu_parts(dot(n2, w1[:, cols]))
    return hidden.astype(BF), (dot_nt(cot, w2[cols, :]) * slope).astype(BF)


def store_grads(n2t, cott, hidden, dpre, lead, c, keep, away):
    mine = pl.ds(pl.multiple_of(c * 256, 256), 256)
    sibs = pl.ds(pl.multiple_of((1 - c) * 256, 256), 256)
    for rows, out in ((sibs, away), (mine, keep)):
        store_rows(out, dot(n2t[rows, :], dpre), lead, slice(0, 256))
        store_rows(out, dot(cott[rows, :], hidden), lead, slice(256, 512))


def mlp_own_kernel(
    place, mixed_ref, tile, near, far, below, moved, g2, w1_own, w2_own,
    n2_ref, n2t, cot_ref, cott, out_acc, norm_acc, keep, away,
    hid_scr, dpre_scr, stage, wins,
):
    mx, c = place[0], place[3]
    load_windows(place[4], 1, tile, near, far, below, moved, stage, wins)
    mixed = mixed_ref[...].astype(F32)
    normed = norm(mixed, g2[...])[0]
    n2_ref[...] = normed.astype(BF)
    n2t[...] = normed.T.astype(BF)
    cott[...] = wins[...].T.astype(BF)
    cot_ref[...] = wins[...].astype(BF)
    n2, cot = n2_ref[...], cot_ref[...]
    for x in range(4):
        cols = slice(x * 256, x * 256 + 256)
        hidden, dpre = mlp_block(w1_own, w2_own, cols, n2, cot)
        hid_scr[:, cols] = hidden
        dpre_scr[:, cols] = dpre
        store_grads(n2t, cott, hidden, dpre, (x ^ mx,), c, keep, away)
    out_acc[...] = mixed + dot(hid_scr[...], w2_own[...])
    norm_acc[...] = dot_nt(dpre_scr[...], w1_own[...])


def mlp_other_kernel(
    place, mixed_ref, n2_ref, n2t, cot_ref, cott, out_acc, norm_acc, g2, w12_m, w12_s,
    band, tail, dm_ref, keep, away,
    hid_scr, dpre_scr, stage, wins,
):
    mx, c = place[0], place[3]
    n2, cot = n2_ref[...], cot_ref[...]
    for n, (pair, half) in enumerate(((w12_m, c), (w12_s, 1 - c))):
        for i in range(2):
            cols = slice(i * 256, i * 256 + 256)
            hidden, dpre = mlp_block(pair.at[0], pair.at[1], cols, n2, cot)
            hid_scr[:, n * 512 + i * 256 : n * 512 + i * 256 + 256] = hidden
            dpre_scr[:, n * 512 + i * 256 : n * 512 + i * 256 + 256] = dpre
            store_grads(n2t, cott, hidden, dpre, ((2 * half + i) ^ mx,), c, keep, away)
    d_norm = norm_acc[...] + (
        dot_nt(dpre_scr[:, :512], w12_m[0]) + dot_nt(dpre_scr[:, 512:], w12_s[0])
    )
    gain = g2[...]
    xhat, rstd = norm(mixed_ref[...].astype(F32), gain)[1:]
    scaled = d_norm * gain
    dm = cot.astype(F32) + rstd * (
        scaled
        - jnp.mean(scaled, -1, keepdims=True)
        - xhat * jnp.mean(scaled * xhat, -1, keepdims=True)
    )
    dm_ref[...] = dm.astype(BF)
    wins[...] = out_acc[...] + (dot(hid_scr[:, :512], w12_m[1]) + dot(hid_scr[:, 512:], w12_s[1]))
    store_windows(wins, stage, band, tail)


def attend_back_kernel(
    dm_ref, prob_ref, qkv_ref, wo_full, first, second,
    dqkv, dmt,
    dheads,
):
    dm = dm_ref[...]
    dmt[...] = dm.astype(F32).T.astype(BF)
    dheads[...] = dot_nt(dm, wo_full[...]).astype(BF)

    def window(w, carry):
        rows = pl.ds(pl.multiple_of(w * SEATS, 16), SEATS)
        for p in range(4):
            pc = slice(p * 128, p * 128 + 128)
            q2 = qkv_ref[rows, p * 128 : p * 128 + 128]
            k2 = qkv_ref[rows, 512 + p * 128 : 640 + p * 128]
            v2 = qkv_ref[rows, 1024 + p * 128 : 1152 + p * 128]
            do2 = dheads[rows, pc]
            dq = dk = dv = None
            for h in range(2):
                keep = head_mask(h)
                prob_b = prob_ref[w * 8 + p * 2 + h]
                prob = prob_b.astype(F32)
                do_h = jnp.where(keep, do2, BF(0))
                d_prob = dot_nt(do_h, v2)
                moment = jnp.sum(prob * d_prob, -1, keepdims=True)
                d_scores = (prob * (d_prob - moment)).astype(BF)
                pq = dot(d_scores, jnp.where(keep, k2, BF(0)))
                pk = dot_tn(d_scores, jnp.where(keep, q2, BF(0)))
                pv = dot_tn(prob_b, do_h)
                dq = pq if dq is None else dq + pq
                dk = pk if dk is None else dk + pk
                dv = pv if dv is None else dv + pv
            dqkv[rows, p * 128 : p * 128 + 128] = (dq * 0.125).astype(BF)
            dqkv[rows, 512 + p * 128 : 640 + p * 128] = dk.astype(BF)
            dqkv[rows, 1024 + p * 128 : 1152 + p * 128] = dv.astype(BF)
        return carry

    lax.fori_loop(0, WINS, window, 0)


def attend_grads_kernel(
    place, dqkv, dmt, heads_ref, n1t_ref, first, second, third, fourth,
    keep, away,
):
    mx, c, mt = place[0], place[3], place[4]
    mine = pl.ds(pl.multiple_of(c * 256, 256), 256)
    sibs = pl.ds(pl.multiple_of((1 - c) * 256, 256), 256)
    for rows, out in ((sibs, away), (mine, keep)):
        for t in range(2):
            for half in range(2):
                for which in range(2):
                    if which == 0 or half == 0:
                        start = (2 * which + half) * 512 + t * 256
                        grad = dot(n1t_ref[rows, :], dqkv[:, start : start + 256])
                    else:
                        grad = dot(dmt[rows, :], heads_ref[:, t * 256 : t * 256 + 256])
                    for sub in range(2):
                        lead = ((half * 2 + sub) ^ mx, t ^ mt)
                        cols = slice(which * 128, which * 128 + 128)
                        store_rows(out, grad[:, sub * 128 : sub * 128 + 128], lead, cols)


def whole(shape, dtype=BF):
    return jax.ShapeDtypeStruct(shape, dtype)


def call(kernel, args, outs, scratch=(), place=None, flops=0, name=None, after=(), limit=8):
    spec = pl.BlockSpec(memory_space=pltpu.VMEM)
    args = tuple(args) + tuple(after)
    specs = [spec] * len(args)
    if place is not None:
        args = (place,) + args
        specs = [pl.BlockSpec(memory_space=pltpu.SMEM)] + specs
    size = sum(a.size * a.dtype.itemsize for a in list(args) + list(outs))
    return pl.pallas_call(
        kernel,
        out_shape=tuple(outs),
        in_specs=specs,
        out_specs=tuple([spec] * len(outs)),
        scratch_shapes=list(scratch),
        compiler_params=pltpu.CompilerParams(vmem_limit_bytes=limit * MIB),
        cost_estimate=pl.CostEstimate(flops=flops, bytes_accessed=size, transcendentals=0),
        name=name,
    )(*args)


def add(*values):
    total = values[0].astype(F32)
    for value in values[1:]:
        total = total + value.astype(F32)
    return total.astype(BF)


def core_sum_kernel(keep, arrived, *outs):
    for x in range(4):
        outs[x][...] = add(keep[x], arrived[x])


def core_sum_two_kernel(keep, arrived, keep_two, arrived_two, *outs):
    for x in range(4):
        outs[x][0] = add(keep[x], arrived[x])
        outs[x][1] = add(keep_two[x], arrived_two[x])


def x_sum_kernel(place, *refs):
    fc, at, out = refs[0:4], refs[4:8], refs[-1]
    t = place[4]
    out[t, :, :, :, :512] = add(*[r[0] for r in fc])
    out[1 - t, :, :, :, :512] = add(*[r[1] for r in fc])
    out[:, :, :, :, 512:] = add(*[r[...] for r in at])


def last_sum_kernel(parts, out):
    total = parts[0].astype(F32)
    for i in range(1, 32):
        total = total + parts[i].astype(F32)
    for z in range(8):
        out[z] = total.astype(BF)


def copies_kernel(part, out):
    for i in range(8):
        out[i] = part[...]


def place_kernel(place, mine, sib, gq, go, g1, g2, scr2, scro):
    c = place[3]
    for src, cc in ((mine, c), (sib, 1 - c)):
        base = cc * 256
        for yl in range(2):
            for x in range(4):
                for z in range(8):
                    rows = pl.ds(pl.multiple_of(base + z * 32 + yl * 16, 16), 16)
                    chunk = src[2 * x + yl, z]
                    lo = (x % 2) * 128
                    g1[rows, x * 256 : x * 256 + 256] = chunk[:, :256]
                    scr2[rows, x * 256 : x * 256 + 256] = chunk[:, 256:512]
                    gq[x // 2, rows, lo : lo + 128] = chunk[:, 512:640]
                    if x < 2:
                        gq[2, rows, lo : lo + 128] = chunk[:, 640:]
                    else:
                        scro[rows, lo : lo + 128] = chunk[:, 640:]
    for i in range(4):
        g2[i * 256 : i * 256 + 256, :] = scr2[:, i * 256 : i * 256 + 256].astype(F32).T.astype(BF)
    go[...] = scro[...].astype(F32).T.astype(BF)


def core_phase(keep, away, after):
    outs = [whole(keep.shape[1:])] * 4
    kernel = without(core_sum_kernel, 2, len(after))
    return call(kernel, (keep, flip(away, c=1)), outs, name="core_sum", after=after)


def core_phase_two(keep, arrived, keep_two, arrived_two):
    outs = [whole((2,) + keep.shape[1:])] * 4
    return call(core_sum_two_kernel, (keep, arrived, keep_two, arrived_two), outs, name="core_sum_two")


def x_phase(cut):
    return [cut[0]] + [flip(cut[k], x=k) for k in (1, 2, 3)]


def reduce_and_gather(place, fc, at, after):
    (total,) = call(
        x_sum_kernel, (*fc, *at), [whole((2, 2, 8, 16, 768))], (), place, name="x_sum", after=after
    )
    parts = lax.all_to_all(total.reshape(32, 16, 768), ("tp", "yl", "z"), 0, 0)
    (chunks,) = call(last_sum_kernel, (parts,), [whole((8, 16, 768))], name="last_sum")
    column = lax.all_to_all(chunks, "z", 0, 0)
    (columns,) = call(copies_kernel, (column,), [whole((8, 8, 16, 768))], name="copies")
    mine = lax.all_to_all(columns, ("x", "yl"), 0, 0)
    sib = flip(mine, c=1)
    outs = [whole((3, 512, 256)), whole((256, 512)), whole((512, 1024)), whole((1024, 512))]
    scratch = [pltpu.VMEM((512, 1024), BF), pltpu.VMEM((512, 256), BF)]
    return call(place_kernel, (mine, sib), outs, scratch, place, name="place")


def per_device(tokens, labels, gain_one, second_norm_gain, w_qkv, w_out, w_fc1, w_fc2, cotangent):
    x, yl, z, c, t = [lax.axis_index(name) for name in AXES]
    place = jnp.stack([x, yl, z, c, t]).astype(jnp.int32)
    tile, cot = tokens[0], cotangent[0]

    near, far, below, wqo, w12 = cut_parts(place, tile, cot, w_qkv, w_out, w_fc1, w_fc2)
    wqo = flip(wqo, yl=1, t=1)
    rows = (flip(near, t=1), send(far, far_move), send(below, lat_move(-1)))
    (edge,) = call(edge_kernel, (tile, cot, *rows), [whole((2, 12, 6, D))], (), place, name="edge")
    moved = send(edge, lon_move(-1))
    wqo, w12 = fence((wqo, flip(w12, yl=1, t=1)), (edge,))
    wqo = join(place, wqo, "join_attend", (moved,))
    wqo_sib = flip(wqo, c=1)

    band = lax.dynamic_slice_in_dim(labels, t * 6, 6, 1)
    band = jnp.where(t == 0, band, band[::-1]).reshape(12, 48, 1)
    lab = to_windows(band).reshape(TOK)
    labc = jnp.broadcast_to(lab[:, None], (TOK, 128))
    labr = jnp.broadcast_to(lab.reshape(WINS, 1, SEATS), (WINS, 8, SEATS))

    stage = [pltpu.VMEM((12, 56, D), F32), pltpu.VMEM((TOK, D), F32)]
    n1t, qkv, prob, heads, wo_full, mixed = call(
        attend_kernel,
        (tile, *rows, moved, labc, labr, gain_one[None], w_qkv, w_out, wqo, wqo_sib),
        [
            whole((D, TOK)), whole((TOK, 3 * D)), whole((WINS * 8, SEATS, SEATS)),
            whole((TOK, D)), whole((D, D)), whole((TOK, D)),
        ],
        [pltpu.VMEM((TOK, D), BF)] + stage,
        place,
        flops=3 * 10**9,
        name="attend",
        limit=12,
    )
    grads = [whole((4, 2, 8, 16, 512))] * 2
    scratch = [pltpu.VMEM((TOK, 1024), BF), pltpu.VMEM((TOK, 1024), BF)] + stage
    tokens_like = [whole((TOK, D)), whole((D, TOK))] * 2 + [whole((TOK, D), F32)] * 2
    *carried, keep, away = call(
        mlp_own_kernel,
        (mixed, cot, *rows, moved, second_norm_gain[None], w_fc1, w_fc2),
        tokens_like + grads,
        scratch,
        place,
        flops=4 * 10**9,
        name="mlp_own",
        limit=12,
    )
    w12 = join(place, w12, "join_mlp", (mixed, keep))
    w12_sib = flip(w12, c=1)
    arrived = flip(away, c=1)
    out_band, tail, dm, keep_two, away_two = call(
        mlp_other_kernel,
        (mixed, *carried, second_norm_gain[None], w12, w12_sib),
        [whole((12, 48, D)), whole((12, 6, D)), whole((TOK, D))] + grads,
        scratch,
        place,
        flops=4 * 10**9,
        name="mlp_other",
        limit=12,
    )
    fc_cut = core_phase_two(keep, arrived, keep_two, flip(away_two, c=1))
    fc_parts = x_phase(fc_cut)
    out_moved = send(tail, lon_move(1))
    out = jnp.concatenate([out_moved, out_band[:, 6:]], 1)
    near, far, above = flip(out[6:9], t=1), send(out[9:12], far_back), send(out[3:6], lat_move(1))
    dqkv, dmt = call(
        attend_back_kernel,
        (dm, prob, qkv, wo_full),
        [whole((TOK, 3 * D)), whole((D, TOK))],
        [pltpu.VMEM((TOK, D), BF)],
        flops=4 * 10**9,
        name="attend_back",
        limit=12,
        after=(fc_cut[0], out_moved),
    )
    at = call(
        attend_grads_kernel,
        (dqkv, dmt, heads, n1t),
        [whole((4, 2, 2, 8, 16, 256))] * 2,
        (),
        place,
        name="attend_grads",
        limit=12,
        after=(fc_parts[1], fc_parts[3], near, far),
    )
    keep, away = at
    (away,) = fence((away,), fc_parts[2:3])
    at_cut = core_phase(keep, away, ())
    at_parts = x_phase(at_cut)
    gq, go, g1, g2 = reduce_and_gather(place, fc_parts, at_parts, (above,))
    out = jnp.where(
        t == 0,
        jnp.concatenate([far, out[0:6], near], 0),
        jnp.concatenate([above, near, far, out[0:3]], 0),
    )
    return out[None], gq, go, g1, g2


def without(kernel, start, count):
    return lambda *refs: kernel(*refs[:start], *refs[start + count :])


def solution(mesh):
    fine = Mesh(mesh.devices.reshape(4, 2, 8, 2, 2), AXES)
    lat, lon = ("x", "yl"), ("z", "c")
    return jax.shard_map(
        per_device,
        mesh=fine,
        in_specs=(
            P("tp", lat, lon, None),
            P(None, lat, lon),
            P(),
            P(),
            P(None, None, "tp"),
            P("tp", None),
            P(None, "tp"),
            P("tp", None),
            P("tp", lat, lon, None),
        ),
        out_specs=(
            P("tp", lat, lon, None),
            P(None, None, "tp"),
            P("tp", None),
            P(None, "tp"),
            P("tp", None),
        ),
        check_vma=False,
    )
```

```python
import functools

import jax
import jax.numpy as jnp
from jax import lax
from jax.experimental import pallas as pl
from jax.experimental.pallas import tpu as pltpu
from jax.sharding import Mesh
from jax.sharding import PartitionSpec as P

D = 512
FF = 2048
WLAT = 6
WLON = 12
SEATS = 144
WINS = 4
TOK = SEATS * WINS
EPS = 1e-05
GELU_C = 0.7978845608028654
BF = jnp.bfloat16
F32 = jnp.float32
AXES = ("x", "yl", "z", "c", "tp")
MIB = 1024 * 1024


def pairs_of(move):
    pairs = []
    for x in range(4):
        for yl in range(2):
            for z in range(8):
                for c in range(2):
                    for t in range(2):
                        dest = move(x, yl, z, c, t)
                        if dest is not None:
                            pairs.append((rank(x, yl, z, c, t), rank(*dest)))
    return pairs


def rank(x, yl, z, c, t):
    return ((2 * x + yl) * 16 + 2 * z + c) * 2 + t


def send(value, move):
    return lax.ppermute(value, AXES, pairs_of(move))


def flip(value, x=0, yl=0, z=0, c=0, t=0):
    return send(value, lambda a, b, d, e, f: (a ^ x, b ^ yl, d ^ z, e ^ c, f ^ t))


def shift_lat(x, yl, step):
    lat = (2 * x + yl + step) % 8
    return lat // 2, lat % 2


def shift_lon(z, c, step):
    lon = (2 * z + c + step) % 16
    return lon // 2, lon % 2


def lon_move(step):
    def move(x, yl, z, c, t):
        zz, cc = shift_lon(z, c, step)
        return x, yl, zz, cc, t

    return move


def far_move(x, yl, z, c, t):
    if t == 1:
        return x, yl, z, c, 0
    xx, yy = shift_lat(x, yl, -1)
    return xx, yy, z, c, 1


def far_back(x, yl, z, c, t):
    if t == 0:
        return x, yl, z, c, 1
    xx, yy = shift_lat(x, yl, 1)
    return xx, yy, z, c, 0


def lat_move(step):
    def move(x, yl, z, c, t):
        if t == 0:
            return None
        xx, yy = shift_lat(x, yl, step)
        return xx, yy, z, c, t

    return move


def fence(values, after):
    n = len(values)
    spec = pl.BlockSpec(memory_space=pltpu.VMEM)
    return pl.pallas_call(
        lambda *refs: None,
        out_shape=tuple(jax.ShapeDtypeStruct(v.shape, v.dtype) for v in values),
        in_specs=[spec] * (n + len(after)),
        out_specs=tuple([spec] * n),
        input_output_aliases={i: i for i in range(n)},
        compiler_params=pltpu.CompilerParams(vmem_limit_bytes=MIB),
        name="fence",
    )(*values, *after)


def cut_kernel(place, tile, cot, wq, wo, w1, w2, *refs):
    rows, attend, mlp, sems = refs[0:6], refs[6], refs[7], refs[8]
    c, t = place[3], place[4]
    half = pl.ds(pl.multiple_of(c * 256, 256), 256)
    halves = pl.ds(pl.multiple_of(c * 512, 512), 512)
    copies = []
    for ref, (near, far, below) in ((tile, rows[:3]), (cot, rows[3:])):
        copies.append((ref.at[pl.ds(9 - 6 * t, 3)], near))
        copies.append((ref.at[pl.ds(6 * t, 3)], far))
        copies.append((ref.at[pl.ds(0, 3)], below))
    copies.append((wq.at[:, half], attend.at[pl.ds(0, 3)]))
    copies.append((wo.at[:, half], attend.at[3]))
    copies.append((w1.at[:, halves], mlp.at[0]))
    copies.append((w2.at[halves], mlp.at[1]))
    copies = [pltpu.make_async_copy(a, b, sems.at[i]) for i, (a, b) in enumerate(copies)]
    for copy in copies:
        copy.start()
    for copy in copies:
        copy.wait()


def cut_parts(place, *arrays):
    shapes = [(3, 48, D)] * 6 + [(4, 256, 256), (2, 512, 512)]
    hbm = pl.BlockSpec(memory_space=pltpu.HBM)
    return pl.pallas_call(
        cut_kernel,
        out_shape=tuple(whole(shape) for shape in shapes),
        in_specs=[pl.BlockSpec(memory_space=pltpu.SMEM)] + [hbm] * len(arrays),
        out_specs=tuple([pl.BlockSpec(memory_space=pltpu.VMEM)] * len(shapes)),
        scratch_shapes=[pltpu.SemaphoreType.DMA((10,))],
        compiler_params=pltpu.CompilerParams(vmem_limit_bytes=52 * MIB),
        name="cut",
    )(place, *arrays)


def exchange_rows(near, far, below):
    return flip(near, t=1), send(far, far_move), send(below, lat_move(-1))


def edge_kernel(place, tile, near, far, below, edge):
    t = place[4]
    for i in range(3):
        edge[i] = tile[3 + i + 6 * t, :6]
        row = jnp.where(t == 0, tile[6 + i, :6].astype(F32), below[i, :6].astype(F32))
        edge[3 + i] = row.astype(BF)
        edge[6 + i] = near[i, :6]
        edge[9 + i] = far[i, :6]


def first_columns(place, tile, rows, name, after=()):
    kernel = without(edge_kernel, 5, len(after))
    (edge,) = call(kernel, (tile, *rows), [whole((12, 6, D))], (), place, name=name, after=after)
    return edge


def to_windows(band):
    width = band.shape[-1]
    return band.reshape(12, WINS, WLON, width).transpose(1, 0, 2, 3).reshape(TOK, width)


def load_windows(t, tile, near, far, below, moved, stage, wins):
    for row in range(12):
        if row < 3:
            value = tile[3 + row + 6 * t].astype(F32)
        elif row < 6:
            value = jnp.where(t == 0, tile[3 + row].astype(F32), below[row - 3].astype(F32))
        elif row < 9:
            value = near[row - 6].astype(F32)
        else:
            value = far[row - 9].astype(F32)
        stage[row, 0:48] = value
        stage[row, 48:54] = moved[row].astype(F32)
        for w in range(WINS):
            start = w * SEATS + row * WLON
            wins[start : start + WLON, :] = stage[row, 6 + 12 * w : 18 + 12 * w]


def store_windows(wins, stage, band, tail):
    for row in range(12):
        for w in range(WINS):
            start = w * SEATS + row * WLON
            stage[row, 6 + 12 * w : 18 + 12 * w] = wins[start : start + WLON, :]
        band[row] = stage[row, 0:48].astype(BF)
        tail[row] = stage[row, 48:54].astype(BF)


def norm(value, gain):
    centered = value - jnp.mean(value, -1, keepdims=True)
    rstd = lax.rsqrt(jnp.mean(centered * centered, -1, keepdims=True) + EPS)
    xhat = centered * rstd
    return xhat * gain, xhat, rstd


def dot(a, b):
    return lax.dot_general(a, b, (((1,), (0,)), ((), ())), preferred_element_type=F32)


def dot_nt(a, b):
    return lax.dot_general(a, b, (((1,), (1,)), ((), ())), preferred_element_type=F32)


def dot_tn(a, b):
    return lax.dot_general(a, b, (((0,), (0,)), ((), ())), preferred_element_type=F32)


def head_mask(h):
    lane = lax.broadcasted_iota(jnp.int32, (1, 128), 1)
    return (lane < 64) if h == 0 else (lane >= 64)


def attend_kernel(
    place, tile, near, far, below, moved, labc, labr, g1, wq_own, wo_own, wqo_m, wqo_s,
    n1t_ref, qkv_ref, prob_ref, heads_ref, wo_full, mixed_ref, n1_scr, stage, wins,
):
    c = place[3]
    mine = pl.ds(pl.multiple_of(c * 256, 256), 256)
    sibs = pl.ds(pl.multiple_of((1 - c) * 256, 256), 256)
    load_windows(place[4], tile, near, far, below, moved, stage, wins)
    x = wins[...]
    normed = norm(x, g1[...])[0]
    n1_scr[...] = normed.astype(BF)
    n1t_ref[...] = normed.T.astype(BF)
    n1 = n1_scr[...]
    for i in range(3):
        scale = 0.125 if i == 0 else 1.0
        own = dot(n1, wq_own[i]).astype(BF)
        other = (dot(n1_scr[:, mine], wqo_m[i]) + dot(n1_scr[:, sibs], wqo_s[i])).astype(BF)
        qkv_ref[:, i * 512 : i * 512 + 256] = own * BF(scale)
        qkv_ref[:, i * 512 + 256 : i * 512 + 512] = other * BF(scale)

    def window(w, carry):
        rows = pl.ds(pl.multiple_of(w * SEATS, 16), SEATS)
        same = labc[rows, 0:1] == labr[w, 0:1, :]
        for p in range(4):
            q2 = qkv_ref[rows, p * 128 : p * 128 + 128]
            k2 = qkv_ref[rows, 512 + p * 128 : 640 + p * 128]
            v2 = qkv_ref[rows, 1024 + p * 128 : 1152 + p * 128]
            total = None
            for h in range(2):
                keep = head_mask(h)
                scores = dot_nt(jnp.where(keep, q2, BF(0)), k2)
                scores = jnp.where(same, scores, -1e30)
                expo = jnp.exp(scores - jnp.max(scores, -1, keepdims=True))
                prob = (expo * (1.0 / jnp.sum(expo, -1, keepdims=True))).astype(BF)
                prob_ref[w * 8 + p * 2 + h] = prob
                part = dot(prob, jnp.where(keep, v2, BF(0)))
                total = part if total is None else total + part
            heads_ref[rows, p * 128 : p * 128 + 128] = total.astype(BF)
        return carry

    lax.fori_loop(0, WINS, window, 0)
    wo_full[0:256, :] = wo_own[...]
    wo_full[256:512, mine] = wqo_m[3]
    wo_full[256:512, sibs] = wqo_s[3]
    attn = dot(heads_ref[...], wo_full[...]).astype(BF).astype(F32)
    mixed_ref[...] = (x + attn).astype(BF)


def gelu_parts(v):
    square = v * v
    tanh_v = jnp.tanh(GELU_C * v * (1.0 + 0.044715 * square))
    half = 0.5 * (1.0 + tanh_v)
    slope = half + 0.5 * v * (1.0 - tanh_v * tanh_v) * (GELU_C + (3.0 * 0.044715 * GELU_C) * square)
    return v * half, slope


def store_rows(out, block, lead, cols):
    for yl in range(2):
        for z in range(8):
            rows = slice(z * 32 + yl * 16, z * 32 + yl * 16 + 16)
            out[lead + (yl, z, slice(None), cols)] = block[rows].astype(BF)


def mlp_block(w1, w2, cols, n2, cot):
    hidden, slope = gelu_parts(dot(n2, w1[:, cols]))
    return hidden.astype(BF), (dot_nt(cot, w2[cols, :]) * slope).astype(BF)


def store_grads(n2t, cott, hidden, dpre, lead, c, keep, away):
    mine = pl.ds(pl.multiple_of(c * 256, 256), 256)
    sibs = pl.ds(pl.multiple_of((1 - c) * 256, 256), 256)
    for rows, out in ((sibs, away), (mine, keep)):
        store_rows(out, dot(n2t[rows, :], dpre), lead, slice(0, 256))
        store_rows(out, dot(cott[rows, :], hidden), lead, slice(256, 512))


def mlp_own_kernel(
    place, mixed_ref, tile, near, far, below, moved, g2, w1_own, w2_own,
    n2_ref, n2t, cot_ref, cott, out_acc, norm_acc, keep, away,
    hid_scr, dpre_scr, stage, wins,
):
    mx, c = place[0], place[3]
    load_windows(place[4], tile, near, far, below, moved, stage, wins)
    mixed = mixed_ref[...].astype(F32)
    normed = norm(mixed, g2[...])[0]
    n2_ref[...] = normed.astype(BF)
    n2t[...] = normed.T.astype(BF)
    cott[...] = wins[...].T.astype(BF)
    cot_ref[...] = wins[...].astype(BF)
    n2, cot = n2_ref[...], cot_ref[...]
    for x in range(4):
        cols = slice(x * 256, x * 256 + 256)
        hidden, dpre = mlp_block(w1_own, w2_own, cols, n2, cot)
        hid_scr[:, cols] = hidden
        dpre_scr[:, cols] = dpre
        store_grads(n2t, cott, hidden, dpre, (x ^ mx,), c, keep, away)
    out_acc[...] = mixed + dot(hid_scr[...], w2_own[...])
    norm_acc[...] = dot_nt(dpre_scr[...], w1_own[...])


def mlp_other_kernel(
    place, mixed_ref, n2_ref, n2t, cot_ref, cott, out_acc, norm_acc, g2, w12_m, w12_s,
    band, tail, dm_ref, keep, away,
    hid_scr, dpre_scr, stage, wins,
):
    mx, c = place[0], place[3]
    n2, cot = n2_ref[...], cot_ref[...]
    for n, (pair, half) in enumerate(((w12_m, c), (w12_s, 1 - c))):
        for i in range(2):
            cols = slice(i * 256, i * 256 + 256)
            hidden, dpre = mlp_block(pair.at[0], pair.at[1], cols, n2, cot)
            hid_scr[:, n * 512 + i * 256 : n * 512 + i * 256 + 256] = hidden
            dpre_scr[:, n * 512 + i * 256 : n * 512 + i * 256 + 256] = dpre
            store_grads(n2t, cott, hidden, dpre, ((2 * half + i) ^ mx,), c, keep, away)
    d_norm = norm_acc[...] + (
        dot_nt(dpre_scr[:, :512], w12_m[0]) + dot_nt(dpre_scr[:, 512:], w12_s[0])
    )
    gain = g2[...]
    xhat, rstd = norm(mixed_ref[...].astype(F32), gain)[1:]
    scaled = d_norm * gain
    dm = cot.astype(F32) + rstd * (
        scaled
        - jnp.mean(scaled, -1, keepdims=True)
        - xhat * jnp.mean(scaled * xhat, -1, keepdims=True)
    )
    dm_ref[...] = dm.astype(BF)
    wins[...] = out_acc[...] + (dot(hid_scr[:, :512], w12_m[1]) + dot(hid_scr[:, 512:], w12_s[1]))
    store_windows(wins, stage, band, tail)


def attend_back_kernel(
    dm_ref, prob_ref, qkv_ref, wo_full, first, second,
    dqkv, dmt,
    dheads,
):
    dm = dm_ref[...]
    dmt[...] = dm.astype(F32).T.astype(BF)
    dheads[...] = dot_nt(dm, wo_full[...]).astype(BF)

    def window(w, carry):
        rows = pl.ds(pl.multiple_of(w * SEATS, 16), SEATS)
        for p in range(4):
            pc = slice(p * 128, p * 128 + 128)
            q2 = qkv_ref[rows, p * 128 : p * 128 + 128]
            k2 = qkv_ref[rows, 512 + p * 128 : 640 + p * 128]
            v2 = qkv_ref[rows, 1024 + p * 128 : 1152 + p * 128]
            do2 = dheads[rows, pc]
            dq = dk = dv = None
            for h in range(2):
                keep = head_mask(h)
                prob_b = prob_ref[w * 8 + p * 2 + h]
                prob = prob_b.astype(F32)
                do_h = jnp.where(keep, do2, BF(0))
                d_prob = dot_nt(do_h, v2)
                moment = jnp.sum(prob * d_prob, -1, keepdims=True)
                d_scores = (prob * (d_prob - moment)).astype(BF)
                pq = dot(d_scores, jnp.where(keep, k2, BF(0)))
                pk = dot_tn(d_scores, jnp.where(keep, q2, BF(0)))
                pv = dot_tn(prob_b, do_h)
                dq = pq if dq is None else dq + pq
                dk = pk if dk is None else dk + pk
                dv = pv if dv is None else dv + pv
            dqkv[rows, p * 128 : p * 128 + 128] = (dq * 0.125).astype(BF)
            dqkv[rows, 512 + p * 128 : 640 + p * 128] = dk.astype(BF)
            dqkv[rows, 1024 + p * 128 : 1152 + p * 128] = dv.astype(BF)
        return carry

    lax.fori_loop(0, WINS, window, 0)


def attend_grads_kernel(
    place, dqkv, dmt, heads_ref, n1t_ref, first, second,
    keep, away,
):
    mx, c, mt = place[0], place[3], place[4]
    mine = pl.ds(pl.multiple_of(c * 256, 256), 256)
    sibs = pl.ds(pl.multiple_of((1 - c) * 256, 256), 256)
    for rows, out in ((sibs, away), (mine, keep)):
        for t in range(2):
            for half in range(2):
                for which in range(2):
                    if which == 0 or half == 0:
                        start = (2 * which + half) * 512 + t * 256
                        grad = dot(n1t_ref[rows, :], dqkv[:, start : start + 256])
                    else:
                        grad = dot(dmt[rows, :], heads_ref[:, t * 256 : t * 256 + 256])
                    for sub in range(2):
                        lead = ((half * 2 + sub) ^ mx, t ^ mt)
                        cols = slice(which * 128, which * 128 + 128)
                        store_rows(out, grad[:, sub * 128 : sub * 128 + 128], lead, cols)


def whole(shape, dtype=BF):
    return jax.ShapeDtypeStruct(shape, dtype)


def call(kernel, args, outs, scratch=(), place=None, flops=0, name=None, after=(), limit=8):
    spec = pl.BlockSpec(memory_space=pltpu.VMEM)
    args = tuple(args) + tuple(after)
    specs = [spec] * len(args)
    if place is not None:
        args = (place,) + args
        specs = [pl.BlockSpec(memory_space=pltpu.SMEM)] + specs
    size = sum(a.size * a.dtype.itemsize for a in list(args) + list(outs))
    return pl.pallas_call(
        kernel,
        out_shape=tuple(outs),
        in_specs=specs,
        out_specs=tuple([spec] * len(outs)),
        scratch_shapes=list(scratch),
        compiler_params=pltpu.CompilerParams(vmem_limit_bytes=limit * MIB),
        cost_estimate=pl.CostEstimate(flops=flops, bytes_accessed=size, transcendentals=0),
        name=name,
    )(*args)


def add(*values):
    total = values[0].astype(F32)
    for value in values[1:]:
        total = total + value.astype(F32)
    return total.astype(BF)


def core_sum_kernel(keep, arrived, *outs):
    for x in range(4):
        outs[x][...] = add(keep[x], arrived[x])


def core_sum_two_kernel(keep, arrived, keep_two, arrived_two, *outs):
    for x in range(4):
        outs[x][0] = add(keep[x], arrived[x])
        outs[x][1] = add(keep_two[x], arrived_two[x])


def x_sum_kernel(place, *refs):
    fc, at, out = refs[0:4], refs[4:8], refs[-1]
    t = place[4]
    out[t, :, :, :, :512] = add(*[r[0] for r in fc])
    out[1 - t, :, :, :, :512] = add(*[r[1] for r in fc])
    out[:, :, :, :, 512:] = add(*[r[...] for r in at])


def last_sum_kernel(parts, out):
    total = parts[0].astype(F32)
    for i in range(1, 32):
        total = total + parts[i].astype(F32)
    for z in range(8):
        out[z] = total.astype(BF)


def copies_kernel(part, out):
    for i in range(8):
        out[i] = part[...]


def place_kernel(place, mine, sib, gq, go, g1, g2, scr2, scro):
    c = place[3]
    for src, cc in ((mine, c), (sib, 1 - c)):
        base = cc * 256
        for yl in range(2):
            for x in range(4):
                for z in range(8):
                    rows = pl.ds(pl.multiple_of(base + z * 32 + yl * 16, 16), 16)
                    chunk = src[2 * x + yl, z]
                    lo = (x % 2) * 128
                    g1[rows, x * 256 : x * 256 + 256] = chunk[:, :256]
                    scr2[rows, x * 256 : x * 256 + 256] = chunk[:, 256:512]
                    gq[x // 2, rows, lo : lo + 128] = chunk[:, 512:640]
                    if x < 2:
                        gq[2, rows, lo : lo + 128] = chunk[:, 640:]
                    else:
                        scro[rows, lo : lo + 128] = chunk[:, 640:]
    for i in range(4):
        g2[i * 256 : i * 256 + 256, :] = scr2[:, i * 256 : i * 256 + 256].astype(F32).T.astype(BF)
    go[...] = scro[...].astype(F32).T.astype(BF)


def core_phase(keep, away, after):
    outs = [whole(keep.shape[1:])] * 4
    kernel = without(core_sum_kernel, 2, len(after))
    return call(kernel, (keep, flip(away, c=1)), outs, name="core_sum", after=after)


def core_phase_two(keep, arrived, keep_two, arrived_two):
    outs = [whole((2,) + keep.shape[1:])] * 4
    return call(core_sum_two_kernel, (keep, arrived, keep_two, arrived_two), outs, name="core_sum_two")


def x_phase(cut):
    return [cut[0]] + [flip(cut[k], x=k) for k in (1, 2, 3)]


def reduce_and_gather(place, total, after):
    parts = lax.all_to_all(total.reshape(32, 16, 768), ("tp", "yl", "z"), 0, 0)
    kernel = without(last_sum_kernel, 1, len(after))
    (chunks,) = call(kernel, (parts,), [whole((8, 16, 768))], name="last_sum", after=after)
    column = lax.all_to_all(chunks, "z", 0, 0)
    (columns,) = call(copies_kernel, (column,), [whole((8, 8, 16, 768))], name="copies")
    mine = lax.all_to_all(columns, ("x", "yl"), 0, 0)
    sib = flip(mine, c=1)
    outs = [whole((3, 512, 256)), whole((256, 512)), whole((512, 1024)), whole((1024, 512))]
    scratch = [pltpu.VMEM((512, 1024), BF), pltpu.VMEM((512, 256), BF)]
    return call(place_kernel, (mine, sib), outs, scratch, place, name="place")


def per_device(tokens, labels, gain_one, second_norm_gain, w_qkv, w_out, w_fc1, w_fc2, cotangent):
    x, yl, z, c, t = [lax.axis_index(name) for name in AXES]
    place = jnp.stack([x, yl, z, c, t]).astype(jnp.int32)
    tile, cot = tokens[0], cotangent[0]

    *pieces, wqo, w12 = cut_parts(place, tile, cot, w_qkv, w_out, w_fc1, w_fc2)
    wqo = flip(wqo, yl=1, t=1)
    rows = exchange_rows(*pieces[:3])

    band = lax.dynamic_slice_in_dim(labels, t * 6, 6, 1)
    band = jnp.where(t == 0, band, band[::-1]).reshape(12, 48, 1)
    lab = to_windows(band).reshape(TOK)
    labc = jnp.broadcast_to(lab[:, None], (TOK, 128))
    labr = jnp.broadcast_to(lab.reshape(WINS, 1, SEATS), (WINS, 8, SEATS))

    edge = first_columns(place, tile, rows, "edge", (labc, labr))
    moved = send(edge, lon_move(-1))
    cot_rows = exchange_rows(*fence(pieces[3:], (edge,)))
    wqo_sib = flip(wqo, c=1)
    cot_edge = first_columns(place, cot, cot_rows, "cot_edge", (moved, wqo))
    (w12,) = fence((w12,), (cot_edge,))
    w12 = flip(w12, yl=1, t=1)
    cot_moved = send(cot_edge, lon_move(-1))

    stage = [pltpu.VMEM((12, 56, D), F32), pltpu.VMEM((TOK, D), F32)]
    n1t, qkv, prob, heads, wo_full, mixed = call(
        without(attend_kernel, 13, 1),
        (tile, *rows, moved, labc, labr, gain_one[None], w_qkv, w_out, wqo, wqo_sib),
        [
            whole((D, TOK)), whole((TOK, 3 * D)), whole((WINS * 8, SEATS, SEATS)),
            whole((TOK, D)), whole((D, D)), whole((TOK, D)),
        ],
        [pltpu.VMEM((TOK, D), BF)] + stage,
        place,
        flops=3 * 10**9,
        name="attend",
        limit=12,
        after=(cot_edge,),
    )
    grads = [whole((4, 2, 8, 16, 512))] * 2
    scratch = [pltpu.VMEM((TOK, 1024), BF), pltpu.VMEM((TOK, 1024), BF)] + stage
    tokens_like = [whole((TOK, D)), whole((D, TOK))] * 2 + [whole((TOK, D), F32)] * 2
    *carried, keep, away = call(
        mlp_own_kernel,
        (mixed, cot, *cot_rows, cot_moved, second_norm_gain[None], w_fc1, w_fc2),
        tokens_like + grads,
        scratch,
        place,
        flops=4 * 10**9,
        name="mlp_own",
        limit=12,
    )
    (w12,) = fence((w12,), (keep,))
    w12_sib = flip(w12, c=1)
    arrived = flip(away, c=1)
    out_band, tail, dm, keep_two, away_two = call(
        mlp_other_kernel,
        (mixed, *carried, second_norm_gain[None], w12, w12_sib),
        [whole((12, 48, D)), whole((12, 6, D)), whole((TOK, D))] + grads,
        scratch,
        place,
        flops=4 * 10**9,
        name="mlp_other",
        limit=12,
    )
    fc_cut = core_phase_two(keep, arrived, keep_two, flip(away_two, c=1))
    fc_parts = x_phase(fc_cut)
    out_moved = send(tail, lon_move(1))
    out = jnp.concatenate([out_moved, out_band[:, 6:]], 1)
    dqkv, dmt = call(
        attend_back_kernel,
        (dm, prob, qkv, wo_full),
        [whole((TOK, 3 * D)), whole((D, TOK))],
        [pltpu.VMEM((TOK, D), BF)],
        flops=4 * 10**9,
        name="attend_back",
        limit=12,
        after=(fc_cut[0], out_moved),
    )
    at = call(
        attend_grads_kernel,
        (dqkv, dmt, heads, n1t),
        [whole((4, 2, 2, 8, 16, 256))] * 2,
        (),
        place,
        name="attend_grads",
        limit=12,
        after=(fc_parts[1], fc_parts[3]),
    )
    keep, away = at
    (away,) = fence((away,), fc_parts[2:3])
    at_cut = core_phase(keep, away, ())
    at_parts = x_phase(at_cut)
    (total,) = call(
        x_sum_kernel, (*fc_parts, *at_parts), [whole((2, 2, 8, 16, 768))], (), place, name="x_sum"
    )
    near, far, above = fence((out[6:9], out[9:12], out[3:6]), (total,))
    near, far, above = flip(near, t=1), send(far, far_back), send(above, lat_move(1))
    gq, go, g1, g2 = reduce_and_gather(place, total, (near, far, above))
    out = jnp.where(
        t == 0,
        jnp.concatenate([far, out[0:6], near], 0),
        jnp.concatenate([above, near, far, out[0:3]], 0),
    )
    return out[None], gq, go, g1, g2


def without(kernel, start, count):
    return lambda *refs: kernel(*refs[:start], *refs[start + count :])


def solution(mesh):
    fine = Mesh(mesh.devices.reshape(4, 2, 8, 2, 2), AXES)
    lat, lon = ("x", "yl"), ("z", "c")
    return jax.shard_map(
        per_device,
        mesh=fine,
        in_specs=(
            P("tp", lat, lon, None),
            P(None, lat, lon),
            P(),
            P(),
            P(None, None, "tp"),
            P("tp", None),
            P(None, "tp"),
            P("tp", None),
            P("tp", lat, lon, None),
        ),
        out_specs=(
            P("tp", lat, lon, None),
            P(None, None, "tp"),
            P("tp", None),
            P(None, "tp"),
            P("tp", None),
        ),
        check_vma=False,
    )
```

```python
import functools

import jax
import jax.numpy as jnp
from jax import lax
from jax.experimental import pallas as pl
from jax.experimental.pallas import tpu as pltpu
from jax.sharding import Mesh
from jax.sharding import PartitionSpec as P

D = 512
FF = 2048
WLAT = 6
WLON = 12
SEATS = 144
WINS = 4
TOK = SEATS * WINS
EPS = 1e-05
GELU_C = 0.7978845608028654
BF = jnp.bfloat16
F32 = jnp.float32
AXES = ("x", "yl", "z", "c", "tp")
MIB = 1024 * 1024


def pairs_of(move):
    pairs = []
    for x in range(4):
        for yl in range(2):
            for z in range(8):
                for c in range(2):
                    for t in range(2):
                        dest = move(x, yl, z, c, t)
                        if dest is not None:
                            pairs.append((rank(x, yl, z, c, t), rank(*dest)))
    return pairs


def rank(x, yl, z, c, t):
    return ((2 * x + yl) * 16 + 2 * z + c) * 2 + t


def send(value, move):
    return lax.ppermute(value, AXES, pairs_of(move))


def flip(value, x=0, yl=0, z=0, c=0, t=0):
    return send(value, lambda a, b, d, e, f: (a ^ x, b ^ yl, d ^ z, e ^ c, f ^ t))


def shift_lat(x, yl, step):
    lat = (2 * x + yl + step) % 8
    return lat // 2, lat % 2


def shift_lon(z, c, step):
    lon = (2 * z + c + step) % 16
    return lon // 2, lon % 2


def lon_move(step):
    def move(x, yl, z, c, t):
        zz, cc = shift_lon(z, c, step)
        return x, yl, zz, cc, t

    return move


def far_move(x, yl, z, c, t):
    if t == 1:
        return x, yl, z, c, 0
    xx, yy = shift_lat(x, yl, -1)
    return xx, yy, z, c, 1


def far_back(x, yl, z, c, t):
    if t == 0:
        return x, yl, z, c, 1
    xx, yy = shift_lat(x, yl, 1)
    return xx, yy, z, c, 0


def lat_move(step):
    def move(x, yl, z, c, t):
        if t == 0:
            return None
        xx, yy = shift_lat(x, yl, step)
        return xx, yy, z, c, t

    return move


def fence(values, after):
    n = len(values)
    spec = pl.BlockSpec(memory_space=pltpu.VMEM)
    return pl.pallas_call(
        lambda *refs: None,
        out_shape=tuple(jax.ShapeDtypeStruct(v.shape, v.dtype) for v in values),
        in_specs=[spec] * (n + len(after)),
        out_specs=tuple([spec] * n),
        input_output_aliases={i: i for i in range(n)},
        compiler_params=pltpu.CompilerParams(vmem_limit_bytes=8 * MIB),
        name="fence",
    )(*values, *after)


def cut_kernel(place, tile, cot, wq, wo, w1, w2, *refs):
    rows, attend, mlp, sems = refs[0:6], refs[6], refs[7], refs[8]
    c, t = place[3], place[4]
    half = pl.ds(pl.multiple_of(c * 256, 256), 256)
    halves = pl.ds(pl.multiple_of(c * 512, 512), 512)
    copies = []
    for ref, (near, far, below) in ((tile, rows[:3]), (cot, rows[3:])):
        copies.append((ref.at[pl.ds(9 - 6 * t, 3)], near))
        copies.append((ref.at[pl.ds(6 * t, 3)], far))
        copies.append((ref.at[pl.ds(0, 3)], below))
    copies.append((wq.at[:, half], attend.at[pl.ds(0, 3)]))
    copies.append((wo.at[:, half], attend.at[3]))
    x = place[0]
    copies.append((w1.at[pl.ds(pl.multiple_of(x * 128, 128), 128), halves], mlp.at[0]))
    copies.append((w2.at[pl.ds(pl.multiple_of((c * 4 + x) * 128, 128), 128)], mlp.at[1]))
    copies = [pltpu.make_async_copy(a, b, sems.at[i]) for i, (a, b) in enumerate(copies)]
    for copy in copies:
        copy.start()
    for copy in copies:
        copy.wait()


def cut_parts(place, *arrays):
    shapes = [(3, 48, D)] * 6 + [(4, 256, 256), (2, 128, 512)]
    hbm = pl.BlockSpec(memory_space=pltpu.HBM)
    return pl.pallas_call(
        cut_kernel,
        out_shape=tuple(whole(shape) for shape in shapes),
        in_specs=[pl.BlockSpec(memory_space=pltpu.SMEM)] + [hbm] * len(arrays),
        out_specs=tuple([pl.BlockSpec(memory_space=pltpu.VMEM)] * len(shapes)),
        scratch_shapes=[pltpu.SemaphoreType.DMA((10,))],
        compiler_params=pltpu.CompilerParams(vmem_limit_bytes=52 * MIB),
        name="cut",
    )(place, *arrays)


def exchange_rows(near, far, below):
    return flip(near, t=1), send(far, far_move), send(below, lat_move(-1))


def edge_kernel(place, tile, near, far, below, edge):
    t = place[4]
    for i in range(3):
        edge[i] = tile[3 + i + 6 * t, :6]
        row = jnp.where(t == 0, tile[6 + i, :6].astype(F32), below[i, :6].astype(F32))
        edge[3 + i] = row.astype(BF)
        edge[6 + i] = near[i, :6]
        edge[9 + i] = far[i, :6]


def join_kernel(place, *refs):
    out = refs[4]
    rows = refs[0].shape[1]
    for k in range(4):
        out[:, pl.ds(pl.multiple_of((place[0] ^ k) * rows, rows), rows), :] = refs[k][...]


def join(place, part, name, after=()):
    depth, rows, width = part.shape
    parts = [part] + [flip(part, x=k) for k in (1, 2, 3)]
    out = whole((depth, 4 * rows, width))
    (out,) = call(without(join_kernel, 5, len(after)), parts, [out], (), place, name=name, after=after)
    return out


def first_columns(place, tile, rows, name, after=()):
    kernel = without(edge_kernel, 5, len(after))
    (edge,) = call(kernel, (tile, *rows), [whole((12, 6, D))], (), place, name=name, after=after)
    return edge


def to_windows(band):
    width = band.shape[-1]
    return band.reshape(12, WINS, WLON, width).transpose(1, 0, 2, 3).reshape(TOK, width)


def load_windows(t, tile, near, far, below, moved, stage, wins):
    for row in range(12):
        if row < 3:
            value = tile[3 + row + 6 * t].astype(F32)
        elif row < 6:
            value = jnp.where(t == 0, tile[3 + row].astype(F32), below[row - 3].astype(F32))
        elif row < 9:
            value = near[row - 6].astype(F32)
        else:
            value = far[row - 9].astype(F32)
        stage[row, 0:48] = value
        stage[row, 48:54] = moved[row].astype(F32)
        for w in range(WINS):
            start = w * SEATS + row * WLON
            wins[start : start + WLON, :] = stage[row, 6 + 12 * w : 18 + 12 * w]


def store_windows(wins, stage, band, tail):
    for row in range(12):
        for w in range(WINS):
            start = w * SEATS + row * WLON
            stage[row, 6 + 12 * w : 18 + 12 * w] = wins[start : start + WLON, :]
        band[row] = stage[row, 0:48].astype(BF)
        tail[row] = stage[row, 48:54].astype(BF)


def norm(value, gain):
    centered = value - jnp.mean(value, -1, keepdims=True)
    rstd = lax.rsqrt(jnp.mean(centered * centered, -1, keepdims=True) + EPS)
    xhat = centered * rstd
    return xhat * gain, xhat, rstd


def dot(a, b):
    return lax.dot_general(a, b, (((1,), (0,)), ((), ())), preferred_element_type=F32)


def dot_nt(a, b):
    return lax.dot_general(a, b, (((1,), (1,)), ((), ())), preferred_element_type=F32)


def dot_tn(a, b):
    return lax.dot_general(a, b, (((0,), (0,)), ((), ())), preferred_element_type=F32)


def head_mask(h):
    lane = lax.broadcasted_iota(jnp.int32, (1, 128), 1)
    return (lane < 64) if h == 0 else (lane >= 64)


def attend_kernel(
    place, tile, near, far, below, moved, labc, labr, g1, wq_own, wo_own, wqo_m, wqo_s,
    n1t_ref, qkv_ref, prob_ref, heads_ref, wo_full, mixed_ref, n1_scr, stage, wins,
):
    c = place[3]
    mine = pl.ds(pl.multiple_of(c * 256, 256), 256)
    sibs = pl.ds(pl.multiple_of((1 - c) * 256, 256), 256)
    load_windows(place[4], tile, near, far, below, moved, stage, wins)
    x = wins[...]
    normed = norm(x, g1[...])[0]
    n1_scr[...] = normed.astype(BF)
    n1t_ref[...] = normed.T.astype(BF)
    n1 = n1_scr[...]
    for i in range(3):
        scale = 0.125 if i == 0 else 1.0
        own = dot(n1, wq_own[i]).astype(BF)
        other = (dot(n1_scr[:, mine], wqo_m[i]) + dot(n1_scr[:, sibs], wqo_s[i])).astype(BF)
        qkv_ref[:, i * 512 : i * 512 + 256] = own * BF(scale)
        qkv_ref[:, i * 512 + 256 : i * 512 + 512] = other * BF(scale)

    def window(w, carry):
        rows = pl.ds(pl.multiple_of(w * SEATS, 16), SEATS)
        same = labc[rows, 0:1] == labr[w, 0:1, :]
        for p in range(4):
            q2 = qkv_ref[rows, p * 128 : p * 128 + 128]
            k2 = qkv_ref[rows, 512 + p * 128 : 640 + p * 128]
            v2 = qkv_ref[rows, 1024 + p * 128 : 1152 + p * 128]
            total = None
            for h in range(2):
                keep = head_mask(h)
                scores = dot_nt(jnp.where(keep, q2, BF(0)), k2)
                scores = jnp.where(same, scores, -1e30)
                expo = jnp.exp(scores - jnp.max(scores, -1, keepdims=True))
                prob = (expo * (1.0 / jnp.sum(expo, -1, keepdims=True))).astype(BF)
                prob_ref[w * 8 + p * 2 + h] = prob
                part = dot(prob, jnp.where(keep, v2, BF(0)))
                total = part if total is None else total + part
            heads_ref[rows, p * 128 : p * 128 + 128] = total.astype(BF)
        return carry

    lax.fori_loop(0, WINS, window, 0)
    wo_full[0:256, :] = wo_own[...]
    wo_full[256:512, mine] = wqo_m[3]
    wo_full[256:512, sibs] = wqo_s[3]
    attn = dot(heads_ref[...], wo_full[...]).astype(BF).astype(F32)
    mixed_ref[...] = (x + attn).astype(BF)


def gelu_parts(v):
    square = v * v
    tanh_v = jnp.tanh(GELU_C * v * (1.0 + 0.044715 * square))
    half = 0.5 * (1.0 + tanh_v)
    slope = half + 0.5 * v * (1.0 - tanh_v * tanh_v) * (GELU_C + (3.0 * 0.044715 * GELU_C) * square)
    return v * half, slope


def store_rows(out, block, lead, cols, my=0):
    for yl in range(2):
        for z in range(8):
            rows = slice(z * 32 + yl * 16, z * 32 + yl * 16 + 16)
            out[lead + (yl ^ my, z, slice(None), cols)] = block[rows].astype(BF)


def mlp_block(w1, w2, cols, n2, cot):
    hidden, slope = gelu_parts(dot(n2, w1[:, cols]))
    return hidden.astype(BF), (dot_nt(cot, w2[cols, :]) * slope).astype(BF)


def store_grads(place, n2t, cott, hidden, dpre, x, keep, away):
    c, my, lead = place[3], place[1], (x ^ place[0],)
    mine = pl.ds(pl.multiple_of(c * 256, 256), 256)
    sibs = pl.ds(pl.multiple_of((1 - c) * 256, 256), 256)
    for rows, out in ((sibs, away), (mine, keep)):
        store_rows(out, dot(n2t[rows, :], dpre), lead, slice(0, 256), my)
        store_rows(out, dot(cott[rows, :], hidden), lead, slice(256, 512), my)


def mlp_own_kernel(
    place, mixed_ref, tile, near, far, below, moved, g2, w1_own, w2_own,
    n2_ref, n2t, cot_ref, cott, out_acc, norm_acc, keep, away,
    hid_scr, dpre_scr, stage, wins,
):
    load_windows(place[4], tile, near, far, below, moved, stage, wins)
    mixed = mixed_ref[...].astype(F32)
    normed = norm(mixed, g2[...])[0]
    n2_ref[...] = normed.astype(BF)
    n2t[...] = normed.T.astype(BF)
    cott[...] = wins[...].T.astype(BF)
    cot_ref[...] = wins[...].astype(BF)
    n2, cot = n2_ref[...], cot_ref[...]
    for x in range(4):
        cols = slice(x * 256, x * 256 + 256)
        hidden, dpre = mlp_block(w1_own, w2_own, cols, n2, cot)
        hid_scr[:, cols] = hidden
        dpre_scr[:, cols] = dpre
        store_grads(place, n2t, cott, hidden, dpre, x, keep, away)
    out_acc[...] = mixed + dot(hid_scr[...], w2_own[...])
    norm_acc[...] = dot_nt(dpre_scr[...], w1_own[...])


def mlp_other_kernel(
    place, mixed_ref, n2_ref, n2t, cot_ref, cott, out_acc, norm_acc, g2, w12_m, w12_s,
    band, tail, dm_ref, keep, away,
    hid_scr, dpre_scr, stage, wins,
):
    c = place[3]
    n2, cot = n2_ref[...], cot_ref[...]
    for n, (pair, half) in enumerate(((w12_m, c), (w12_s, 1 - c))):
        for i in range(2):
            cols = slice(i * 256, i * 256 + 256)
            hidden, dpre = mlp_block(pair.at[0], pair.at[1], cols, n2, cot)
            hid_scr[:, n * 512 + i * 256 : n * 512 + i * 256 + 256] = hidden
            dpre_scr[:, n * 512 + i * 256 : n * 512 + i * 256 + 256] = dpre
            store_grads(place, n2t, cott, hidden, dpre, 2 * half + i, keep, away)
    d_norm = norm_acc[...] + (
        dot_nt(dpre_scr[:, :512], w12_m[0]) + dot_nt(dpre_scr[:, 512:], w12_s[0])
    )
    gain = g2[...]
    xhat, rstd = norm(mixed_ref[...].astype(F32), gain)[1:]
    scaled = d_norm * gain
    dm = cot.astype(F32) + rstd * (
        scaled
        - jnp.mean(scaled, -1, keepdims=True)
        - xhat * jnp.mean(scaled * xhat, -1, keepdims=True)
    )
    dm_ref[...] = dm.astype(BF)
    wins[...] = out_acc[...] + (dot(hid_scr[:, :512], w12_m[1]) + dot(hid_scr[:, 512:], w12_s[1]))
    store_windows(wins, stage, band, tail)


def attend_back_kernel(
    dm_ref, prob_ref, qkv_ref, wo_full, first,
    dqkv, dmt,
    dheads,
):
    dm = dm_ref[...]
    dmt[...] = dm.astype(F32).T.astype(BF)
    dheads[...] = dot_nt(dm, wo_full[...]).astype(BF)

    def window(w, carry):
        rows = pl.ds(pl.multiple_of(w * SEATS, 16), SEATS)
        for p in range(4):
            pc = slice(p * 128, p * 128 + 128)
            q2 = qkv_ref[rows, p * 128 : p * 128 + 128]
            k2 = qkv_ref[rows, 512 + p * 128 : 640 + p * 128]
            v2 = qkv_ref[rows, 1024 + p * 128 : 1152 + p * 128]
            do2 = dheads[rows, pc]
            dq = dk = dv = None
            for h in range(2):
                keep = head_mask(h)
                prob_b = prob_ref[w * 8 + p * 2 + h]
                prob = prob_b.astype(F32)
                do_h = jnp.where(keep, do2, BF(0))
                d_prob = dot_nt(do_h, v2)
                moment = jnp.sum(prob * d_prob, -1, keepdims=True)
                d_scores = (prob * (d_prob - moment)).astype(BF)
                pq = dot(d_scores, jnp.where(keep, k2, BF(0)))
                pk = dot_tn(d_scores, jnp.where(keep, q2, BF(0)))
                pv = dot_tn(prob_b, do_h)
                dq = pq if dq is None else dq + pq
                dk = pk if dk is None else dk + pk
                dv = pv if dv is None else dv + pv
            dqkv[rows, p * 128 : p * 128 + 128] = (dq * 0.125).astype(BF)
            dqkv[rows, 512 + p * 128 : 640 + p * 128] = dk.astype(BF)
            dqkv[rows, 1024 + p * 128 : 1152 + p * 128] = dv.astype(BF)
        return carry

    lax.fori_loop(0, WINS, window, 0)


def attend_grads_kernel(
    place, dqkv, dmt, heads_ref, n1t_ref, first, second, third,
    keep, away,
):
    c, mt = place[3], place[4]
    mine = pl.ds(pl.multiple_of(c * 256, 256), 256)
    sibs = pl.ds(pl.multiple_of((1 - c) * 256, 256), 256)
    for rows, out in ((sibs, away), (mine, keep)):
        for t in range(2):
            for half in range(2):
                for which in range(2):
                    if which == 0 or half == 0:
                        start = (2 * which + half) * 512 + t * 256
                        grad = dot(n1t_ref[rows, :], dqkv[:, start : start + 256])
                    else:
                        grad = dot(dmt[rows, :], heads_ref[:, t * 256 : t * 256 + 256])
                    for sub in range(2):
                        lead = (half * 2 + sub, t ^ mt)
                        cols = slice(which * 128, which * 128 + 128)
                        store_rows(out, grad[:, sub * 128 : sub * 128 + 128], lead, cols)


def whole(shape, dtype=BF):
    return jax.ShapeDtypeStruct(shape, dtype)


def call(kernel, args, outs, scratch=(), place=None, flops=0, name=None, after=(), limit=8):
    spec = pl.BlockSpec(memory_space=pltpu.VMEM)
    args = tuple(args) + tuple(after)
    specs = [spec] * len(args)
    if place is not None:
        args = (place,) + args
        specs = [pl.BlockSpec(memory_space=pltpu.SMEM)] + specs
    size = sum(a.size * a.dtype.itemsize for a in list(args) + list(outs))
    return pl.pallas_call(
        kernel,
        out_shape=tuple(outs),
        in_specs=specs,
        out_specs=tuple([spec] * len(outs)),
        scratch_shapes=list(scratch),
        compiler_params=pltpu.CompilerParams(vmem_limit_bytes=limit * MIB),
        cost_estimate=pl.CostEstimate(flops=flops, bytes_accessed=size, transcendentals=0),
        name=name,
    )(*args)


def add(*values):
    total = values[0].astype(F32)
    for value in values[1:]:
        total = total + value.astype(F32)
    return total.astype(BF)


def core_sum_kernel(keep, arrived, out):
    out[...] = add(keep[...], arrived[...])


def core_sum_two_kernel(keep, arrived, keep_two, arrived_two, *outs):
    for refs, near, far, kept, sent in (
        ((keep, arrived), 1, 3, outs[0], outs[1]),
        ((keep_two, arrived_two), 3, 1, outs[2], outs[3]),
    ):
        for out, order in ((kept, (0, far)), (sent, (near, 2))):
            for i, x in enumerate(order):
                out[i] = add(*[r[x] for r in refs])


def half_sum_kernel(kept, arrived, kept_two, arrived_two, *outs):
    for i in range(2):
        outs[i][...] = add(kept[i], arrived[i])
        outs[2 + i][...] = add(kept_two[i], arrived_two[i])


def x_sum_kernel(own, arrived, other, arrived_two, *outs):
    for yl in range(2):
        outs[yl][...] = add(own[yl], arrived[yl])
        outs[2 + yl][...] = add(other[yl], arrived_two[yl])


def xy_sum_kernel(*refs):
    fc, at, out = refs[0:4], refs[4], refs[5]
    out[:, :, :512] = add(*[r[...] for r in fc])
    total = at[0].astype(F32)
    for i in range(1, 16):
        total = total + at[i].astype(F32)
    out[:, :, 512:] = total.astype(BF)


def last_sum_kernel(parts, out):
    total = parts[0].astype(F32)
    for i in range(1, 8):
        total = total + parts[i].astype(F32)
    for z in range(8):
        out[z] = total.astype(BF)


def copies_kernel(part, out):
    for i in range(8):
        out[i] = part[...]


def place_kernel(place, mine, sib, gq, go, g1, g2, scr2, scro):
    c = place[3]
    for src, cc in ((mine, c), (sib, 1 - c)):
        base = cc * 256
        for yl in range(2):
            for x in range(4):
                for z in range(8):
                    rows = pl.ds(pl.multiple_of(base + z * 32 + yl * 16, 16), 16)
                    chunk = src[2 * x + yl, z]
                    lo = (x % 2) * 128
                    g1[rows, x * 256 : x * 256 + 256] = chunk[:, :256]
                    scr2[rows, x * 256 : x * 256 + 256] = chunk[:, 256:512]
                    gq[x // 2, rows, lo : lo + 128] = chunk[:, 512:640]
                    if x < 2:
                        gq[2, rows, lo : lo + 128] = chunk[:, 640:]
                    else:
                        scro[rows, lo : lo + 128] = chunk[:, 640:]
    for i in range(4):
        g2[i * 256 : i * 256 + 256, :] = scr2[:, i * 256 : i * 256 + 256].astype(F32).T.astype(BF)
    go[...] = scro[...].astype(F32).T.astype(BF)


def core_phase_two(keep, arrived, keep_two, arrived_two):
    outs = [whole((2,) + keep.shape[1:])] * 4
    return call(core_sum_two_kernel, (keep, arrived, keep_two, arrived_two), outs, name="core_sum_two")


def y_phase(cut):
    return [cut[0]] + [flip(cut[k], t=k // 2, yl=k % 2) for k in (1, 2, 3)]


def reduce_over_z(total):
    parts = lax.all_to_all(total, "z", 0, 0)
    (chunks,) = call(last_sum_kernel, (parts,), [whole((8, 16, 768))], name="last_sum")
    column = lax.all_to_all(chunks, "z", 0, 0)
    (columns,) = call(copies_kernel, (column,), [whole((8, 8, 16, 768))], name="copies")
    return columns


def gather_grads(place, columns, after):
    (mine,) = fence((lax.all_to_all(columns, ("x", "yl"), 0, 0),), after)
    sib = flip(mine, c=1)
    outs = [whole((3, 512, 256)), whole((256, 512)), whole((512, 1024)), whole((1024, 512))]
    scratch = [pltpu.VMEM((512, 1024), BF), pltpu.VMEM((512, 256), BF)]
    return call(place_kernel, (mine, sib), outs, scratch, place, name="place")


def per_device(tokens, labels, gain_one, second_norm_gain, w_qkv, w_out, w_fc1, w_fc2, cotangent):
    x, yl, z, c, t = [lax.axis_index(name) for name in AXES]
    place = jnp.stack([x, yl, z, c, t]).astype(jnp.int32)
    tile, cot = tokens[0], cotangent[0]

    *pieces, wqo, w12 = cut_parts(place, tile, cot, w_qkv, w_out, w_fc1, w_fc2)
    wqo = flip(wqo, yl=1, t=1)
    rows = exchange_rows(*pieces[:3])

    band = lax.dynamic_slice_in_dim(labels, t * 6, 6, 1)
    band = jnp.where(t == 0, band, band[::-1]).reshape(12, 48, 1)
    lab = to_windows(band).reshape(TOK)
    labc = jnp.broadcast_to(lab[:, None], (TOK, 128))
    labr = jnp.broadcast_to(lab.reshape(WINS, 1, SEATS), (WINS, 8, SEATS))

    edge = first_columns(place, tile, rows, "edge", (labc, labr))
    moved = send(edge, lon_move(-1))
    cot_rows = exchange_rows(*fence(pieces[3:], (edge,)))
    (wqo,) = fence((wqo,), (edge,))
    wqo_sib = flip(wqo, c=1)
    (w12,) = fence((w12,), (wqo,))
    w12 = flip(w12, yl=1, t=1)
    cot_edge = first_columns(place, cot, cot_rows, "cot_edge", (moved, wqo))
    cot_moved = send(cot_edge, lon_move(-1))
    (w12,) = fence((w12,), (cot_edge,))

    stage = [pltpu.VMEM((12, 56, D), F32), pltpu.VMEM((TOK, D), F32)]
    n1t, qkv, prob, heads, wo_full, mixed = call(
        without(attend_kernel, 13, 1),
        (tile, *rows, moved, labc, labr, gain_one[None], w_qkv, w_out, wqo, wqo_sib),
        [
            whole((D, TOK)), whole((TOK, 3 * D)), whole((WINS * 8, SEATS, SEATS)),
            whole((TOK, D)), whole((D, D)), whole((TOK, D)),
        ],
        [pltpu.VMEM((TOK, D), BF)] + stage,
        place,
        flops=3 * 10**9,
        name="attend",
        limit=12,
        after=(cot_edge,),
    )
    grads = [whole((4, 2, 8, 16, 512))] * 2
    scratch = [pltpu.VMEM((TOK, 1024), BF), pltpu.VMEM((TOK, 1024), BF)] + stage
    tokens_like = [whole((TOK, D)), whole((D, TOK))] * 2 + [whole((TOK, D), F32)] * 2
    *carried, keep, away = call(
        mlp_own_kernel,
        (mixed, cot, *cot_rows, cot_moved, second_norm_gain[None], w_fc1, w_fc2),
        tokens_like + grads,
        scratch,
        place,
        flops=4 * 10**9,
        name="mlp_own",
        limit=12,
    )
    w12 = join(place, w12, "join_mlp", (keep,))
    w12_sib = flip(w12, c=1)
    arrived = flip(away, c=1)
    out_band, tail, dm, keep_two, away_two = call(
        mlp_other_kernel,
        (mixed, *carried, second_norm_gain[None], w12, w12_sib),
        [whole((12, 48, D)), whole((12, 6, D)), whole((TOK, D))] + grads,
        scratch,
        place,
        flops=4 * 10**9,
        name="mlp_other",
        limit=12,
    )
    fc_cut = core_phase_two(keep, arrived, keep_two, flip(away_two, c=1))
    kept, sent, kept_two, sent_two = fc_cut
    first, second = flip(sent, x=1), flip(sent_two, x=3)
    out_moved = send(tail, lon_move(1))
    out = jnp.concatenate([out_moved, out_band[:, 6:]], 1)
    dqkv, dmt = call(
        attend_back_kernel,
        (dm, prob, qkv, wo_full),
        [whole((TOK, 3 * D)), whole((D, TOK))],
        [pltpu.VMEM((TOK, D), BF)],
        flops=4 * 10**9,
        name="attend_back",
        limit=12,
        after=(kept,),
    )
    halves = [whole((2, 8, 16, 512))] * 4
    own, own_sent, other, other_sent = call(
        half_sum_kernel, (kept, first, kept_two, second), halves, name="half_sum"
    )
    at = call(
        attend_grads_kernel,
        (dqkv, dmt, heads, n1t),
        [whole((4, 2, 2, 8, 16, 256))] * 2,
        (),
        place,
        name="attend_grads",
        limit=12,
        after=(own_sent, other_sent, out_moved),
    )
    keep, away = at
    arrived, arrived_two = flip(own_sent, x=3), flip(other_sent, x=1)
    fc_cut = call(
        x_sum_kernel, (own, arrived, other, arrived_two), [whole((8, 16, 512))] * 4, name="x_sum"
    )
    fc_parts = y_phase(fc_cut)
    (at_total,) = call(
        without(core_sum_kernel, 2, 1), (keep, flip(away, c=1)), [whole(keep.shape)], name="core_sum", after=fc_cut[:1]
    )
    at_parts = lax.all_to_all(at_total.reshape(16, 8, 16, 256), ("x", "tp", "yl"), 0, 0)
    (total,) = call(xy_sum_kernel, (*fc_parts, at_parts), [whole((8, 16, 768))], name="xy_sum")
    columns = reduce_over_z(total)
    near, far, above = fence((out[6:9], out[9:12], out[3:6]), (columns,))
    near, far, above = flip(near, t=1), send(far, far_back), send(above, lat_move(1))
    gq, go, g1, g2 = gather_grads(place, columns, (near, far, above))
    out = jnp.where(
        t == 0,
        jnp.concatenate([far, out[0:6], near], 0),
        jnp.concatenate([above, near, far, out[0:3]], 0),
    )
    return out[None], gq, go, g1, g2


def without(kernel, start, count):
    return lambda *refs: kernel(*refs[:start], *refs[start + count :])


def solution(mesh):
    fine = Mesh(mesh.devices.reshape(4, 2, 8, 2, 2), AXES)
    lat, lon = ("x", "yl"), ("z", "c")
    return jax.shard_map(
        per_device,
        mesh=fine,
        in_specs=(
            P("tp", lat, lon, None),
            P(None, lat, lon),
            P(),
            P(),
            P(None, None, "tp"),
            P("tp", None),
            P(None, "tp"),
            P("tp", None),
            P("tp", lat, lon, None),
        ),
        out_specs=(
            P("tp", lat, lon, None),
            P(None, None, "tp"),
            P("tp", None),
            P(None, "tp"),
            P("tp", None),
        ),
        check_vma=False,
    )
```

```python
import functools

import jax
import jax.numpy as jnp
from jax import lax
from jax.experimental import pallas as pl
from jax.experimental.pallas import tpu as pltpu
from jax.sharding import Mesh
from jax.sharding import PartitionSpec as P

D = 512
FF = 2048
WLAT = 6
WLON = 12
SEATS = 144
WINS = 4
TOK = SEATS * WINS
EPS = 1e-05
GELU_C = 0.7978845608028654
BF = jnp.bfloat16
F32 = jnp.float32
AXES = ("x", "yl", "z", "c", "tp")
MIB = 1024 * 1024


def pairs_of(move):
    pairs = []
    for x in range(4):
        for yl in range(2):
            for z in range(8):
                for c in range(2):
                    for t in range(2):
                        dest = move(x, yl, z, c, t)
                        if dest is not None:
                            pairs.append((rank(x, yl, z, c, t), rank(*dest)))
    return pairs


def rank(x, yl, z, c, t):
    return ((2 * x + yl) * 16 + 2 * z + c) * 2 + t


def send(value, move):
    return lax.ppermute(value, AXES, pairs_of(move))


def flip(value, x=0, yl=0, z=0, c=0, t=0):
    return send(value, lambda a, b, d, e, f: (a ^ x, b ^ yl, d ^ z, e ^ c, f ^ t))


def shift_lat(x, yl, step):
    lat = (2 * x + yl + step) % 8
    return lat // 2, lat % 2


def shift_lon(z, c, step):
    lon = (2 * z + c + step) % 16
    return lon // 2, lon % 2


def lon_move(step):
    def move(x, yl, z, c, t):
        zz, cc = shift_lon(z, c, step)
        return x, yl, zz, cc, t

    return move


def far_move(x, yl, z, c, t):
    if t == 1:
        return x, yl, z, c, 0
    xx, yy = shift_lat(x, yl, -1)
    return xx, yy, z, c, 1


def far_back(x, yl, z, c, t):
    if t == 0:
        return x, yl, z, c, 1
    xx, yy = shift_lat(x, yl, 1)
    return xx, yy, z, c, 0


def lat_move(step):
    def move(x, yl, z, c, t):
        if t == 0:
            return None
        xx, yy = shift_lat(x, yl, step)
        return xx, yy, z, c, t

    return move


def fence(values, after):
    n = len(values)
    spec = pl.BlockSpec(memory_space=pltpu.VMEM)
    return pl.pallas_call(
        lambda *refs: None,
        out_shape=tuple(jax.ShapeDtypeStruct(v.shape, v.dtype) for v in values),
        in_specs=[spec] * (n + len(after)),
        out_specs=tuple([spec] * n),
        input_output_aliases={i: i for i in range(n)},
        compiler_params=pltpu.CompilerParams(vmem_limit_bytes=8 * MIB),
        name="fence",
    )(*values, *after)


def cut_kernel(place, tile, cot, wq, wo, w1, w2, *refs):
    rows, attend, mlp, sems = refs[0:6], refs[6], refs[7], refs[8]
    c, t = place[3], place[4]
    half = pl.ds(pl.multiple_of(c * 256, 256), 256)
    halves = pl.ds(pl.multiple_of(c * 512, 512), 512)
    copies = []
    for ref, (near, far, below) in ((tile, rows[:3]), (cot, rows[3:])):
        copies.append((ref.at[pl.ds(9 - 6 * t, 3)], near))
        copies.append((ref.at[pl.ds(6 * t, 3)], far))
        copies.append((ref.at[pl.ds(0, 3)], below))
    x = place[0]
    p = lax.rem(x, 2)
    quarter = pl.ds(pl.multiple_of(c * 256 + p * 128, 128), 128)
    copies.append((wq.at[:, quarter], attend.at[pl.ds(0, 3)]))
    copies.append((wo.at[pl.ds(pl.multiple_of(p * 128, 128), 128), half], attend.at[3]))
    copies.append((w1.at[pl.ds(pl.multiple_of(x * 128, 128), 128), halves], mlp.at[0]))
    copies.append((w2.at[pl.ds(pl.multiple_of((c * 4 + x) * 128, 128), 128)], mlp.at[1]))
    copies = [pltpu.make_async_copy(a, b, sems.at[i]) for i, (a, b) in enumerate(copies)]
    for copy in copies:
        copy.start()
    for copy in copies:
        copy.wait()


def cut_parts(place, *arrays):
    shapes = [(3, 48, D)] * 6 + [(4, 128, 256), (2, 128, 512)]
    hbm = pl.BlockSpec(memory_space=pltpu.HBM)
    return pl.pallas_call(
        cut_kernel,
        out_shape=tuple(whole(shape) for shape in shapes),
        in_specs=[pl.BlockSpec(memory_space=pltpu.SMEM)] + [hbm] * len(arrays),
        out_specs=tuple([pl.BlockSpec(memory_space=pltpu.VMEM)] * len(shapes)),
        scratch_shapes=[pltpu.SemaphoreType.DMA((10,))],
        compiler_params=pltpu.CompilerParams(vmem_limit_bytes=52 * MIB),
        name="cut",
    )(place, *arrays)


def exchange_rows(near, far, below):
    return flip(near, t=1), send(far, far_move), send(below, lat_move(-1))


def edge_kernel(place, tile, near, far, below, edge):
    t = place[4]
    for i in range(3):
        edge[i] = tile[3 + i + 6 * t, :6]
        row = jnp.where(t == 0, tile[6 + i, :6].astype(F32), below[i, :6].astype(F32))
        edge[3 + i] = row.astype(BF)
        edge[6 + i] = near[i, :6]
        edge[9 + i] = far[i, :6]


def join_kernel(place, *refs):
    parts, out = refs[:-1], refs[-1]
    rows = parts[0].shape[1]
    own = lax.rem(place[0], len(parts))
    for k, part in enumerate(parts):
        out[:, pl.ds(pl.multiple_of((own ^ k) * rows, rows), rows), :] = part[...]


def join(place, own, others, name, after=()):
    parts = [own] + list(others)
    depth, rows, width = own.shape
    out = whole((depth, len(parts) * rows, width))
    kernel = without(join_kernel, 1 + len(parts), len(after))
    (out,) = call(kernel, parts, [out], (), place, name=name, after=after)
    return out


def first_columns(place, tile, rows, name, after=()):
    kernel = without(edge_kernel, 5, len(after))
    (edge,) = call(kernel, (tile, *rows), [whole((12, 6, D))], (), place, name=name, after=after)
    return edge


def to_windows(band):
    width = band.shape[-1]
    return band.reshape(12, WINS, WLON, width).transpose(1, 0, 2, 3).reshape(TOK, width)


def load_windows(t, tile, near, far, below, moved, stage, wins):
    for row in range(12):
        if row < 3:
            value = tile[3 + row + 6 * t].astype(F32)
        elif row < 6:
            value = jnp.where(t == 0, tile[3 + row].astype(F32), below[row - 3].astype(F32))
        elif row < 9:
            value = near[row - 6].astype(F32)
        else:
            value = far[row - 9].astype(F32)
        stage[row, 0:48] = value
        stage[row, 48:54] = moved[row].astype(F32)
        for w in range(WINS):
            start = w * SEATS + row * WLON
            wins[start : start + WLON, :] = stage[row, 6 + 12 * w : 18 + 12 * w]


def store_windows(wins, stage, band, tail):
    for row in range(12):
        for w in range(WINS):
            start = w * SEATS + row * WLON
            stage[row, 6 + 12 * w : 18 + 12 * w] = wins[start : start + WLON, :]
        band[row] = stage[row, 0:48].astype(BF)
        tail[row] = stage[row, 48:54].astype(BF)


def norm(value, gain):
    centered = value - jnp.mean(value, -1, keepdims=True)
    rstd = lax.rsqrt(jnp.mean(centered * centered, -1, keepdims=True) + EPS)
    xhat = centered * rstd
    return xhat * gain, xhat, rstd


def dot(a, b):
    return lax.dot_general(a, b, (((1,), (0,)), ((), ())), preferred_element_type=F32)


def dot_nt(a, b):
    return lax.dot_general(a, b, (((1,), (1,)), ((), ())), preferred_element_type=F32)


def dot_tn(a, b):
    return lax.dot_general(a, b, (((0,), (0,)), ((), ())), preferred_element_type=F32)


def head_mask(h):
    lane = lax.broadcasted_iota(jnp.int32, (1, 128), 1)
    return (lane < 64) if h == 0 else (lane >= 64)


def attend_kernel(
    place, tile, near, far, below, moved, labc, labr, g1, wq_own, wo_own, wqo_m, wqo_s,
    n1t_ref, qkv_ref, prob_ref, heads_ref, wo_full, mixed_ref, n1_scr, stage, wins,
):
    c = place[3]
    mine = pl.ds(pl.multiple_of(c * 256, 256), 256)
    sibs = pl.ds(pl.multiple_of((1 - c) * 256, 256), 256)
    load_windows(place[4], tile, near, far, below, moved, stage, wins)
    x = wins[...]
    normed = norm(x, g1[...])[0]
    n1_scr[...] = normed.astype(BF)
    n1t_ref[...] = normed.T.astype(BF)
    n1 = n1_scr[...]
    for i in range(3):
        scale = 0.125 if i == 0 else 1.0
        own = dot(n1, wq_own[i]).astype(BF)
        other = (dot(n1_scr[:, mine], wqo_m[i]) + dot(n1_scr[:, sibs], wqo_s[i])).astype(BF)
        qkv_ref[:, i * 512 : i * 512 + 256] = own * BF(scale)
        qkv_ref[:, i * 512 + 256 : i * 512 + 512] = other * BF(scale)

    def window(w, carry):
        rows = pl.ds(pl.multiple_of(w * SEATS, 16), SEATS)
        same = labc[rows, 0:1] == labr[w, 0:1, :]
        for p in range(4):
            q2 = qkv_ref[rows, p * 128 : p * 128 + 128]
            k2 = qkv_ref[rows, 512 + p * 128 : 640 + p * 128]
            v2 = qkv_ref[rows, 1024 + p * 128 : 1152 + p * 128]
            total = None
            for h in range(2):
                keep = head_mask(h)
                scores = dot_nt(jnp.where(keep, q2, BF(0)), k2)
                scores = jnp.where(same, scores, -1e30)
                expo = jnp.exp(scores - jnp.max(scores, -1, keepdims=True))
                prob = (expo * (1.0 / jnp.sum(expo, -1, keepdims=True))).astype(BF)
                prob_ref[w * 8 + p * 2 + h] = prob
                part = dot(prob, jnp.where(keep, v2, BF(0)))
                total = part if total is None else total + part
            heads_ref[rows, p * 128 : p * 128 + 128] = total.astype(BF)
        return carry

    lax.fori_loop(0, WINS, window, 0, unroll=True)
    wo_full[0:256, :] = wo_own[...]
    wo_full[256:512, mine] = wqo_m[3]
    wo_full[256:512, sibs] = wqo_s[3]
    attn = dot(heads_ref[...], wo_full[...]).astype(BF).astype(F32)
    mixed_ref[...] = (x + attn).astype(BF)


def gelu_parts(v):
    square = v * v
    tanh_v = jnp.tanh(GELU_C * v * (1.0 + 0.044715 * square))
    half = 0.5 * (1.0 + tanh_v)
    slope = half + 0.5 * v * (1.0 - tanh_v * tanh_v) * (GELU_C + (3.0 * 0.044715 * GELU_C) * square)
    return v * half, slope


def store_rows(out, block, lead, cols, my=0):
    for yl in range(2):
        for z in range(8):
            rows = slice(z * 32 + yl * 16, z * 32 + yl * 16 + 16)
            out[lead + (yl ^ my, z, slice(None), cols)] = block[rows].astype(BF)


def mlp_block(w1, w2, cols, n2, cot):
    hidden, slope = gelu_parts(dot(n2, w1[:, cols]))
    return hidden.astype(BF), (dot_nt(cot, w2[cols, :]) * slope).astype(BF)


def store_grads(place, n2t, cott, hidden, dpre, x, keep, away):
    c, my, lead = place[3], place[1], (x ^ place[0],)
    mine = pl.ds(pl.multiple_of(c * 256, 256), 256)
    sibs = pl.ds(pl.multiple_of((1 - c) * 256, 256), 256)
    for rows, out in ((sibs, away), (mine, keep)):
        store_rows(out, dot(n2t[rows, :], dpre), lead, slice(0, 256), my)
        store_rows(out, dot(cott[rows, :], hidden), lead, slice(256, 512), my)


def mlp_own_kernel(
    place, mixed_ref, tile, near, far, below, moved, g2, w1_own, w2_own,
    n2_ref, n2t, cot_ref, cott, out_acc, norm_acc, keep, away,
    hid_scr, dpre_scr, stage, wins,
):
    load_windows(place[4], tile, near, far, below, moved, stage, wins)
    mixed = mixed_ref[...].astype(F32)
    normed = norm(mixed, g2[...])[0]
    n2_ref[...] = normed.astype(BF)
    n2t[...] = normed.T.astype(BF)
    cott[...] = wins[...].T.astype(BF)
    cot_ref[...] = wins[...].astype(BF)
    n2, cot = n2_ref[...], cot_ref[...]
    for x in range(4):
        cols = slice(x * 256, x * 256 + 256)
        hidden, dpre = mlp_block(w1_own, w2_own, cols, n2, cot)
        hid_scr[:, cols] = hidden
        dpre_scr[:, cols] = dpre
        store_grads(place, n2t, cott, hidden, dpre, x, keep, away)
    out_acc[...] = mixed + dot(hid_scr[...], w2_own[...])
    norm_acc[...] = dot_nt(dpre_scr[...], w1_own[...])


def mlp_other_kernel(
    place, mixed_ref, n2_ref, n2t, cot_ref, cott, out_acc, norm_acc, g2, w12_m, w12_s,
    band, tail, dm_ref, keep, away,
    hid_scr, dpre_scr, stage, wins,
):
    c = place[3]
    n2, cot = n2_ref[...], cot_ref[...]
    for n, (pair, half) in enumerate(((w12_m, c), (w12_s, 1 - c))):
        for i in range(2):
            cols = slice(i * 256, i * 256 + 256)
            hidden, dpre = mlp_block(pair.at[0], pair.at[1], cols, n2, cot)
            hid_scr[:, n * 512 + i * 256 : n * 512 + i * 256 + 256] = hidden
            dpre_scr[:, n * 512 + i * 256 : n * 512 + i * 256 + 256] = dpre
            store_grads(place, n2t, cott, hidden, dpre, 2 * half + i, keep, away)
    d_norm = norm_acc[...] + (
        dot_nt(dpre_scr[:, :512], w12_m[0]) + dot_nt(dpre_scr[:, 512:], w12_s[0])
    )
    gain = g2[...]
    xhat, rstd = norm(mixed_ref[...].astype(F32), gain)[1:]
    scaled = d_norm * gain
    dm = cot.astype(F32) + rstd * (
        scaled
        - jnp.mean(scaled, -1, keepdims=True)
        - xhat * jnp.mean(scaled * xhat, -1, keepdims=True)
    )
    dm_ref[...] = dm.astype(BF)
    wins[...] = out_acc[...] + (dot(hid_scr[:, :512], w12_m[1]) + dot(hid_scr[:, 512:], w12_s[1]))
    store_windows(wins, stage, band, tail)


def attend_back_kernel(
    dm_ref, prob_ref, qkv_ref, wo_full, first,
    dqkv, dmt,
    dheads,
):
    dm = dm_ref[...]
    dmt[...] = dm.astype(F32).T.astype(BF)
    dheads[...] = dot_nt(dm, wo_full[...]).astype(BF)

    def window(w, carry):
        rows = pl.ds(pl.multiple_of(w * SEATS, 16), SEATS)
        for p in range(4):
            pc = slice(p * 128, p * 128 + 128)
            q2 = qkv_ref[rows, p * 128 : p * 128 + 128]
            k2 = qkv_ref[rows, 512 + p * 128 : 640 + p * 128]
            v2 = qkv_ref[rows, 1024 + p * 128 : 1152 + p * 128]
            do2 = dheads[rows, pc]
            dq = dk = dv = None
            for h in range(2):
                keep = head_mask(h)
                prob_b = prob_ref[w * 8 + p * 2 + h]
                prob = prob_b.astype(F32)
                do_h = jnp.where(keep, do2, BF(0))
                d_prob = dot_nt(do_h, v2)
                moment = jnp.sum(prob * d_prob, -1, keepdims=True)
                d_scores = (prob * (d_prob - moment)).astype(BF)
                pq = dot(d_scores, jnp.where(keep, k2, BF(0)))
                pk = dot_tn(d_scores, jnp.where(keep, q2, BF(0)))
                pv = dot_tn(prob_b, do_h)
                dq = pq if dq is None else dq + pq
                dk = pk if dk is None else dk + pk
                dv = pv if dv is None else dv + pv
            dqkv[rows, p * 128 : p * 128 + 128] = (dq * 0.125).astype(BF)
            dqkv[rows, 512 + p * 128 : 640 + p * 128] = dk.astype(BF)
            dqkv[rows, 1024 + p * 128 : 1152 + p * 128] = dv.astype(BF)
        return carry

    lax.fori_loop(0, WINS, window, 0, unroll=True)


def attend_grads_kernel(
    place, dqkv, dmt, heads_ref, n1t_ref, first, second, third,
    keep, away,
):
    c, mt = place[3], place[4]
    mine = pl.ds(pl.multiple_of(c * 256, 256), 256)
    sibs = pl.ds(pl.multiple_of((1 - c) * 256, 256), 256)
    for rows, out in ((sibs, away), (mine, keep)):
        for t in range(2):
            for half in range(2):
                for which in range(2):
                    if which == 0 or half == 0:
                        start = (2 * which + half) * 512 + t * 256
                        grad = dot(n1t_ref[rows, :], dqkv[:, start : start + 256])
                    else:
                        grad = dot(dmt[rows, :], heads_ref[:, t * 256 : t * 256 + 256])
                    for sub in range(2):
                        lead = (half * 2 + sub, t ^ mt)
                        cols = slice(which * 128, which * 128 + 128)
                        store_rows(out, grad[:, sub * 128 : sub * 128 + 128], lead, cols)


def whole(shape, dtype=BF):
    return jax.ShapeDtypeStruct(shape, dtype)


def call(kernel, args, outs, scratch=(), place=None, flops=0, name=None, after=(), limit=8):
    spec = pl.BlockSpec(memory_space=pltpu.VMEM)
    args = tuple(args) + tuple(after)
    specs = [spec] * len(args)
    if place is not None:
        args = (place,) + args
        specs = [pl.BlockSpec(memory_space=pltpu.SMEM)] + specs
    size = sum(a.size * a.dtype.itemsize for a in list(args) + list(outs))
    return pl.pallas_call(
        kernel,
        out_shape=tuple(outs),
        in_specs=specs,
        out_specs=tuple([spec] * len(outs)),
        scratch_shapes=list(scratch),
        compiler_params=pltpu.CompilerParams(vmem_limit_bytes=limit * MIB),
        cost_estimate=pl.CostEstimate(flops=flops, bytes_accessed=size, transcendentals=0),
        name=name,
    )(*args)


def add(*values):
    total = values[0].astype(F32)
    for value in values[1:]:
        total = total + value.astype(F32)
    return total.astype(BF)


def core_sum_kernel(keep, arrived, out):
    out[...] = add(keep[...], arrived[...])


def core_sum_two_kernel(keep, arrived, keep_two, arrived_two, *outs):
    for refs, near, far, kept, sent in (
        ((keep, arrived), 1, 3, outs[0], outs[1]),
        ((keep_two, arrived_two), 3, 1, outs[2], outs[3]),
    ):
        for out, order in ((kept, (0, far)), (sent, (near, 2))):
            for i, x in enumerate(order):
                out[i] = add(*[r[x] for r in refs])


def half_sum_kernel(kept, arrived, kept_two, arrived_two, *outs):
    for i in range(2):
        outs[i][...] = add(kept[i], arrived[i])
        outs[2 + i][...] = add(kept_two[i], arrived_two[i])


def x_sum_kernel(own, arrived, other, arrived_two, *outs):
    for yl in range(2):
        outs[yl][...] = add(own[yl], arrived[yl])
        outs[2 + yl][...] = add(other[yl], arrived_two[yl])


def xy_sum_kernel(*refs):
    fc, at, out = refs[0:4], refs[4], refs[5]
    out[:, :, :512] = add(*[r[...] for r in fc])
    total = at[0].astype(F32)
    for i in range(1, 16):
        total = total + at[i].astype(F32)
    out[:, :, 512:] = total.astype(BF)


def last_sum_kernel(parts, out):
    total = parts[0].astype(F32)
    for i in range(1, 8):
        total = total + parts[i].astype(F32)
    for z in range(8):
        out[z] = total.astype(BF)


def copies_kernel(part, out):
    for i in range(8):
        out[i] = part[...]


def place_kernel(place, mine, sib, gq, go, g1, g2, scr2, scro):
    c = place[3]
    for src, cc in ((mine, c), (sib, 1 - c)):
        base = cc * 256
        for yl in range(2):
            for x in range(4):
                for z in range(8):
                    rows = pl.ds(pl.multiple_of(base + z * 32 + yl * 16, 16), 16)
                    chunk = src[2 * x + yl, z]
                    lo = (x % 2) * 128
                    g1[rows, x * 256 : x * 256 + 256] = chunk[:, :256]
                    scr2[rows, x * 256 : x * 256 + 256] = chunk[:, 256:512]
                    gq[x // 2, rows, lo : lo + 128] = chunk[:, 512:640]
                    if x < 2:
                        gq[2, rows, lo : lo + 128] = chunk[:, 640:]
                    else:
                        scro[rows, lo : lo + 128] = chunk[:, 640:]
    for i in range(4):
        g2[i * 256 : i * 256 + 256, :] = scr2[:, i * 256 : i * 256 + 256].astype(F32).T.astype(BF)
    go[...] = scro[...].astype(F32).T.astype(BF)


def core_phase_two(keep, arrived, keep_two, arrived_two):
    outs = [whole((2,) + keep.shape[1:])] * 4
    return call(core_sum_two_kernel, (keep, arrived, keep_two, arrived_two), outs, name="core_sum_two")


def y_phase(cut):
    return [cut[0]] + [flip(cut[k], t=k // 2, yl=k % 2) for k in (1, 2, 3)]


def reduce_over_z(total, after):
    parts = lax.all_to_all(total, "z", 0, 0)
    kernel = without(last_sum_kernel, 1, len(after))
    (chunks,) = call(kernel, (parts,), [whole((8, 16, 768))], name="last_sum", after=after)
    column = lax.all_to_all(chunks, "z", 0, 0)
    (columns,) = call(copies_kernel, (column,), [whole((8, 8, 16, 768))], name="copies")
    return columns


def gather_grads(place, columns):
    mine = lax.all_to_all(columns, ("x", "yl"), 0, 0)
    sib = flip(mine, c=1)
    outs = [whole((3, 512, 256)), whole((256, 512)), whole((512, 1024)), whole((1024, 512))]
    scratch = [pltpu.VMEM((512, 1024), BF), pltpu.VMEM((512, 256), BF)]
    return call(place_kernel, (mine, sib), outs, scratch, place, name="place")


def per_device(tokens, labels, gain_one, second_norm_gain, w_qkv, w_out, w_fc1, w_fc2, cotangent):
    x, yl, z, c, t = [lax.axis_index(name) for name in AXES]
    place = jnp.stack([x, yl, z, c, t]).astype(jnp.int32)
    tile, cot = tokens[0], cotangent[0]

    *pieces, wqo, w12 = cut_parts(place, tile, cot, w_qkv, w_out, w_fc1, w_fc2)
    wqo = flip(wqo, yl=1, t=1)
    rows = exchange_rows(*pieces[:3])

    band = lax.dynamic_slice_in_dim(labels, t * 6, 6, 1)
    band = jnp.where(t == 0, band, band[::-1]).reshape(12, 48, 1)
    lab = to_windows(band).reshape(TOK)
    labc = jnp.broadcast_to(lab[:, None], (TOK, 128))
    labr = jnp.broadcast_to(lab.reshape(WINS, 1, SEATS), (WINS, 8, SEATS))

    edge = first_columns(place, tile, rows, "edge", (labc, labr))
    moved = send(edge, lon_move(-1))
    (wqo,) = fence((wqo,), (edge,))
    wqo_two = flip(wqo, x=1)
    w12 = flip(fence((w12,), (wqo,))[0], yl=1, t=1)
    cot_rows = exchange_rows(*fence(pieces[3:], (edge,)))
    wqo = join(place, wqo, [wqo_two], "join_attend", (moved, *cot_rows, w12))
    wqo_sib = flip(wqo, c=1)
    cot_edge = first_columns(place, cot, cot_rows, "cot_edge", (wqo,))
    cot_moved = send(cot_edge, lon_move(-1))
    (w12,) = fence((w12,), (cot_edge,))

    stage = [pltpu.VMEM((12, 56, D), F32), pltpu.VMEM((TOK, D), F32)]
    n1t, qkv, prob, heads, wo_full, mixed = call(
        without(attend_kernel, 13, 1),
        (tile, *rows, moved, labc, labr, gain_one[None], w_qkv, w_out, wqo, wqo_sib),
        [
            whole((D, TOK)), whole((TOK, 3 * D)), whole((WINS * 8, SEATS, SEATS)),
            whole((TOK, D)), whole((D, D)), whole((TOK, D)),
        ],
        [pltpu.VMEM((TOK, D), BF)] + stage,
        place,
        flops=3 * 10**9,
        name="attend",
        limit=12,
        after=(cot_edge,),
    )
    grads = [whole((4, 2, 8, 16, 512))] * 2
    scratch = [pltpu.VMEM((TOK, 1024), BF), pltpu.VMEM((TOK, 1024), BF)] + stage
    tokens_like = [whole((TOK, D)), whole((D, TOK))] * 2 + [whole((TOK, D), F32)] * 2
    *carried, keep, away = call(
        mlp_own_kernel,
        (mixed, cot, *cot_rows, cot_moved, second_norm_gain[None], w_fc1, w_fc2),
        tokens_like + grads,
        scratch,
        place,
        flops=4 * 10**9,
        name="mlp_own",
        limit=12,
    )
    w12 = join(place, w12, [flip(w12, x=k) for k in (1, 2, 3)], "join_mlp", (keep,))
    w12_sib = flip(w12, c=1)
    arrived = flip(away, c=1)
    out_band, tail, dm, keep_two, away_two = call(
        mlp_other_kernel,
        (mixed, *carried, second_norm_gain[None], w12, w12_sib),
        [whole((12, 48, D)), whole((12, 6, D)), whole((TOK, D))] + grads,
        scratch,
        place,
        flops=4 * 10**9,
        name="mlp_other",
        limit=12,
    )
    fc_cut = core_phase_two(keep, arrived, keep_two, flip(away_two, c=1))
    kept, sent, kept_two, sent_two = fc_cut
    first, second = flip(sent, x=1), flip(sent_two, x=3)
    out_moved = send(tail, lon_move(1))
    out = jnp.concatenate([out_moved, out_band[:, 6:]], 1)
    dqkv, dmt = call(
        attend_back_kernel,
        (dm, prob, qkv, wo_full),
        [whole((TOK, 3 * D)), whole((D, TOK))],
        [pltpu.VMEM((TOK, D), BF)],
        flops=4 * 10**9,
        name="attend_back",
        limit=12,
        after=(kept,),
    )
    halves = [whole((2, 8, 16, 512))] * 4
    own, own_sent, other, other_sent = call(
        half_sum_kernel, (kept, first, kept_two, second), halves, name="half_sum"
    )
    at = call(
        attend_grads_kernel,
        (dqkv, dmt, heads, n1t),
        [whole((4, 2, 2, 8, 16, 256))] * 2,
        (),
        place,
        name="attend_grads",
        limit=12,
        after=(own_sent, other_sent, out_moved),
    )
    keep, away = at
    arrived, arrived_two = flip(own_sent, x=3), flip(other_sent, x=1)
    fc_cut = call(
        x_sum_kernel, (own, arrived, other, arrived_two), [whole((8, 16, 512))] * 4, name="x_sum"
    )
    fc_parts = y_phase(fc_cut)
    near = flip(out[6:9], t=1)
    (at_total,) = call(
        without(core_sum_kernel, 2, 2),
        (keep, flip(away, c=1)),
        [whole(keep.shape)],
        name="core_sum",
        after=(fc_cut[0], near),
    )
    at_parts = lax.all_to_all(at_total.reshape(16, 8, 16, 256), ("x", "tp", "yl"), 0, 0)
    (total,) = call(xy_sum_kernel, (*fc_parts, at_parts), [whole((8, 16, 768))], name="xy_sum")
    far, above = fence((out[9:12], out[3:6]), (total,))
    far, above = send(far, far_back), send(above, lat_move(1))
    columns = reduce_over_z(total, (far, above))
    gq, go, g1, g2 = gather_grads(place, columns)
    out = jnp.where(
        t == 0,
        jnp.concatenate([far, out[0:6], near], 0),
        jnp.concatenate([above, near, far, out[0:3]], 0),
    )
    return out[None], gq, go, g1, g2


def without(kernel, start, count):
    return lambda *refs: kernel(*refs[:start], *refs[start + count :])


def solution(mesh):
    fine = Mesh(mesh.devices.reshape(4, 2, 8, 2, 2), AXES)
    lat, lon = ("x", "yl"), ("z", "c")
    return jax.shard_map(
        per_device,
        mesh=fine,
        in_specs=(
            P("tp", lat, lon, None),
            P(None, lat, lon),
            P(),
            P(),
            P(None, None, "tp"),
            P("tp", None),
            P(None, "tp"),
            P("tp", None),
            P("tp", lat, lon, None),
        ),
        out_specs=(
            P("tp", lat, lon, None),
            P(None, None, "tp"),
            P("tp", None),
            P(None, "tp"),
            P("tp", None),
        ),
        check_vma=False,
    )
```

```python
import functools

import jax
import jax.numpy as jnp
from jax import lax
from jax.experimental import pallas as pl
from jax.experimental.pallas import tpu as pltpu
from jax.sharding import Mesh
from jax.sharding import PartitionSpec as P

D = 512
FF = 2048
WLAT = 6
WLON = 12
SEATS = 144
WINS = 4
TOK = SEATS * WINS
EPS = 1e-05
GELU_C = 0.7978845608028654
BF = jnp.bfloat16
F32 = jnp.float32
AXES = ("x", "yl", "z", "c", "tp")
MIB = 1024 * 1024


def pairs_of(move):
    pairs = []
    for x in range(4):
        for yl in range(2):
            for z in range(8):
                for c in range(2):
                    for t in range(2):
                        dest = move(x, yl, z, c, t)
                        if dest is not None:
                            pairs.append((rank(x, yl, z, c, t), rank(*dest)))
    return pairs


def rank(x, yl, z, c, t):
    return ((2 * x + yl) * 16 + 2 * z + c) * 2 + t


def send(value, move):
    return lax.ppermute(value, AXES, pairs_of(move))


def flip(value, x=0, yl=0, z=0, c=0, t=0):
    return send(value, lambda a, b, d, e, f: (a ^ x, b ^ yl, d ^ z, e ^ c, f ^ t))


def shift_lat(x, yl, step):
    lat = (2 * x + yl + step) % 8
    return lat // 2, lat % 2


def shift_lon(z, c, step):
    lon = (2 * z + c + step) % 16
    return lon // 2, lon % 2


def lon_move(step):
    def move(x, yl, z, c, t):
        zz, cc = shift_lon(z, c, step)
        return x, yl, zz, cc, t

    return move


def far_move(x, yl, z, c, t):
    if t == 1:
        return x, yl, z, c, 0
    xx, yy = shift_lat(x, yl, -1)
    return xx, yy, z, c, 1


def far_back(x, yl, z, c, t):
    if t == 0:
        return x, yl, z, c, 1
    xx, yy = shift_lat(x, yl, 1)
    return xx, yy, z, c, 0


def lat_move(step):
    def move(x, yl, z, c, t):
        if t == 0:
            return None
        xx, yy = shift_lat(x, yl, step)
        return xx, yy, z, c, t

    return move


def fence(values, after):
    n = len(values)
    spec = pl.BlockSpec(memory_space=pltpu.VMEM)
    return pl.pallas_call(
        lambda *refs: None,
        out_shape=tuple(jax.ShapeDtypeStruct(v.shape, v.dtype) for v in values),
        in_specs=[spec] * (n + len(after)),
        out_specs=tuple([spec] * n),
        input_output_aliases={i: i for i in range(n)},
        compiler_params=pltpu.CompilerParams(vmem_limit_bytes=8 * MIB),
        name="fence",
    )(*values, *after)


def cut_kernel(place, tile, cot, wq, wo, w1, w2, *refs):
    rows, attend, mlp, sems = refs[0:6], refs[6], refs[7], refs[8]
    c, t = place[3], place[4]
    half = pl.ds(pl.multiple_of(c * 256, 256), 256)
    halves = pl.ds(pl.multiple_of(c * 512, 512), 512)
    copies = []
    for ref, (near, far, below) in ((tile, rows[:3]), (cot, rows[3:])):
        copies.append((ref.at[pl.ds(9 - 6 * t, 3)], near))
        copies.append((ref.at[pl.ds(6 * t, 3)], far))
        copies.append((ref.at[pl.ds(0, 3)], below))
    x = place[0]
    p = lax.rem(x, 2)
    quarter = pl.ds(pl.multiple_of(c * 256 + p * 128, 128), 128)
    copies.append((wq.at[:, quarter], attend.at[pl.ds(0, 3)]))
    copies.append((wo.at[pl.ds(pl.multiple_of(p * 128, 128), 128), half], attend.at[3]))
    copies.append((w1.at[pl.ds(pl.multiple_of(x * 128, 128), 128), halves], mlp.at[0]))
    copies.append((w2.at[pl.ds(pl.multiple_of((c * 4 + x) * 128, 128), 128)], mlp.at[1]))
    copies = [pltpu.make_async_copy(a, b, sems.at[i]) for i, (a, b) in enumerate(copies)]
    for copy in copies:
        copy.start()
    for copy in copies:
        copy.wait()


def cut_parts(place, *arrays):
    shapes = [(3, 48, D)] * 6 + [(4, 128, 256), (2, 128, 512)]
    hbm = pl.BlockSpec(memory_space=pltpu.HBM)
    return pl.pallas_call(
        cut_kernel,
        out_shape=tuple(whole(shape) for shape in shapes),
        in_specs=[pl.BlockSpec(memory_space=pltpu.SMEM)] + [hbm] * len(arrays),
        out_specs=tuple([pl.BlockSpec(memory_space=pltpu.VMEM)] * len(shapes)),
        scratch_shapes=[pltpu.SemaphoreType.DMA((10,))],
        compiler_params=pltpu.CompilerParams(vmem_limit_bytes=52 * MIB),
        name="cut",
    )(place, *arrays)


def exchange_rows(near, far, below):
    return flip(near, t=1), send(far, far_move), send(below, lat_move(-1))


def edge_kernel(place, tile, near, far, below, edge):
    t = place[4]
    for i in range(3):
        edge[i] = tile[3 + i + 6 * t, :6]
        row = jnp.where(t == 0, tile[6 + i, :6].astype(F32), below[i, :6].astype(F32))
        edge[3 + i] = row.astype(BF)
        edge[6 + i] = near[i, :6]
        edge[9 + i] = far[i, :6]


def join_kernel(place, *refs):
    parts, out = refs[:-1], refs[-1]
    rows = parts[0].shape[1]
    own = lax.rem(place[0], len(parts))
    for k, part in enumerate(parts):
        out[:, pl.ds(pl.multiple_of((own ^ k) * rows, rows), rows), :] = part[...]


def join(place, own, others, name, after=()):
    parts = [own] + list(others)
    depth, rows, width = own.shape
    out = whole((depth, len(parts) * rows, width))
    kernel = without(join_kernel, 1 + len(parts), len(after))
    (out,) = call(kernel, parts, [out], (), place, name=name, after=after)
    return out


def first_columns(place, tile, rows, name, after=()):
    kernel = without(edge_kernel, 5, len(after))
    (edge,) = call(kernel, (tile, *rows), [whole((12, 6, D))], (), place, name=name, after=after)
    return edge


def to_windows(band):
    width = band.shape[-1]
    return band.reshape(12, WINS, WLON, width).transpose(1, 0, 2, 3).reshape(TOK, width)


def load_windows(t, tile, near, far, below, moved, stage, wins):
    for row in range(12):
        if row < 3:
            value = tile[3 + row + 6 * t].astype(F32)
        elif row < 6:
            value = jnp.where(t == 0, tile[3 + row].astype(F32), below[row - 3].astype(F32))
        elif row < 9:
            value = near[row - 6].astype(F32)
        else:
            value = far[row - 9].astype(F32)
        stage[row, 0:48] = value
        stage[row, 48:54] = moved[row].astype(F32)
        for w in range(WINS):
            start = w * SEATS + row * WLON
            wins[start : start + WLON, :] = stage[row, 6 + 12 * w : 18 + 12 * w]


def store_windows(wins, stage, band, tail):
    for row in range(12):
        for w in range(WINS):
            start = w * SEATS + row * WLON
            stage[row, 6 + 12 * w : 18 + 12 * w] = wins[start : start + WLON, :]
        band[row] = stage[row, 0:48].astype(BF)
        tail[row] = stage[row, 48:54].astype(BF)


def norm(value, gain):
    centered = value - jnp.mean(value, -1, keepdims=True)
    rstd = lax.rsqrt(jnp.mean(centered * centered, -1, keepdims=True) + EPS)
    xhat = centered * rstd
    return xhat * gain, xhat, rstd


def dot(a, b):
    return lax.dot_general(a, b, (((1,), (0,)), ((), ())), preferred_element_type=F32)


def dot_nt(a, b):
    return lax.dot_general(a, b, (((1,), (1,)), ((), ())), preferred_element_type=F32)


def dot_tn(a, b):
    return lax.dot_general(a, b, (((0,), (0,)), ((), ())), preferred_element_type=F32)


def head_mask(h):
    lane = lax.broadcasted_iota(jnp.int32, (1, 128), 1)
    return (lane < 64) if h == 0 else (lane >= 64)


def attend_kernel(
    place, tile, near, far, below, moved, labc, labr, g1, wq_own, wo_own, wqo_m, wqo_s,
    n1t_ref, qkv_ref, prob_ref, heads_ref, wo_full, mixed_ref, n1_scr, stage, wins,
):
    c = place[3]
    mine = pl.ds(pl.multiple_of(c * 256, 256), 256)
    sibs = pl.ds(pl.multiple_of((1 - c) * 256, 256), 256)
    load_windows(place[4], tile, near, far, below, moved, stage, wins)
    x = wins[...]
    normed = norm(x, g1[...])[0]
    n1_scr[...] = normed.astype(BF)
    n1t_ref[...] = normed.T.astype(BF)
    n1 = n1_scr[...]
    for i in range(3):
        scale = 0.125 if i == 0 else 1.0
        own = dot(n1, wq_own[i]).astype(BF)
        other = (dot(n1_scr[:, mine], wqo_m[i]) + dot(n1_scr[:, sibs], wqo_s[i])).astype(BF)
        qkv_ref[:, i * 512 : i * 512 + 256] = own * BF(scale)
        qkv_ref[:, i * 512 + 256 : i * 512 + 512] = other * BF(scale)

    def window(w, carry):
        rows = pl.ds(pl.multiple_of(w * SEATS, 16), SEATS)
        same = labc[rows, 0:1] == labr[w, 0:1, :]
        for p in range(4):
            q2 = qkv_ref[rows, p * 128 : p * 128 + 128]
            k2 = qkv_ref[rows, 512 + p * 128 : 640 + p * 128]
            v2 = qkv_ref[rows, 1024 + p * 128 : 1152 + p * 128]
            total = None
            for h in range(2):
                keep = head_mask(h)
                scores = dot_nt(jnp.where(keep, q2, BF(0)), k2)
                scores = jnp.where(same, scores, -1e30)
                expo = jnp.exp(scores - jnp.max(scores, -1, keepdims=True))
                prob = (expo * (1.0 / jnp.sum(expo, -1, keepdims=True))).astype(BF)
                prob_ref[w * 8 + p * 2 + h] = prob
                part = dot(prob, jnp.where(keep, v2, BF(0)))
                total = part if total is None else total + part
            heads_ref[rows, p * 128 : p * 128 + 128] = total.astype(BF)
        return carry

    lax.fori_loop(0, WINS // 2, lambda i, carry: window(2 * i + 1, window(2 * i, carry)), 0)
    wo_full[0:256, :] = wo_own[...]
    wo_full[256:512, mine] = wqo_m[3]
    wo_full[256:512, sibs] = wqo_s[3]
    attn = dot(heads_ref[...], wo_full[...]).astype(BF).astype(F32)
    mixed_ref[...] = (x + attn).astype(BF)


def gelu_parts(v):
    square = v * v
    tanh_v = jnp.tanh(GELU_C * v * (1.0 + 0.044715 * square))
    half = 0.5 * (1.0 + tanh_v)
    slope = half + 0.5 * v * (1.0 - tanh_v * tanh_v) * (GELU_C + (3.0 * 0.044715 * GELU_C) * square)
    return v * half, slope


def store_rows(out, block, lead, cols, my=0):
    for yl in range(2):
        for z in range(8):
            rows = slice(z * 32 + yl * 16, z * 32 + yl * 16 + 16)
            out[lead + (yl ^ my, z, slice(None), cols)] = block[rows].astype(BF)


def mlp_block(w1, w2, cols, n2, cot):
    hidden, slope = gelu_parts(dot(n2, w1[:, cols]))
    return hidden.astype(BF), (dot_nt(cot, w2[cols, :]) * slope).astype(BF)


def store_grads(place, n2t, cott, hidden, dpre, x, keep, away):
    c, my, lead = place[3], place[1], (x ^ place[0],)
    mine = pl.ds(pl.multiple_of(c * 256, 256), 256)
    sibs = pl.ds(pl.multiple_of((1 - c) * 256, 256), 256)
    for rows, out in ((sibs, away), (mine, keep)):
        store_rows(out, dot(n2t[rows, :], dpre), lead, slice(0, 256), my)
        store_rows(out, dot(cott[rows, :], hidden), lead, slice(256, 512), my)


def mlp_own_kernel(
    place, mixed_ref, tile, near, far, below, moved, g2, w1_own, w2_own,
    n2_ref, n2t, cot_ref, cott, out_acc, norm_acc, keep, away,
    hid_scr, dpre_scr, stage, wins,
):
    load_windows(place[4], tile, near, far, below, moved, stage, wins)
    mixed = mixed_ref[...].astype(F32)
    normed = norm(mixed, g2[...])[0]
    n2_ref[...] = normed.astype(BF)
    n2t[...] = normed.T.astype(BF)
    cott[...] = wins[...].T.astype(BF)
    cot_ref[...] = wins[...].astype(BF)
    n2, cot = n2_ref[...], cot_ref[...]
    for x in range(4):
        cols = slice(x * 256, x * 256 + 256)
        hidden, dpre = mlp_block(w1_own, w2_own, cols, n2, cot)
        hid_scr[:, cols] = hidden
        dpre_scr[:, cols] = dpre
        store_grads(place, n2t, cott, hidden, dpre, x, keep, away)
    out_acc[...] = mixed + dot(hid_scr[...], w2_own[...])
    norm_acc[...] = dot_nt(dpre_scr[...], w1_own[...])


def mlp_other_kernel(
    place, mixed_ref, n2_ref, n2t, cot_ref, cott, out_acc, norm_acc, g2, w12_m, w12_s,
    band, tail, dm_ref, keep, away,
    hid_scr, dpre_scr, stage, wins,
):
    c = place[3]
    n2, cot = n2_ref[...], cot_ref[...]
    for n, (pair, half) in enumerate(((w12_m, c), (w12_s, 1 - c))):
        for i in range(2):
            cols = slice(i * 256, i * 256 + 256)
            hidden, dpre = mlp_block(pair.at[0], pair.at[1], cols, n2, cot)
            hid_scr[:, n * 512 + i * 256 : n * 512 + i * 256 + 256] = hidden
            dpre_scr[:, n * 512 + i * 256 : n * 512 + i * 256 + 256] = dpre
            store_grads(place, n2t, cott, hidden, dpre, 2 * half + i, keep, away)
    d_norm = norm_acc[...] + (
        dot_nt(dpre_scr[:, :512], w12_m[0]) + dot_nt(dpre_scr[:, 512:], w12_s[0])
    )
    gain = g2[...]
    xhat, rstd = norm(mixed_ref[...].astype(F32), gain)[1:]
    scaled = d_norm * gain
    dm = cot.astype(F32) + rstd * (
        scaled
        - jnp.mean(scaled, -1, keepdims=True)
        - xhat * jnp.mean(scaled * xhat, -1, keepdims=True)
    )
    dm_ref[...] = dm.astype(BF)
    wins[...] = out_acc[...] + (dot(hid_scr[:, :512], w12_m[1]) + dot(hid_scr[:, 512:], w12_s[1]))
    store_windows(wins, stage, band, tail)


def attend_back_kernel(
    dm_ref, prob_ref, qkv_ref, wo_full, first,
    dqkv, dmt,
    dheads,
):
    dm = dm_ref[...]
    dmt[...] = dm.astype(F32).T.astype(BF)
    dheads[...] = dot_nt(dm, wo_full[...]).astype(BF)

    def window(w, carry):
        rows = pl.ds(pl.multiple_of(w * SEATS, 16), SEATS)
        for p in range(4):
            pc = slice(p * 128, p * 128 + 128)
            q2 = qkv_ref[rows, p * 128 : p * 128 + 128]
            k2 = qkv_ref[rows, 512 + p * 128 : 640 + p * 128]
            v2 = qkv_ref[rows, 1024 + p * 128 : 1152 + p * 128]
            do2 = dheads[rows, pc]
            dq = dk = dv = None
            for h in range(2):
                keep = head_mask(h)
                prob_b = prob_ref[w * 8 + p * 2 + h]
                prob = prob_b.astype(F32)
                do_h = jnp.where(keep, do2, BF(0))
                d_prob = dot_nt(do_h, v2)
                moment = jnp.sum(prob * d_prob, -1, keepdims=True)
                d_scores = (prob * (d_prob - moment)).astype(BF)
                pq = dot(d_scores, jnp.where(keep, k2, BF(0)))
                pk = dot_tn(d_scores, jnp.where(keep, q2, BF(0)))
                pv = dot_tn(prob_b, do_h)
                dq = pq if dq is None else dq + pq
                dk = pk if dk is None else dk + pk
                dv = pv if dv is None else dv + pv
            dqkv[rows, p * 128 : p * 128 + 128] = (dq * 0.125).astype(BF)
            dqkv[rows, 512 + p * 128 : 640 + p * 128] = dk.astype(BF)
            dqkv[rows, 1024 + p * 128 : 1152 + p * 128] = dv.astype(BF)
        return carry

    lax.fori_loop(0, WINS, window, 0)


def attend_grads_kernel(
    place, dqkv, dmt, heads_ref, n1t_ref, first, second, third,
    keep, away,
):
    c, mt = place[3], place[4]
    mine = pl.ds(pl.multiple_of(c * 256, 256), 256)
    sibs = pl.ds(pl.multiple_of((1 - c) * 256, 256), 256)
    for rows, out in ((sibs, away), (mine, keep)):
        for t in range(2):
            for half in range(2):
                for which in range(2):
                    if which == 0 or half == 0:
                        start = (2 * which + half) * 512 + t * 256
                        grad = dot(n1t_ref[rows, :], dqkv[:, start : start + 256])
                    else:
                        grad = dot(dmt[rows, :], heads_ref[:, t * 256 : t * 256 + 256])
                    for sub in range(2):
                        lead = (half * 2 + sub, t ^ mt)
                        cols = slice(which * 128, which * 128 + 128)
                        store_rows(out, grad[:, sub * 128 : sub * 128 + 128], lead, cols)


def whole(shape, dtype=BF):
    return jax.ShapeDtypeStruct(shape, dtype)


def call(kernel, args, outs, scratch=(), place=None, flops=0, name=None, after=(), limit=8):
    spec = pl.BlockSpec(memory_space=pltpu.VMEM)
    args = tuple(args) + tuple(after)
    specs = [spec] * len(args)
    if place is not None:
        args = (place,) + args
        specs = [pl.BlockSpec(memory_space=pltpu.SMEM)] + specs
    size = sum(a.size * a.dtype.itemsize for a in list(args) + list(outs))
    return pl.pallas_call(
        kernel,
        out_shape=tuple(outs),
        in_specs=specs,
        out_specs=tuple([spec] * len(outs)),
        scratch_shapes=list(scratch),
        compiler_params=pltpu.CompilerParams(vmem_limit_bytes=limit * MIB),
        cost_estimate=pl.CostEstimate(flops=flops, bytes_accessed=size, transcendentals=0),
        name=name,
    )(*args)


def add(*values):
    total = values[0].astype(F32)
    for value in values[1:]:
        total = total + value.astype(F32)
    return total.astype(BF)


def core_sum_kernel(keep, arrived, out):
    out[...] = add(keep[...], arrived[...])


def core_sum_two_kernel(keep, arrived, keep_two, arrived_two, *outs):
    for refs, near, far, kept, sent in (
        ((keep, arrived), 1, 3, outs[0], outs[1]),
        ((keep_two, arrived_two), 3, 1, outs[2], outs[3]),
    ):
        for out, order in ((kept, (0, far)), (sent, (near, 2))):
            for i, x in enumerate(order):
                out[i] = add(*[r[x] for r in refs])


def half_sum_kernel(kept, arrived, kept_two, arrived_two, *outs):
    for i in range(2):
        outs[i][...] = add(kept[i], arrived[i])
        outs[2 + i][...] = add(kept_two[i], arrived_two[i])


def x_sum_kernel(own, arrived, other, arrived_two, *outs):
    for yl in range(2):
        outs[yl][...] = add(own[yl], arrived[yl])
        outs[2 + yl][...] = add(other[yl], arrived_two[yl])


def xy_sum_kernel(*refs):
    fc, at, out = refs[0:4], refs[4], refs[5]
    out[:, :, :512] = add(*[r[...] for r in fc])
    total = at[0].astype(F32)
    for i in range(1, 16):
        total = total + at[i].astype(F32)
    out[:, :, 512:] = total.astype(BF)


def last_sum_kernel(parts, out):
    total = parts[0].astype(F32)
    for i in range(1, 8):
        total = total + parts[i].astype(F32)
    for z in range(8):
        out[z] = total.astype(BF)


def copies_kernel(part, out):
    for i in range(8):
        out[i] = part[...]


def place_kernel(place, mine, sib, gq, go, g1, g2, scr2, scro):
    c = place[3]
    for src, cc in ((mine, c), (sib, 1 - c)):
        base = cc * 256
        for yl in range(2):
            for x in range(4):
                for z in range(8):
                    rows = pl.ds(pl.multiple_of(base + z * 32 + yl * 16, 16), 16)
                    chunk = src[2 * x + yl, z]
                    lo = (x % 2) * 128
                    g1[rows, x * 256 : x * 256 + 256] = chunk[:, :256]
                    scr2[rows, x * 256 : x * 256 + 256] = chunk[:, 256:512]
                    gq[x // 2, rows, lo : lo + 128] = chunk[:, 512:640]
                    if x < 2:
                        gq[2, rows, lo : lo + 128] = chunk[:, 640:]
                    else:
                        scro[rows, lo : lo + 128] = chunk[:, 640:]
    for i in range(4):
        g2[i * 256 : i * 256 + 256, :] = scr2[:, i * 256 : i * 256 + 256].astype(F32).T.astype(BF)
    go[...] = scro[...].astype(F32).T.astype(BF)


def core_phase_two(keep, arrived, keep_two, arrived_two):
    outs = [whole((2,) + keep.shape[1:])] * 4
    return call(core_sum_two_kernel, (keep, arrived, keep_two, arrived_two), outs, name="core_sum_two")


def y_phase(cut):
    return [cut[0]] + [flip(cut[k], t=k // 2, yl=k % 2) for k in (1, 2, 3)]


def reduce_over_z(total, after):
    parts = lax.all_to_all(total, "z", 0, 0)
    kernel = without(last_sum_kernel, 1, len(after))
    (chunks,) = call(kernel, (parts,), [whole((8, 16, 768))], name="last_sum", after=after)
    column = lax.all_to_all(chunks, "z", 0, 0)
    (columns,) = call(copies_kernel, (column,), [whole((8, 8, 16, 768))], name="copies")
    return columns


def gather_grads(place, columns):
    mine = lax.all_to_all(columns, ("x", "yl"), 0, 0)
    sib = flip(mine, c=1)
    outs = [whole((3, 512, 256)), whole((256, 512)), whole((512, 1024)), whole((1024, 512))]
    scratch = [pltpu.VMEM((512, 1024), BF), pltpu.VMEM((512, 256), BF)]
    return call(place_kernel, (mine, sib), outs, scratch, place, name="place")


def per_device(tokens, labels, gain_one, second_norm_gain, w_qkv, w_out, w_fc1, w_fc2, cotangent):
    x, yl, z, c, t = [lax.axis_index(name) for name in AXES]
    place = jnp.stack([x, yl, z, c, t]).astype(jnp.int32)
    tile, cot = tokens[0], cotangent[0]

    *pieces, wqo, w12 = cut_parts(place, tile, cot, w_qkv, w_out, w_fc1, w_fc2)
    wqo = flip(wqo, yl=1, t=1)
    rows = exchange_rows(*pieces[:3])

    band = lax.dynamic_slice_in_dim(labels, t * 6, 6, 1)
    band = jnp.where(t == 0, band, band[::-1]).reshape(12, 48, 1)
    lab = to_windows(band).reshape(TOK)
    labc = jnp.broadcast_to(lab[:, None], (TOK, 128))
    labr = jnp.broadcast_to(lab.reshape(WINS, 1, SEATS), (WINS, 8, SEATS))

    edge = first_columns(place, tile, rows, "edge", (labc, labr))
    moved = send(edge, lon_move(-1))
    (wqo,) = fence((wqo,), (edge,))
    wqo_two = flip(wqo, x=1)
    w12 = flip(fence((w12,), (wqo,))[0], yl=1, t=1)
    cot_rows = exchange_rows(*fence(pieces[3:], (edge,)))
    wqo = join(place, wqo, [wqo_two], "join_attend", (moved, *cot_rows, w12))
    wqo_sib = flip(wqo, c=1)
    cot_edge = first_columns(place, cot, cot_rows, "cot_edge", (wqo,))
    cot_moved = send(cot_edge, lon_move(-1))
    (w12,) = fence((w12,), (cot_edge,))

    stage = [pltpu.VMEM((12, 56, D), F32), pltpu.VMEM((TOK, D), F32)]
    n1t, qkv, prob, heads, wo_full, mixed = call(
        without(attend_kernel, 13, 1),
        (tile, *rows, moved, labc, labr, gain_one[None], w_qkv, w_out, wqo, wqo_sib),
        [
            whole((D, TOK)), whole((TOK, 3 * D)), whole((WINS * 8, SEATS, SEATS)),
            whole((TOK, D)), whole((D, D)), whole((TOK, D)),
        ],
        [pltpu.VMEM((TOK, D), BF)] + stage,
        place,
        flops=3 * 10**9,
        name="attend",
        limit=12,
        after=(cot_edge,),
    )
    grads = [whole((4, 2, 8, 16, 512))] * 2
    scratch = [pltpu.VMEM((TOK, 1024), BF), pltpu.VMEM((TOK, 1024), BF)] + stage
    tokens_like = [whole((TOK, D)), whole((D, TOK))] * 2 + [whole((TOK, D), F32)] * 2
    *carried, keep, away = call(
        mlp_own_kernel,
        (mixed, cot, *cot_rows, cot_moved, second_norm_gain[None], w_fc1, w_fc2),
        tokens_like + grads,
        scratch,
        place,
        flops=4 * 10**9,
        name="mlp_own",
        limit=12,
    )
    w12 = join(place, w12, [flip(w12, x=k) for k in (1, 2, 3)], "join_mlp", (keep,))
    w12_sib = flip(w12, c=1)
    arrived = flip(away, c=1)
    out_band, tail, dm, keep_two, away_two = call(
        mlp_other_kernel,
        (mixed, *carried, second_norm_gain[None], w12, w12_sib),
        [whole((12, 48, D)), whole((12, 6, D)), whole((TOK, D))] + grads,
        scratch,
        place,
        flops=4 * 10**9,
        name="mlp_other",
        limit=12,
    )
    fc_cut = core_phase_two(keep, arrived, keep_two, flip(away_two, c=1))
    kept, sent, kept_two, sent_two = fc_cut
    first, second = flip(sent, x=1), flip(sent_two, x=3)
    out_moved = send(tail, lon_move(1))
    out = jnp.concatenate([out_moved, out_band[:, 6:]], 1)
    dqkv, dmt = call(
        attend_back_kernel,
        (dm, prob, qkv, wo_full),
        [whole((TOK, 3 * D)), whole((D, TOK))],
        [pltpu.VMEM((TOK, D), BF)],
        flops=4 * 10**9,
        name="attend_back",
        limit=12,
        after=(kept,),
    )
    halves = [whole((2, 8, 16, 512))] * 4
    own, own_sent, other, other_sent = call(
        half_sum_kernel, (kept, first, kept_two, second), halves, name="half_sum"
    )
    at = call(
        attend_grads_kernel,
        (dqkv, dmt, heads, n1t),
        [whole((4, 2, 2, 8, 16, 256))] * 2,
        (),
        place,
        name="attend_grads",
        limit=12,
        after=(own_sent, other_sent, out_moved),
    )
    keep, away = at
    arrived, arrived_two = flip(own_sent, x=3), flip(other_sent, x=1)
    fc_cut = call(
        x_sum_kernel, (own, arrived, other, arrived_two), [whole((8, 16, 512))] * 4, name="x_sum"
    )
    fc_parts = y_phase(fc_cut)
    near = flip(out[6:9], t=1)
    (at_total,) = call(
        without(core_sum_kernel, 2, 2),
        (keep, flip(away, c=1)),
        [whole(keep.shape)],
        name="core_sum",
        after=(fc_cut[0], near),
    )
    at_parts = lax.all_to_all(at_total.reshape(16, 8, 16, 256), ("x", "tp", "yl"), 0, 0)
    (total,) = call(xy_sum_kernel, (*fc_parts, at_parts), [whole((8, 16, 768))], name="xy_sum")
    far, above = fence((out[9:12], out[3:6]), (total,))
    far, above = send(far, far_back), send(above, lat_move(1))
    columns = reduce_over_z(total, (far, above))
    gq, go, g1, g2 = gather_grads(place, columns)
    out = jnp.where(
        t == 0,
        jnp.concatenate([far, out[0:6], near], 0),
        jnp.concatenate([above, near, far, out[0:3]], 0),
    )
    return out[None], gq, go, g1, g2


def without(kernel, start, count):
    return lambda *refs: kernel(*refs[:start], *refs[start + count :])


def solution(mesh):
    fine = Mesh(mesh.devices.reshape(4, 2, 8, 2, 2), AXES)
    lat, lon = ("x", "yl"), ("z", "c")
    return jax.shard_map(
        per_device,
        mesh=fine,
        in_specs=(
            P("tp", lat, lon, None),
            P(None, lat, lon),
            P(),
            P(),
            P(None, None, "tp"),
            P("tp", None),
            P(None, "tp"),
            P("tp", None),
            P("tp", lat, lon, None),
        ),
        out_specs=(
            P("tp", lat, lon, None),
            P(None, None, "tp"),
            P("tp", None),
            P(None, "tp"),
            P("tp", None),
        ),
        check_vma=False,
    )
```
